32 devices in a mesh: sen: 16 (over z, y, x), par: 2 (over core).
Axes of the slice: x: 2, y: 2, z: 4, core: 2. Of those that a mesh axis runs over, the one named last changes fastest.
Arguments:
- vectors: float32 [2, 128, 256], P(None, 'sen'), may hold values from -6 to 6
- observed: float32 [2, 128, 256], P(None, 'sen'), may hold values from -6 to 6
- operator: bfloat16 [2, 128, 128, 768], P(None, None, 'sen', 'par'), may hold values from -0.4375 to 0.4375
- noise: float32 [128], P('sen'), may hold values from 0.3 to 3
- coefficient: float32 [2, 384], P('par'), may hold values from 0.05 to 0.24
- offsets: int32 [2, 384], P('par'), may hold values from -3 to 3
Outputs:
- residual: float32 [2, 128, 256], P(None, 'sen')
- applied: float32 [2, 128, 256], P(None, 'sen')
The draws below stay inside these ranges and needn't reach their ends.
All inputs are finite; a program needn't handle non-finite values.
Results may differ from the reference program's by a relative error of at most 0.0018.
Values may be sent and summed in bfloat16 or wider, within the bound.
No kernel may reach another device: no remote copies, remote signals or barrier semaphores. Data moves between devices by JAX's collectives and lax.ppermute only.
A program may use at most 64 MiB of HBM per device.

```python
import math
import jax
import jax.numpy as jnp
from jax import lax

NT = 256
NF = 128
RHS = 2
SWEEPS = 4
GY = 384
NS = 128
GX = 2
NP = 768


def plant(values, stream_key, least, largest):
    place = [jax.random.randint(jax.random.fold_in(stream_key, axis), (), 0, length) for axis, length in enumerate(values.shape)]
    main_axis = values.shape.index(max(values.shape))
    beside = place[:main_axis] + [(place[main_axis] + 1) % values.shape[main_axis]] + place[main_axis + 1:]
    return values.at[tuple(place)].set(least).at[tuple(beside)].set(largest)


def levels(own_key, dims, shards, least, high):
    factor_of, own = 1.0, jax.random.fold_in(own_key, 6)
    for dim, parts in shards:
        draws = jnp.exp(jax.random.uniform(jax.random.fold_in(own, dim), (parts,), jnp.float32, least / len(shards), high / len(shards)))
        factor_of = factor_of * jnp.repeat(draws, dims[dim] // parts).reshape([-1 if axis == dim else 1 for axis in range(len(dims))])
    return factor_of


def centred(own_key, dims, spread, most, split=(), kind=jnp.bfloat16):
    entries = spread * jax.random.normal(own_key, dims, jnp.float32)
    if split:
        entries = entries * levels(own_key, dims, split, -0.22, 0.18)
    return jnp.clip(entries, -most, most).astype(kind)


def setup_inputs(seed: int = 0) -> dict:
    arg_keys = jax.random.split(jax.random.key(seed), 7)
    return {
        "vectors": centred(arg_keys[0], (RHS, NS, NT), 1.0, 6.0, ((1, 16),), jnp.float32),
        "observed": centred(arg_keys[1], (RHS, NS, NT), 1.0, 6.0, ((1, 16),), jnp.float32),
        "operator": centred(arg_keys[2], (2, NF, NS, NP), (NP // 4) ** -0.5, 0.4375, ((2, 16), (3, 2))),
        "noise": jnp.clip(jnp.exp(math.log(3.0) - 2.3025851 * jax.random.uniform(arg_keys[3], (NS,), jnp.float32) ** levels(arg_keys[3], (NS,), ((0, 16),), -0.2, 0.2)), 0.3, 3.0),
        "coefficient": jnp.clip(0.05 + 0.19 * jax.random.uniform(arg_keys[4], (GX, GY), jnp.float32) ** levels(arg_keys[4], (GX, GY), ((0, 2),), -0.2, 0.2), 0.05, 0.24),
        "offsets": plant(jax.random.randint(arg_keys[5], (GX, GY), -3, 4), jax.random.fold_in(arg_keys[5], 1), -3, 3).astype(jnp.int32),
    }


def make_basis(length):
    half = length // 2
    times = jnp.arange(length, dtype=jnp.int32)[:, None]
    freqs = jnp.arange(half, dtype=jnp.int32)[None, :]
    phase = (2 * freqs + 1) * times % (2 * length)
    angle = phase.astype(jnp.float32) * (math.pi / length)
    scale = math.sqrt(2.0 / length)
    return jnp.concatenate([jnp.cos(angle), jnp.sin(angle)], axis=1) * scale

def smooth(field, coefficient, offsets):
    width = field.shape[-1]
    for sweep in range(SWEEPS):
        padded = jnp.pad(field, ((0, 0), (0, 0), (0, 0), (1, 1), (0, 0)))
        upper = padded[..., :-2, :]
        lower = padded[..., 2:, :]
        lower_pad = jnp.pad(lower, ((0, 0), (0, 0), (0, 0), (0, 0), (3, 3)))
        linked = jnp.zeros_like(field)
        for shift in range(-3, 4):
            linked = linked + jnp.where(offsets == shift, lower_pad[..., 3 + shift:3 + shift + width], 0.0)
        sides = jnp.pad(field, ((0, 0), (0, 0), (0, 0), (0, 0), (1, 1)))
        field = field + coefficient * (sides[..., :-2] + sides[..., 2:] + upper + linked - 4.0 * field)
    return field

def hessian(record, operator, noise, coefficient, offsets, basis):
    rows, sensors, length = record.shape
    half = length // 2
    spectrum = jnp.dot(record.reshape(rows * sensors, length), basis, precision=lax.Precision.HIGHEST)
    spectrum = spectrum.reshape(rows, sensors, 2, half).transpose(2, 3, 0, 1).astype(jnp.bfloat16)

    def adjoint_one(freq):
        resp = lax.dynamic_index_in_dim(operator, freq, 1, keepdims=False)
        spec = lax.dynamic_index_in_dim(spectrum, freq, 1, keepdims=False)
        real = jnp.dot(spec[0], resp[0], preferred_element_type=jnp.float32) + jnp.dot(spec[1], resp[1], preferred_element_type=jnp.float32)
        imag = jnp.dot(spec[1], resp[0], preferred_element_type=jnp.float32) - jnp.dot(spec[0], resp[1], preferred_element_type=jnp.float32)
        return jnp.stack([real, imag])
    adjoint = lax.map(adjoint_one, jnp.arange(half, dtype=jnp.int32))
    cells = adjoint.shape[-1]
    field = jnp.moveaxis(adjoint, 0, 1).reshape(2, half, rows, cells // GY, GY)
    prior = smooth(field, coefficient, offsets).astype(jnp.bfloat16).reshape(2, half, rows, cells)

    def forward_one(freq):
        resp = lax.dynamic_index_in_dim(operator, freq, 1, keepdims=False)
        par = lax.dynamic_index_in_dim(prior, freq, 1, keepdims=False)
        real = jnp.dot(par[0], resp[0].T, preferred_element_type=jnp.float32) - jnp.dot(par[1], resp[1].T, preferred_element_type=jnp.float32)
        imag = jnp.dot(par[1], resp[0].T, preferred_element_type=jnp.float32) + jnp.dot(par[0], resp[1].T, preferred_element_type=jnp.float32)
        return jnp.stack([real, imag])
    forward = lax.map(forward_one, jnp.arange(half, dtype=jnp.int32))
    forward = forward.transpose(2, 3, 1, 0).reshape(rows * sensors, length)
    back = jnp.dot(forward, basis.T, precision=lax.Precision.HIGHEST).reshape(rows, sensors, length)
    return back + noise[None, :, None] * record

def reference(vectors, observed, operator, noise, coefficient, offsets):
    basis = make_basis(vectors.shape[-1])
    residual = observed - hessian(vectors, operator, noise, coefficient, offsets, basis)
    applied = hessian(residual, operator, noise, coefficient, offsets, basis)
    return (residual, applied)
```

```python
import math

import jax
import jax.numpy as jnp
import numpy as np
from jax import lax
from jax.sharding import PartitionSpec as P

SWEEPS = 4
REACH = 3


def make_basis(length):
    half = length // 2
    times = np.arange(length)[:, None]
    freqs = np.arange(half)[None, :]
    phase = (2 * freqs + 1) * times % (2 * length)
    angle = phase.astype(np.float64) * (math.pi / length)
    scale = math.sqrt(2.0 / length)
    return (np.concatenate([np.cos(angle), np.sin(angle)], axis=1) * scale).astype(np.float32)


def halo(field, axis, dim):
    count = lax.axis_size(axis)
    if count == 1:
        edge = jnp.zeros_like(lax.slice_in_dim(field, 0, 1, axis=dim))
        return jnp.concatenate([edge, field, edge], axis=dim)
    ends = count - 1
    head = lax.slice_in_dim(field, 0, 1, axis=dim)
    tail = lax.slice_in_dim(field, field.shape[dim] - 1, field.shape[dim], axis=dim)
    return jnp.concatenate(
        [
            lax.ppermute(tail, axis, [(i, i + 1) for i in range(ends)]),
            field,
            lax.ppermute(head, axis, [(i + 1, i) for i in range(ends)]),
        ],
        axis=dim,
    )


def zero_halo(field):
    return jnp.pad(field, [(0, 0)] * (field.ndim - 2) + [(1, 1), (0, 0)])


def smooth(field, coefficient, offsets, extend):
    width = field.shape[-1]
    lead = [(0, 0)] * (field.ndim - 1)
    for _ in range(SWEEPS):
        padded = extend(field)
        upper = padded[..., :-2, :]
        lower = jnp.pad(padded[..., 2:, :], lead + [(REACH, REACH)])
        linked = jnp.zeros_like(field)
        for shift in range(-REACH, REACH + 1):
            start = REACH + shift
            linked = linked + jnp.where(offsets == shift, lower[..., start : start + width], 0.0)
        sides = jnp.pad(field, lead + [(1, 1)])
        field = field + coefficient * (
            sides[..., :-2] + sides[..., 2:] + upper + linked - 4.0 * field
        )
    return field


def apply_part(spectrum, operator, coefficient, offsets, extend):
    low = spectrum.astype(jnp.bfloat16)

    def adjoint_of(spec, resp):
        return jnp.einsum("frs,fsp->frp", spec, resp, preferred_element_type=jnp.float32)

    def forward_of(par, resp):
        return jnp.einsum("frp,fsp->frs", par, resp, preferred_element_type=jnp.float32)

    real = adjoint_of(low[0], operator[0]) + adjoint_of(low[1], operator[1])
    imag = adjoint_of(low[1], operator[0]) - adjoint_of(low[0], operator[1])
    adjoint = jnp.stack([real, imag])
    grid = adjoint.reshape(adjoint.shape[:3] + coefficient.shape)
    prior = smooth(grid, coefficient, offsets, extend).astype(jnp.bfloat16)
    prior = prior.reshape(adjoint.shape)
    real = forward_of(prior[0], operator[0]) - forward_of(prior[1], operator[1])
    imag = forward_of(prior[1], operator[0]) + forward_of(prior[0], operator[1])
    return jnp.stack([real, imag])


def body(vectors, observed, operator, noise, coefficient, offsets):
    sen, par = lax.axis_size("sen"), lax.axis_size("par")
    rows, sensors, length = vectors.shape
    half = length // 2
    grid_rows, width = coefficient.shape
    basis = jnp.asarray(make_basis(length))
    both = jnp.stack([vectors, observed])
    spectra = jnp.dot(
        both.reshape(2 * rows * sensors, length), basis, precision=lax.Precision.HIGHEST
    )
    spectra = spectra.reshape(2, rows, sensors, 2, half)
    whole_cells = half % (sen * par) == 0
    axes = ("sen", "par") if whole_cells else "sen"
    shares = sen * par if whole_cells else sen
    each = half // shares

    cut = operator.reshape(2, shares, each, sensors, grid_rows, width)
    cut = lax.all_to_all(cut, axes, 1, 1, tiled=True)
    if whole_cells:
        resp = cut.reshape(2, sen, par, each, sensors, grid_rows, width)
        resp = resp.transpose(0, 3, 1, 4, 2, 5, 6)
        resp = resp.reshape(2, each, sen * sensors, par * grid_rows * width)
        coefficient = lax.all_gather(coefficient, "par", tiled=True)
        offsets = lax.all_gather(offsets, "par", tiled=True)
        extend = zero_halo
    else:
        resp = cut.transpose(0, 2, 1, 3, 4, 5)
        resp = resp.reshape(2, each, sen * sensors, grid_rows * width)
        extend = lambda field: halo(field, "par", field.ndim - 2)

    def to_frequencies(spec):
        parts = spec.shape[0]
        cut = spec.reshape(parts, rows, sensors, 2, shares, each)
        cut = lax.all_to_all(cut.transpose(4, 0, 3, 5, 1, 2), axes, 0, 0, tiled=True)
        if whole_cells:
            cut = cut.reshape((sen, par) + cut.shape[1:])[:, 0]
        return cut.transpose(1, 2, 3, 4, 0, 5).reshape(parts, 2, each, rows, sen * sensors)

    def to_sensors(spec):
        parts = spec.shape[0]
        cut = spec.reshape(parts, 2, each, rows, sen, sensors).transpose(4, 0, 3, 5, 1, 2)
        if whole_cells:
            cut = jnp.repeat(cut, par, axis=0)
        cut = lax.all_to_all(cut, axes, 0, 0, tiled=True)
        return cut.transpose(1, 2, 3, 4, 0, 5).reshape(parts, rows, sensors, 2 * half)

    def hessian(spectrum):
        forward = apply_part(spectrum, resp, coefficient, offsets, extend)
        return forward if whole_cells else lax.psum(forward, "par")

    rest = spectra[1] - noise[None, :, None, None] * spectra[0]
    own, rest = to_frequencies(jnp.stack([spectra[0], rest]))
    left = rest - hessian(own)
    again = hessian(left)
    home = to_sensors(jnp.stack([left, again]))
    back = jnp.dot(
        home.reshape(2 * rows * sensors, length), basis.T, precision=lax.Precision.HIGHEST
    ).reshape(2, rows, sensors, length)
    residual = back[0]
    applied = back[1] + noise[None, :, None] * residual
    return (residual, applied)


def solution(mesh):
    placed = (
        P(None, "sen", None),
        P(None, "sen", None),
        P(None, None, "sen", "par"),
        P("sen"),
        P("par", None),
        P("par", None),
    )
    return jax.shard_map(
        body,
        mesh=mesh,
        in_specs=placed,
        out_specs=(P(None, "sen", None), P(None, "sen", None)),
        check_vma=False,
    )
```

```python
import math

import jax
import jax.numpy as jnp
import numpy as np
from jax import lax
from jax.experimental import pallas as pl
from jax.experimental.pallas import tpu as pltpu
from jax.sharding import PartitionSpec as P

SWEEPS = 4
REACH = 3


def make_basis(length):
    half = length // 2
    times = np.arange(length)[:, None]
    freqs = np.arange(half)[None, :]
    phase = (2 * freqs + 1) * times % (2 * length)
    angle = phase.astype(np.float64) * (math.pi / length)
    scale = math.sqrt(2.0 / length)
    return (np.concatenate([np.cos(angle), np.sin(angle)], axis=1) * scale).astype(np.float32)


def halo(field, axis, dim):
    count = lax.axis_size(axis)
    if count == 1:
        edge = jnp.zeros_like(lax.slice_in_dim(field, 0, 1, axis=dim))
        return jnp.concatenate([edge, field, edge], axis=dim)
    ends = count - 1
    head = lax.slice_in_dim(field, 0, 1, axis=dim)
    tail = lax.slice_in_dim(field, field.shape[dim] - 1, field.shape[dim], axis=dim)
    return jnp.concatenate(
        [
            lax.ppermute(tail, axis, [(i, i + 1) for i in range(ends)]),
            field,
            lax.ppermute(head, axis, [(i + 1, i) for i in range(ends)]),
        ],
        axis=dim,
    )


def zero_halo(field):
    return jnp.pad(field, [(0, 0)] * (field.ndim - 2) + [(1, 1), (0, 0)])


def smooth(field, coefficient, offsets, extend):
    width = field.shape[-1]
    lead = [(0, 0)] * (field.ndim - 1)
    for _ in range(SWEEPS):
        padded = extend(field)
        upper = padded[..., :-2, :]
        lower = jnp.pad(padded[..., 2:, :], lead + [(REACH, REACH)])
        linked = jnp.zeros_like(field)
        for shift in range(-REACH, REACH + 1):
            start = REACH + shift
            linked = linked + jnp.where(offsets == shift, lower[..., start : start + width], 0.0)
        sides = jnp.pad(field, lead + [(1, 1)])
        field = field + coefficient * (
            sides[..., :-2] + sides[..., 2:] + upper + linked - 4.0 * field
        )
    return field


def apply_part(spectrum, operator, coefficient, offsets, extend):
    low = spectrum.astype(jnp.bfloat16)

    def adjoint_of(spec, resp):
        return jnp.einsum("frs,fsp->frp", spec, resp, preferred_element_type=jnp.float32)

    def forward_of(par, resp):
        return jnp.einsum("frp,fsp->frs", par, resp, preferred_element_type=jnp.float32)

    real = adjoint_of(low[0], operator[0]) + adjoint_of(low[1], operator[1])
    imag = adjoint_of(low[1], operator[0]) - adjoint_of(low[0], operator[1])
    adjoint = jnp.stack([real, imag])
    grid = adjoint.reshape(adjoint.shape[:3] + coefficient.shape)
    prior = smooth(grid, coefficient, offsets, extend).astype(jnp.bfloat16)
    prior = prior.reshape(adjoint.shape)
    real = forward_of(prior[0], operator[0]) - forward_of(prior[1], operator[1])
    imag = forward_of(prior[1], operator[0]) + forward_of(prior[0], operator[1])
    return jnp.stack([real, imag])


def body_plain(vectors, observed, operator, noise, coefficient, offsets):
    sen, par = lax.axis_size("sen"), lax.axis_size("par")
    rows, sensors, length = vectors.shape
    half = length // 2
    grid_rows, width = coefficient.shape
    basis = jnp.asarray(make_basis(length))
    both = jnp.stack([vectors, observed])
    spectra = jnp.dot(
        both.reshape(2 * rows * sensors, length), basis, precision=lax.Precision.HIGHEST
    )
    spectra = spectra.reshape(2, rows, sensors, 2, half)
    whole_cells = half % (sen * par) == 0
    axes = ("sen", "par") if whole_cells else "sen"
    shares = sen * par if whole_cells else sen
    each = half // shares

    cut = operator.reshape(2, shares, each, sensors, grid_rows, width)
    cut = lax.all_to_all(cut, axes, 1, 1, tiled=True)
    if whole_cells:
        resp = cut.reshape(2, sen, par, each, sensors, grid_rows, width)
        resp = resp.transpose(0, 3, 1, 4, 2, 5, 6)
        resp = resp.reshape(2, each, sen * sensors, par * grid_rows * width)
        coefficient = lax.all_gather(coefficient, "par", tiled=True)
        offsets = lax.all_gather(offsets, "par", tiled=True)
        extend = zero_halo
    else:
        resp = cut.transpose(0, 2, 1, 3, 4, 5)
        resp = resp.reshape(2, each, sen * sensors, grid_rows * width)
        extend = lambda field: halo(field, "par", field.ndim - 2)

    def to_frequencies(spec):
        parts = spec.shape[0]
        cut = spec.reshape(parts, rows, sensors, 2, shares, each)
        cut = lax.all_to_all(cut.transpose(4, 0, 3, 5, 1, 2), axes, 0, 0, tiled=True)
        if whole_cells:
            cut = cut.reshape((sen, par) + cut.shape[1:])[:, 0]
        return cut.transpose(1, 2, 3, 4, 0, 5).reshape(parts, 2, each, rows, sen * sensors)

    def to_sensors(spec):
        parts = spec.shape[0]
        cut = spec.reshape(parts, 2, each, rows, sen, sensors).transpose(4, 0, 3, 5, 1, 2)
        if whole_cells:
            cut = jnp.repeat(cut, par, axis=0)
        cut = lax.all_to_all(cut, axes, 0, 0, tiled=True)
        return cut.transpose(1, 2, 3, 4, 0, 5).reshape(parts, rows, sensors, 2 * half)

    def hessian(spectrum):
        forward = apply_part(spectrum, resp, coefficient, offsets, extend)
        return forward if whole_cells else lax.psum(forward, "par")

    rest = spectra[1] - noise[None, :, None, None] * spectra[0]
    own, rest = to_frequencies(jnp.stack([spectra[0], rest]))
    left = rest - hessian(own)
    again = hessian(left)
    home = to_sensors(jnp.stack([left, again]))
    back = jnp.dot(
        home.reshape(2 * rows * sensors, length), basis.T, precision=lax.Precision.HIGHEST
    ).reshape(2, rows, sensors, length)
    residual = back[0]
    applied = back[1] + noise[None, :, None] * residual
    return (residual, applied)


def roll(x, shift, axis):
    size = x.shape[axis]
    return x if shift % size == 0 else pltpu.roll(x, shift % size, axis)


def iota(shape, axis):
    return lax.broadcasted_iota(jnp.int32, shape, axis)


def local_kernel(resp_ref, own_ref, rest_ref, coef_ref, link_ref, out_ref):
    sen, par, each, pair, width = resp_ref.shape
    sensors = pair // 2
    lines, lanes = own_ref.shape
    row, lane = iota((lines, lanes), 0), iota((lines, lanes), 1)
    real_row = row % 2 == 0
    real_lane = lane // sensors % 2 == 0
    freq = row // 2 % each

    def swapped(x):
        return jnp.where(real_row, roll(x, -1, 0), roll(x, 1, 0))

    shape = (lines, width)
    column = iota(shape, 1)
    coefs, links = [], []
    for x in range(par):
        coefs.append(jnp.broadcast_to(coef_ref[x : x + 1, :], shape))
        offset = jnp.broadcast_to(link_ref[x : x + 1, :], shape)
        masks = []
        for shift in range(-REACH, REACH + 1):
            inside = (column + shift >= 0) & (column + shift < width)
            masks.append(jnp.where((offset == shift) & inside, 1.0, 0.0))
        links.append(masks)
    after_first = jnp.where(column > 0, 1.0, 0.0)
    before_last = jnp.where(column < width - 1, 1.0, 0.0)

    def block(f, p):
        return resp_ref[:, p, f].reshape(sen * pair, width)

    def hessian(left):
        field = []
        for p in range(par):
            total = jnp.zeros(shape, jnp.float32)
            for f in range(each):
                part = jnp.where(freq == f, left, 0.0).astype(jnp.bfloat16)
                total += jnp.dot(part, block(f, p), preferred_element_type=jnp.float32)
            field.append(total)
        for _ in range(SWEEPS):
            after = []
            for x, u in enumerate(field):
                around = roll(u, 1, 1) * after_first + roll(u, -1, 1) * before_last
                if x > 0:
                    around += field[x - 1]
                if x < par - 1:
                    linked = jnp.zeros(shape, jnp.float32)
                    for mask, shift in zip(links[x], range(-REACH, REACH + 1)):
                        linked += mask * roll(field[x + 1], -shift, 1)
                    around += linked
                after.append(u + coefs[x] * (around - 4.0 * u))
            field = after
        prior = [u.astype(jnp.bfloat16) for u in field]
        out = jnp.zeros((lines, lanes), jnp.float32)
        for f in range(each):
            part = jnp.zeros((lines, lanes), jnp.float32)
            for p in range(par):
                part += lax.dot_general(
                    prior[p], block(f, p), (((1,), (1,)), ((), ())), preferred_element_type=jnp.float32
                )
            out = jnp.where(freq == f, part, out)
        crossed = swapped(roll(out, -sensors, 1))
        return out + jnp.where(real_row, -crossed, crossed)

    left = rest_ref[...] - hessian(own_ref[...])
    crossed = swapped(left)
    crossed = roll(jnp.where(real_row, crossed, -crossed), sensors, 1)
    again = hessian(jnp.where(real_lane, left, crossed))
    both = jnp.where(real_lane, left, roll(again, sensors, 1))

    count = 2 * each
    wide = count * pair
    to, group = iota((count, wide), 0), iota((count, wide), 1) // pair
    for r in range(lines // count):
        for h in range(lanes // wide):
            tile = both[r * count : (r + 1) * count, h * wide : (h + 1) * wide]
            moved = tile
            for turn in range(1, count):
                turned = roll(roll(tile, -turn, 0), turn * pair, 1)
                moved = jnp.where((group - to + count) % count == turn, turned, moved)
            for i in range(count):
                for p in range(par):
                    out_ref[(h * count + i) * par + p, r : r + 1, :] = moved[i : i + 1, :]


def home_kernel(got_ref, basis_ref, noise_ref, residual_ref, applied_ref):
    sources, rows, wide = got_ref.shape
    sensors = noise_ref.shape[0]
    pair = 2 * sensors
    lines = []
    for r in range(rows):
        turned = got_ref[:, r, :].T
        lines.append(
            jnp.concatenate([turned[i : i + pair, :] for i in range(0, wide, pair)], axis=1)
        )
    back = jnp.dot(
        jnp.concatenate(lines, axis=0),
        basis_ref[...],
        precision=lax.Precision.HIGHEST,
        preferred_element_type=jnp.float32,
    )
    for r in range(rows):
        residual = back[r * pair : r * pair + sensors]
        residual_ref[r] = residual
        applied_ref[r] = back[r * pair + sensors : (r + 1) * pair] + noise_ref[...] * residual


def body_fast(vectors, observed, operator, noise, coefficient, offsets):
    sen, par = lax.axis_size("sen"), lax.axis_size("par")
    rows, sensors, length = vectors.shape
    half = length // 2
    width = coefficient.shape[1]
    shares = sen * par
    each = half // shares
    pair = 2 * sensors
    axes = ("sen", "par")
    basis = make_basis(length)

    cut = operator.reshape(2, shares, each, sensors, width).transpose(1, 2, 0, 3, 4)
    cut = cut.reshape(shares, each, pair, width)
    cut, vectors, observed, coefficient, offsets = lax.optimization_barrier(
        (cut, vectors, observed, coefficient, offsets)
    )
    resp = lax.all_to_all(cut, axes, 0, 0, tiled=True)
    resp = resp.reshape(sen, par, each, pair, width)

    both = jnp.stack([vectors, observed])
    spectra = jnp.dot(
        both.reshape(2 * rows * sensors, length), basis, precision=lax.Precision.HIGHEST
    )
    spectra = spectra.reshape(2, rows, sensors, 2, shares, each)
    rest = spectra[1] - noise[None, :, None, None, None] * spectra[0]
    spectra = jnp.stack([spectra[0], rest]).transpose(4, 0, 1, 5, 3, 2)
    spectra = lax.all_to_all(
        spectra.reshape(shares, 1, 4 * rows * each * sensors), axes, 0, 0, tiled=True
    )
    spectra = spectra.reshape(sen, par, 2, rows, each, 2, sensors)[:, 0]
    own, rest = spectra.transpose(1, 2, 3, 4, 0, 5)
    other = jnp.stack([own[:, :, 1], -own[:, :, 0]], axis=2)
    lines, lanes = rows * each * 2, sen * pair
    own = jnp.stack([own, other], axis=4).reshape(lines, lanes)
    rest = jnp.stack([rest, jnp.zeros_like(rest)], axis=4).reshape(lines, lanes)
    grid = jnp.concatenate([coefficient, offsets.astype(jnp.float32)])
    grid = lax.all_gather(grid, "par").transpose(1, 0, 2)

    message = pl.pallas_call(
        local_kernel,
        out_shape=jax.ShapeDtypeStruct((shares, rows, 2 * each * pair), jnp.float32),
        compiler_params=pltpu.CompilerParams(vmem_limit_bytes=32 * 2**20),
        name="local_hessians",
    )(resp, own, rest, grid[0], grid[1].astype(jnp.int32))
    got = lax.all_to_all(message, axes, 0, 0, tiled=True)
    turned = basis.reshape(length, 2, shares, each).transpose(3, 1, 2, 0).reshape(length, length)
    return pl.pallas_call(
        home_kernel,
        out_shape=[jax.ShapeDtypeStruct((rows, sensors, length), jnp.float32)] * 2,
        name="to_time",
    )(got, jnp.asarray(turned), noise[:, None])


def fits(mesh, args):
    vectors, _, _, _, coefficient, _ = args
    sen, par = mesh.shape["sen"], mesh.shape["par"]
    rows, sensors, length = vectors.shape
    half = length // 2
    if half % (sen * par) or sensors % sen or coefficient.shape[0] != par:
        return False
    each, pair = half // (sen * par), 2 * (sensors // sen)
    return 2 * each * pair == 128 and 2 * each == 8 and sen * pair % 128 == 0 and coefficient.shape[1] % 128 == 0


def solution(mesh):
    placed = (
        P(None, "sen", None),
        P(None, "sen", None),
        P(None, None, "sen", "par"),
        P("sen"),
        P("par", None),
        P("par", None),
    )

    def whole(*args):
        return jax.shard_map(
            body_fast if fits(mesh, args) else body_plain,
            mesh=mesh,
            in_specs=placed,
            out_specs=(P(None, "sen", None), P(None, "sen", None)),
            check_vma=False,
        )(*args)

    return whole
```

```python
import functools
import math

import jax
import jax.numpy as jnp
import numpy as np
from jax import lax
from jax.experimental import pallas as pl
from jax.experimental.pallas import tpu as pltpu
from jax.sharding import PartitionSpec as P

SWEEPS = 4
REACH = 3


def make_basis(length):
    half = length // 2
    times = np.arange(length)[:, None]
    freqs = np.arange(half)[None, :]
    phase = (2 * freqs + 1) * times % (2 * length)
    angle = phase.astype(np.float64) * (math.pi / length)
    scale = math.sqrt(2.0 / length)
    return (np.concatenate([np.cos(angle), np.sin(angle)], axis=1) * scale).astype(np.float32)


def halo(field, axis, dim):
    count = lax.axis_size(axis)
    if count == 1:
        edge = jnp.zeros_like(lax.slice_in_dim(field, 0, 1, axis=dim))
        return jnp.concatenate([edge, field, edge], axis=dim)
    ends = count - 1
    head = lax.slice_in_dim(field, 0, 1, axis=dim)
    tail = lax.slice_in_dim(field, field.shape[dim] - 1, field.shape[dim], axis=dim)
    return jnp.concatenate(
        [
            lax.ppermute(tail, axis, [(i, i + 1) for i in range(ends)]),
            field,
            lax.ppermute(head, axis, [(i + 1, i) for i in range(ends)]),
        ],
        axis=dim,
    )


def zero_halo(field):
    return jnp.pad(field, [(0, 0)] * (field.ndim - 2) + [(1, 1), (0, 0)])


def smooth(field, coefficient, offsets, extend):
    width = field.shape[-1]
    lead = [(0, 0)] * (field.ndim - 1)
    for _ in range(SWEEPS):
        padded = extend(field)
        upper = padded[..., :-2, :]
        lower = jnp.pad(padded[..., 2:, :], lead + [(REACH, REACH)])
        linked = jnp.zeros_like(field)
        for shift in range(-REACH, REACH + 1):
            start = REACH + shift
            linked = linked + jnp.where(offsets == shift, lower[..., start : start + width], 0.0)
        sides = jnp.pad(field, lead + [(1, 1)])
        field = field + coefficient * (
            sides[..., :-2] + sides[..., 2:] + upper + linked - 4.0 * field
        )
    return field


def apply_part(spectrum, operator, coefficient, offsets, extend):
    low = spectrum.astype(jnp.bfloat16)

    def adjoint_of(spec, resp):
        return jnp.einsum("frs,fsp->frp", spec, resp, preferred_element_type=jnp.float32)

    def forward_of(par, resp):
        return jnp.einsum("frp,fsp->frs", par, resp, preferred_element_type=jnp.float32)

    real = adjoint_of(low[0], operator[0]) + adjoint_of(low[1], operator[1])
    imag = adjoint_of(low[1], operator[0]) - adjoint_of(low[0], operator[1])
    adjoint = jnp.stack([real, imag])
    grid = adjoint.reshape(adjoint.shape[:3] + coefficient.shape)
    prior = smooth(grid, coefficient, offsets, extend).astype(jnp.bfloat16)
    prior = prior.reshape(adjoint.shape)
    real = forward_of(prior[0], operator[0]) - forward_of(prior[1], operator[1])
    imag = forward_of(prior[1], operator[0]) + forward_of(prior[0], operator[1])
    return jnp.stack([real, imag])


def body_plain(vectors, observed, operator, noise, coefficient, offsets):
    sen, par = lax.axis_size("sen"), lax.axis_size("par")
    rows, sensors, length = vectors.shape
    half = length // 2
    grid_rows, width = coefficient.shape
    basis = jnp.asarray(make_basis(length))
    both = jnp.stack([vectors, observed])
    spectra = jnp.dot(
        both.reshape(2 * rows * sensors, length), basis, precision=lax.Precision.HIGHEST
    )
    spectra = spectra.reshape(2, rows, sensors, 2, half)
    whole_cells = half % (sen * par) == 0
    axes = ("sen", "par") if whole_cells else "sen"
    shares = sen * par if whole_cells else sen
    each = half // shares

    cut = operator.reshape(2, shares, each, sensors, grid_rows, width)
    cut = lax.all_to_all(cut, axes, 1, 1, tiled=True)
    if whole_cells:
        resp = cut.reshape(2, sen, par, each, sensors, grid_rows, width)
        resp = resp.transpose(0, 3, 1, 4, 2, 5, 6)
        resp = resp.reshape(2, each, sen * sensors, par * grid_rows * width)
        coefficient = lax.all_gather(coefficient, "par", tiled=True)
        offsets = lax.all_gather(offsets, "par", tiled=True)
        extend = zero_halo
    else:
        resp = cut.transpose(0, 2, 1, 3, 4, 5)
        resp = resp.reshape(2, each, sen * sensors, grid_rows * width)
        extend = lambda field: halo(field, "par", field.ndim - 2)

    def to_frequencies(spec):
        parts = spec.shape[0]
        cut = spec.reshape(parts, rows, sensors, 2, shares, each)
        cut = lax.all_to_all(cut.transpose(4, 0, 3, 5, 1, 2), axes, 0, 0, tiled=True)
        if whole_cells:
            cut = cut.reshape((sen, par) + cut.shape[1:])[:, 0]
        return cut.transpose(1, 2, 3, 4, 0, 5).reshape(parts, 2, each, rows, sen * sensors)

    def to_sensors(spec):
        parts = spec.shape[0]
        cut = spec.reshape(parts, 2, each, rows, sen, sensors).transpose(4, 0, 3, 5, 1, 2)
        if whole_cells:
            cut = jnp.repeat(cut, par, axis=0)
        cut = lax.all_to_all(cut, axes, 0, 0, tiled=True)
        return cut.transpose(1, 2, 3, 4, 0, 5).reshape(parts, rows, sensors, 2 * half)

    def hessian(spectrum):
        forward = apply_part(spectrum, resp, coefficient, offsets, extend)
        return forward if whole_cells else lax.psum(forward, "par")

    rest = spectra[1] - noise[None, :, None, None] * spectra[0]
    own, rest = to_frequencies(jnp.stack([spectra[0], rest]))
    left = rest - hessian(own)
    again = hessian(left)
    home = to_sensors(jnp.stack([left, again]))
    back = jnp.dot(
        home.reshape(2 * rows * sensors, length), basis.T, precision=lax.Precision.HIGHEST
    ).reshape(2, rows, sensors, length)
    residual = back[0]
    applied = back[1] + noise[None, :, None] * residual
    return (residual, applied)


def roll(x, shift, axis):
    size = x.shape[axis]
    return x if shift % size == 0 else pltpu.roll(x, shift % size, axis)


def iota(shape, axis):
    return lax.broadcasted_iota(jnp.int32, shape, axis)


def outbound_kernel(resp_ref, vectors_ref, observed_ref, noise_ref, basis_ref, out_ref, spectra_ref):
    _, devices, each, sensors, width = resp_ref.shape
    pair, lines = 2 * sensors, 2 * each
    wide = out_ref.shape[2]
    tiles = width // wide

    @pl.when(pl.program_id(0) == 0)
    def _():
        rows = vectors_ref.shape[0]
        records = []
        for r in range(rows):
            record = vectors_ref[r]
            records += [record, observed_ref[r] - noise_ref[...] * record]
        filled = rows * pair
        records.append(jnp.zeros((wide - filled, records[0].shape[1]), jnp.float32))
        spectra = lax.dot_general(
            basis_ref[...],
            jnp.concatenate(records, axis=0),
            (((1,), (1,)), ((), ())),
            precision=lax.Precision.HIGHEST,
            preferred_element_type=jnp.float32,
        )
        exact = iota(spectra.shape, 1) // sensors % 2 == 1
        high = spectra.astype(jnp.bfloat16).astype(jnp.float32)
        rest = jnp.where(exact, spectra - high, 0.0)
        middle = rest.astype(jnp.bfloat16).astype(jnp.float32)
        low = (rest - middle).astype(jnp.bfloat16).astype(jnp.float32)
        packed = high + roll(middle, filled, 1) + roll(low, 2 * filled, 1)
        spectra_ref[...] = packed.reshape(spectra_ref.shape)

    for f in range(each):
        for j in range(tiles):
            lanes = pl.ds(j * wide, wide)
            part = jnp.concatenate([resp_ref[0, :, f, :, lanes], resp_ref[1, :, f, :, lanes]], axis=1)
            out_ref[:, pl.ds((f * tiles + j) * pair, pair), :] = part
    first = pl.multiple_of(pl.program_id(0) * devices, devices)
    out_ref[:, pl.ds(each * tiles * pair, lines), :] = spectra_ref[pl.ds(first, devices)].astype(
        jnp.bfloat16
    )


def local_kernel(each, got_ref, coef_ref, link_ref, out_ref):
    sen, par, _, wide = got_ref.shape
    width = coef_ref.shape[1]
    tiles = width // wide
    rows = out_ref.shape[1]
    lines = 2 * each
    pair = wide // lines
    sensors = pair // 2
    held, lanes = rows * lines, sen * pair
    per = wide // pair
    body_rows = each * tiles * pair

    tail = got_ref[:, 0, pl.ds(body_rows, lines), :].astype(jnp.float32)
    parts = rows * pair
    at = iota((lines, wide), 1) // pair
    spectra = [[jnp.zeros((lines, wide), jnp.float32) for _ in range(lanes // wide)] for _ in range(rows)]
    for i in range(sen):
        packed = tail[i]
        packed = packed + roll(packed, -parts, 1) + roll(packed, -2 * parts, 1)
        h, place = divmod(i, per)
        for r in range(rows):
            moved = roll(packed, (place - r) * pair, 1)
            spectra[r][h] = jnp.where(at == place, moved, spectra[r][h])
    spectra = jnp.concatenate([jnp.concatenate(line, axis=1) for line in spectra], axis=0)

    row, lane = iota((held, lanes), 0), iota((held, lanes), 1)
    real_row = row % 2 == 0
    real_lane = lane // sensors % 2 == 0
    freq = row // 2 % each

    def swapped(x):
        return jnp.where(real_row, roll(x, -1, 0), roll(x, 1, 0))

    shape = (held, width)
    column = iota(shape, 1)
    coefs, links = [], []
    for x in range(par):
        coefs.append(jnp.broadcast_to(coef_ref[x : x + 1, :], shape))
        offset = jnp.broadcast_to(link_ref[x : x + 1, :], shape)
        masks = []
        for shift in range(-REACH, REACH + 1):
            inside = (column + shift >= 0) & (column + shift < width)
            masks.append(jnp.where((offset == shift) & inside, 1.0, 0.0))
        links.append(masks)
    after_first = jnp.where(column > 0, 1.0, 0.0)
    before_last = jnp.where(column < width - 1, 1.0, 0.0)

    def block(f, p):
        return jnp.concatenate(
            [
                got_ref[:, p, pl.ds((f * tiles + j) * pair, pair), :].reshape(lanes, wide)
                for j in range(tiles)
            ],
            axis=1,
        )

    def hessian(record):
        crossed = swapped(record)
        crossed = roll(jnp.where(real_row, crossed, -crossed), sensors, 1)
        left = jnp.where(real_lane, record, crossed)
        field = []
        for p in range(par):
            total = jnp.zeros(shape, jnp.float32)
            for f in range(each):
                part = jnp.where(freq == f, left, 0.0).astype(jnp.bfloat16)
                total += jnp.dot(part, block(f, p), preferred_element_type=jnp.float32)
            field.append(total)
        for _ in range(SWEEPS):
            after = []
            for x, u in enumerate(field):
                around = roll(u, 1, 1) * after_first + roll(u, -1, 1) * before_last
                if x > 0:
                    around += field[x - 1]
                if x < par - 1:
                    linked = jnp.zeros(shape, jnp.float32)
                    for mask, shift in zip(links[x], range(-REACH, REACH + 1)):
                        linked += mask * roll(field[x + 1], -shift, 1)
                    around += linked
                after.append(u + coefs[x] * (around - 4.0 * u))
            field = after
        prior = [u.astype(jnp.bfloat16) for u in field]
        out = jnp.zeros((held, lanes), jnp.float32)
        for f in range(each):
            part = jnp.zeros((held, lanes), jnp.float32)
            for p in range(par):
                part += lax.dot_general(
                    prior[p], block(f, p), (((1,), (1,)), ((), ())), preferred_element_type=jnp.float32
                )
            out = jnp.where(freq == f, part, out)
        crossed = swapped(roll(out, -sensors, 1))
        return out + jnp.where(real_row, -crossed, crossed)

    residual = roll(spectra, -sensors, 1) - hessian(spectra)
    applied = hessian(residual)
    both = jnp.where(real_lane, residual, roll(applied, sensors, 1))

    to, group = iota((lines, wide), 0), iota((lines, wide), 1) // pair
    for r in range(rows):
        for h in range(lanes // wide):
            tile = both[r * lines : (r + 1) * lines, h * wide : (h + 1) * wide]
            moved = tile
            for turn in range(1, lines):
                turned = roll(roll(tile, -turn, 0), turn * pair, 1)
                moved = jnp.where((group - to + lines) % lines == turn, turned, moved)
            for i in range(lines):
                for p in range(par):
                    out_ref[(h * lines + i) * par + p, r : r + 1, :] = moved[i : i + 1, :]


def home_kernel(got_ref, basis_ref, noise_ref, residual_ref, applied_ref):
    sources, rows, wide = got_ref.shape
    sensors = noise_ref.shape[0]
    pair = 2 * sensors
    lines = []
    for r in range(rows):
        turned = got_ref[:, r, :].T
        lines.append(
            jnp.concatenate([turned[i : i + pair, :] for i in range(0, wide, pair)], axis=1)
        )
    back = jnp.dot(
        jnp.concatenate(lines, axis=0),
        basis_ref[...],
        precision=lax.Precision.HIGHEST,
        preferred_element_type=jnp.float32,
    )
    for r in range(rows):
        residual = back[r * pair : r * pair + sensors]
        residual_ref[r] = residual
        applied_ref[r] = back[r * pair + sensors : (r + 1) * pair] + noise_ref[...] * residual


def body_fast(vectors, observed, operator, noise, coefficient, offsets):
    sen, par = lax.axis_size("sen"), lax.axis_size("par")
    rows, sensors, length = vectors.shape
    width = coefficient.shape[1]
    shares = sen * par
    each = length // 2 // shares
    pair = 2 * sensors
    wide = 2 * each * pair
    axes = ("sen", "par")
    basis = make_basis(length).reshape(length, 2, shares, each)
    noise = noise[:, None]
    whole = lambda shape: pl.BlockSpec(shape, lambda i: (0,) * len(shape))

    steps = 4 if shares % 4 == 0 else 1
    some = shares // steps
    tall = each * width // wide * pair + 2 * each
    message = pl.pallas_call(
        outbound_kernel,
        grid=(steps,),
        in_specs=[
            pl.BlockSpec((2, some, each, sensors, width), lambda i: (0, i, 0, 0, 0)),
            whole(vectors.shape),
            whole(observed.shape),
            whole(noise.shape),
            whole((length, length)),
        ],
        out_specs=pl.BlockSpec((some, tall, wide), lambda i: (i, 0, 0)),
        out_shape=jax.ShapeDtypeStruct((shares, tall, wide), jnp.bfloat16),
        scratch_shapes=[pltpu.VMEM((shares, 2 * each, wide), jnp.float32)],
        compiler_params=pltpu.CompilerParams(vmem_limit_bytes=32 * 2**20),
        name="outbound",
    )(
        operator.reshape(2, shares, each, sensors, width),
        vectors,
        observed,
        noise,
        jnp.asarray(basis.transpose(2, 3, 1, 0).reshape(length, length)),
    )
    got = lax.all_to_all(message, axes, 0, 0, tiled=True).reshape(sen, par, tall, wide)

    grid = jnp.concatenate([coefficient, offsets.astype(jnp.float32)])
    grid = lax.all_gather(grid, "par").transpose(1, 0, 2)
    message = pl.pallas_call(
        functools.partial(local_kernel, each),
        out_shape=jax.ShapeDtypeStruct((shares, rows, wide), jnp.float32),
        compiler_params=pltpu.CompilerParams(vmem_limit_bytes=32 * 2**20),
        name="local_hessians",
    )(got, grid[0], grid[1].astype(jnp.int32))
    got = lax.all_to_all(message, axes, 0, 0, tiled=True)
    return pl.pallas_call(
        home_kernel,
        out_shape=[jax.ShapeDtypeStruct((rows, sensors, length), jnp.float32)] * 2,
        compiler_params=pltpu.CompilerParams(vmem_limit_bytes=16 * 2**20),
        name="to_time",
    )(got, jnp.asarray(basis.transpose(3, 1, 2, 0).reshape(length, length)), noise)


def fits(mesh, args):
    vectors, _, _, _, coefficient, _ = args
    sen, par = mesh.shape["sen"], mesh.shape["par"]
    rows, sensors, length = vectors.shape
    half = length // 2
    if half % (sen * par) or sensors % sen or coefficient.shape[0] != par:
        return False
    each, pair = half // (sen * par), 2 * (sensors // sen)
    return 2 * each * pair == 128 and 2 * each == 8 and 3 * rows * pair <= 128 and sen * pair % 128 == 0 and coefficient.shape[1] % 128 == 0


def solution(mesh):
    placed = (
        P(None, "sen", None),
        P(None, "sen", None),
        P(None, None, "sen", "par"),
        P("sen"),
        P("par", None),
        P("par", None),
    )

    def whole(*args):
        return jax.shard_map(
            body_fast if fits(mesh, args) else body_plain,
            mesh=mesh,
            in_specs=placed,
            out_specs=(P(None, "sen", None), P(None, "sen", None)),
            check_vma=False,
        )(*args)

    return whole
```

```python
import functools
import math

import jax
import jax.numpy as jnp
import numpy as np
from jax import lax
from jax.experimental import pallas as pl
from jax.experimental.pallas import tpu as pltpu
from jax.sharding import PartitionSpec as P

SWEEPS = 4
REACH = 3


def make_basis(length):
    half = length // 2
    times = np.arange(length)[:, None]
    freqs = np.arange(half)[None, :]
    phase = (2 * freqs + 1) * times % (2 * length)
    angle = phase.astype(np.float64) * (math.pi / length)
    scale = math.sqrt(2.0 / length)
    return (np.concatenate([np.cos(angle), np.sin(angle)], axis=1) * scale).astype(np.float32)


def halo(field, axis, dim):
    count = lax.axis_size(axis)
    if count == 1:
        edge = jnp.zeros_like(lax.slice_in_dim(field, 0, 1, axis=dim))
        return jnp.concatenate([edge, field, edge], axis=dim)
    ends = count - 1
    head = lax.slice_in_dim(field, 0, 1, axis=dim)
    tail = lax.slice_in_dim(field, field.shape[dim] - 1, field.shape[dim], axis=dim)
    return jnp.concatenate(
        [
            lax.ppermute(tail, axis, [(i, i + 1) for i in range(ends)]),
            field,
            lax.ppermute(head, axis, [(i + 1, i) for i in range(ends)]),
        ],
        axis=dim,
    )


def zero_halo(field):
    return jnp.pad(field, [(0, 0)] * (field.ndim - 2) + [(1, 1), (0, 0)])


def smooth(field, coefficient, offsets, extend):
    width = field.shape[-1]
    lead = [(0, 0)] * (field.ndim - 1)
    for _ in range(SWEEPS):
        padded = extend(field)
        upper = padded[..., :-2, :]
        lower = jnp.pad(padded[..., 2:, :], lead + [(REACH, REACH)])
        linked = jnp.zeros_like(field)
        for shift in range(-REACH, REACH + 1):
            start = REACH + shift
            linked = linked + jnp.where(offsets == shift, lower[..., start : start + width], 0.0)
        sides = jnp.pad(field, lead + [(1, 1)])
        field = field + coefficient * (
            sides[..., :-2] + sides[..., 2:] + upper + linked - 4.0 * field
        )
    return field


def apply_part(spectrum, operator, coefficient, offsets, extend):
    low = spectrum.astype(jnp.bfloat16)

    def adjoint_of(spec, resp):
        return jnp.einsum("frs,fsp->frp", spec, resp, preferred_element_type=jnp.float32)

    def forward_of(par, resp):
        return jnp.einsum("frp,fsp->frs", par, resp, preferred_element_type=jnp.float32)

    real = adjoint_of(low[0], operator[0]) + adjoint_of(low[1], operator[1])
    imag = adjoint_of(low[1], operator[0]) - adjoint_of(low[0], operator[1])
    adjoint = jnp.stack([real, imag])
    grid = adjoint.reshape(adjoint.shape[:3] + coefficient.shape)
    prior = smooth(grid, coefficient, offsets, extend).astype(jnp.bfloat16)
    prior = prior.reshape(adjoint.shape)
    real = forward_of(prior[0], operator[0]) - forward_of(prior[1], operator[1])
    imag = forward_of(prior[1], operator[0]) + forward_of(prior[0], operator[1])
    return jnp.stack([real, imag])


def body_plain(vectors, observed, operator, noise, coefficient, offsets):
    sen, par = lax.axis_size("sen"), lax.axis_size("par")
    rows, sensors, length = vectors.shape
    half = length // 2
    grid_rows, width = coefficient.shape
    basis = jnp.asarray(make_basis(length))
    both = jnp.stack([vectors, observed])
    spectra = jnp.dot(
        both.reshape(2 * rows * sensors, length), basis, precision=lax.Precision.HIGHEST
    )
    spectra = spectra.reshape(2, rows, sensors, 2, half)
    whole_cells = half % (sen * par) == 0
    axes = ("sen", "par") if whole_cells else "sen"
    shares = sen * par if whole_cells else sen
    each = half // shares

    cut = operator.reshape(2, shares, each, sensors, grid_rows, width)
    cut = lax.all_to_all(cut, axes, 1, 1, tiled=True)
    if whole_cells:
        resp = cut.reshape(2, sen, par, each, sensors, grid_rows, width)
        resp = resp.transpose(0, 3, 1, 4, 2, 5, 6)
        resp = resp.reshape(2, each, sen * sensors, par * grid_rows * width)
        coefficient = lax.all_gather(coefficient, "par", tiled=True)
        offsets = lax.all_gather(offsets, "par", tiled=True)
        extend = zero_halo
    else:
        resp = cut.transpose(0, 2, 1, 3, 4, 5)
        resp = resp.reshape(2, each, sen * sensors, grid_rows * width)
        extend = lambda field: halo(field, "par", field.ndim - 2)

    def to_frequencies(spec):
        parts = spec.shape[0]
        cut = spec.reshape(parts, rows, sensors, 2, shares, each)
        cut = lax.all_to_all(cut.transpose(4, 0, 3, 5, 1, 2), axes, 0, 0, tiled=True)
        if whole_cells:
            cut = cut.reshape((sen, par) + cut.shape[1:])[:, 0]
        return cut.transpose(1, 2, 3, 4, 0, 5).reshape(parts, 2, each, rows, sen * sensors)

    def to_sensors(spec):
        parts = spec.shape[0]
        cut = spec.reshape(parts, 2, each, rows, sen, sensors).transpose(4, 0, 3, 5, 1, 2)
        if whole_cells:
            cut = jnp.repeat(cut, par, axis=0)
        cut = lax.all_to_all(cut, axes, 0, 0, tiled=True)
        return cut.transpose(1, 2, 3, 4, 0, 5).reshape(parts, rows, sensors, 2 * half)

    def hessian(spectrum):
        forward = apply_part(spectrum, resp, coefficient, offsets, extend)
        return forward if whole_cells else lax.psum(forward, "par")

    rest = spectra[1] - noise[None, :, None, None] * spectra[0]
    own, rest = to_frequencies(jnp.stack([spectra[0], rest]))
    left = rest - hessian(own)
    again = hessian(left)
    home = to_sensors(jnp.stack([left, again]))
    back = jnp.dot(
        home.reshape(2 * rows * sensors, length), basis.T, precision=lax.Precision.HIGHEST
    ).reshape(2, rows, sensors, length)
    residual = back[0]
    applied = back[1] + noise[None, :, None] * residual
    return (residual, applied)


def roll(x, shift, axis):
    size = x.shape[axis]
    return x if shift % size == 0 else pltpu.roll(x, shift % size, axis)


def iota(shape, axis):
    return lax.broadcasted_iota(jnp.int32, shape, axis)


def upright(line):
    count = line.shape[1]
    square = jnp.broadcast_to(line, (count, count))
    square = jnp.where(iota((count, count), 0) == iota((count, count), 1), square, 0.0)
    return jnp.sum(square, axis=1, keepdims=True)


def outbound_kernel(resp_ref, vectors_ref, observed_ref, noise_ref, basis_ref, out_ref, spectra_ref):
    _, devices, each, sensors, width = resp_ref.shape
    pair, lines = 2 * sensors, 2 * each
    wide = out_ref.shape[2]
    tiles = width // wide

    @pl.when(pl.program_id(0) == 0)
    def _():
        rows = vectors_ref.shape[0]
        noise = upright(noise_ref[...])
        records = []
        for r in range(rows):
            record = vectors_ref[r]
            records += [record, observed_ref[r] - noise * record]
        filled = rows * pair
        records.append(jnp.zeros((wide - filled, records[0].shape[1]), jnp.float32))
        spectra = lax.dot_general(
            basis_ref[...],
            jnp.concatenate(records, axis=0),
            (((1,), (1,)), ((), ())),
            precision=lax.Precision.HIGHEST,
            preferred_element_type=jnp.float32,
        )
        exact = iota(spectra.shape, 1) // sensors % 2 == 1
        high = spectra.astype(jnp.bfloat16).astype(jnp.float32)
        rest = jnp.where(exact, spectra - high, 0.0)
        middle = rest.astype(jnp.bfloat16).astype(jnp.float32)
        low = (rest - middle).astype(jnp.bfloat16).astype(jnp.float32)
        packed = high + roll(middle, filled, 1) + roll(low, 2 * filled, 1)
        spectra_ref[...] = packed.reshape(spectra_ref.shape)

    for f in range(each):
        for j in range(tiles):
            lanes = pl.ds(j * wide, wide)
            part = jnp.concatenate([resp_ref[0, :, f, :, lanes], resp_ref[1, :, f, :, lanes]], axis=1)
            out_ref[:, pl.ds((f * tiles + j) * pair, pair), :] = part
    first = pl.multiple_of(pl.program_id(0) * devices, devices)
    out_ref[:, pl.ds(each * tiles * pair, lines), :] = spectra_ref[pl.ds(first, devices)].astype(
        jnp.bfloat16
    )


def local_kernel(each, got_ref, coef_ref, link_ref, out_ref):
    sen, par, _, wide = got_ref.shape
    width = coef_ref.shape[1]
    tiles = width // wide
    rows = out_ref.shape[1]
    lines = 2 * each
    pair = wide // lines
    sensors = pair // 2
    held, lanes = rows * lines, sen * pair
    per = wide // pair
    body_rows = each * tiles * pair

    tail = got_ref[:, 0, pl.ds(body_rows, lines), :].astype(jnp.float32)
    parts = rows * pair
    at = iota((lines, wide), 1) // pair
    spectra = [[jnp.zeros((lines, wide), jnp.float32) for _ in range(lanes // wide)] for _ in range(rows)]
    for i in range(sen):
        packed = tail[i]
        packed = packed + roll(packed, -parts, 1) + roll(packed, -2 * parts, 1)
        h, place = divmod(i, per)
        for r in range(rows):
            moved = roll(packed, (place - r) * pair, 1)
            spectra[r][h] = jnp.where(at == place, moved, spectra[r][h])
    spectra = jnp.concatenate([jnp.concatenate(line, axis=1) for line in spectra], axis=0)

    row, lane = iota((held, lanes), 0), iota((held, lanes), 1)
    real_row = row % 2 == 0
    real_lane = lane // sensors % 2 == 0
    freq = row // 2 % each

    def swapped(x):
        return jnp.where(real_row, roll(x, -1, 0), roll(x, 1, 0))

    shape = (held, width)
    column = iota(shape, 1)
    coefs, links = [], []
    for x in range(par):
        coefs.append(jnp.broadcast_to(coef_ref[x : x + 1, :], shape))
        offset = jnp.broadcast_to(link_ref[x : x + 1, :], shape)
        masks = []
        for shift in range(-REACH, REACH + 1):
            inside = (column + shift >= 0) & (column + shift < width)
            masks.append(jnp.where((offset == shift) & inside, 1.0, 0.0))
        links.append(masks)
    after_first = jnp.where(column > 0, 1.0, 0.0)
    before_last = jnp.where(column < width - 1, 1.0, 0.0)

    def block(f, p):
        return jnp.concatenate(
            [
                got_ref[:, p, pl.ds((f * tiles + j) * pair, pair), :].reshape(lanes, wide)
                for j in range(tiles)
            ],
            axis=1,
        )

    def hessian(record):
        crossed = swapped(record)
        crossed = roll(jnp.where(real_row, crossed, -crossed), sensors, 1)
        left = jnp.where(real_lane, record, crossed)
        field = []
        for p in range(par):
            total = jnp.zeros(shape, jnp.float32)
            for f in range(each):
                part = jnp.where(freq == f, left, 0.0).astype(jnp.bfloat16)
                total += jnp.dot(part, block(f, p), preferred_element_type=jnp.float32)
            field.append(total)
        for _ in range(SWEEPS):
            after = []
            for x, u in enumerate(field):
                around = roll(u, 1, 1) * after_first + roll(u, -1, 1) * before_last
                if x > 0:
                    around += field[x - 1]
                if x < par - 1:
                    linked = jnp.zeros(shape, jnp.float32)
                    for mask, shift in zip(links[x], range(-REACH, REACH + 1)):
                        linked += mask * roll(field[x + 1], -shift, 1)
                    around += linked
                after.append(u + coefs[x] * (around - 4.0 * u))
            field = after
        prior = [u.astype(jnp.bfloat16) for u in field]
        out = jnp.zeros((held, lanes), jnp.float32)
        for f in range(each):
            part = jnp.zeros((held, lanes), jnp.float32)
            for p in range(par):
                part += lax.dot_general(
                    prior[p], block(f, p), (((1,), (1,)), ((), ())), preferred_element_type=jnp.float32
                )
            out = jnp.where(freq == f, part, out)
        crossed = swapped(roll(out, -sensors, 1))
        return out + jnp.where(real_row, -crossed, crossed)

    residual = roll(spectra, -sensors, 1) - hessian(spectra)
    applied = hessian(residual)
    both = jnp.where(real_lane, residual, roll(applied, sensors, 1))

    to, group = iota((lines, wide), 0), iota((lines, wide), 1) // pair
    for r in range(rows):
        for h in range(lanes // wide):
            tile = both[r * lines : (r + 1) * lines, h * wide : (h + 1) * wide]
            moved = tile
            for turn in range(1, lines):
                turned = roll(roll(tile, -turn, 0), turn * pair, 1)
                moved = jnp.where((group - to + lines) % lines == turn, turned, moved)
            for i in range(lines):
                for p in range(par):
                    out_ref[(h * lines + i) * par + p, r : r + 1, :] = moved[i : i + 1, :]


def home_kernel(got_ref, basis_ref, noise_ref, residual_ref, applied_ref):
    sources, rows, wide = got_ref.shape
    sensors = noise_ref.shape[1]
    pair = 2 * sensors
    noise = upright(noise_ref[...])
    lines = []
    for r in range(rows):
        turned = got_ref[:, r, :].T
        lines.append(
            jnp.concatenate([turned[i : i + pair, :] for i in range(0, wide, pair)], axis=1)
        )
    back = jnp.dot(
        jnp.concatenate(lines, axis=0),
        basis_ref[...],
        precision=lax.Precision.HIGHEST,
        preferred_element_type=jnp.float32,
    )
    for r in range(rows):
        residual = back[r * pair : r * pair + sensors]
        residual_ref[r] = residual
        applied_ref[r] = back[r * pair + sensors : (r + 1) * pair] + noise * residual


def body_fast(vectors, observed, operator, noise, coefficient, offsets):
    sen, par = lax.axis_size("sen"), lax.axis_size("par")
    rows, sensors, length = vectors.shape
    width = coefficient.shape[1]
    shares = sen * par
    each = length // 2 // shares
    pair = 2 * sensors
    wide = 2 * each * pair
    axes = ("sen", "par")
    basis = make_basis(length).reshape(length, 2, shares, each)
    noise = noise[None, :]
    whole = lambda shape: pl.BlockSpec(shape, lambda i: (0,) * len(shape))

    steps = 4 if shares % 4 == 0 else 1
    some = shares // steps
    tall = each * width // wide * pair + 2 * each
    message = pl.pallas_call(
        outbound_kernel,
        grid=(steps,),
        in_specs=[
            pl.BlockSpec((2, some, each, sensors, width), lambda i: (0, i, 0, 0, 0)),
            whole(vectors.shape),
            whole(observed.shape),
            whole(noise.shape),
            whole((length, length)),
        ],
        out_specs=pl.BlockSpec((some, tall, wide), lambda i: (i, 0, 0)),
        out_shape=jax.ShapeDtypeStruct((shares, tall, wide), jnp.bfloat16),
        scratch_shapes=[pltpu.VMEM((shares, 2 * each, wide), jnp.float32)],
        compiler_params=pltpu.CompilerParams(vmem_limit_bytes=60 * 2**20),
        name="outbound",
    )(
        operator.reshape(2, shares, each, sensors, width),
        vectors,
        observed,
        noise,
        jnp.asarray(basis.transpose(2, 3, 1, 0).reshape(length, length)),
    )
    got = lax.all_to_all(message, axes, 0, 0, tiled=True).reshape(sen, par, tall, wide)

    grid = jnp.concatenate([coefficient, offsets.astype(jnp.float32)])
    grid = lax.all_gather(grid, "par").transpose(1, 0, 2)
    message = pl.pallas_call(
        functools.partial(local_kernel, each),
        out_shape=jax.ShapeDtypeStruct((shares, rows, wide), jnp.float32),
        compiler_params=pltpu.CompilerParams(vmem_limit_bytes=32 * 2**20),
        name="local_hessians",
    )(got, grid[0], grid[1].astype(jnp.int32))
    got = lax.all_to_all(message, axes, 0, 0, tiled=True)
    return pl.pallas_call(
        home_kernel,
        out_shape=[jax.ShapeDtypeStruct((rows, sensors, length), jnp.float32)] * 2,
        compiler_params=pltpu.CompilerParams(vmem_limit_bytes=16 * 2**20),
        name="to_time",
    )(got, jnp.asarray(basis.transpose(3, 1, 2, 0).reshape(length, length)), noise)


def fits(mesh, args):
    vectors, _, _, _, coefficient, _ = args
    sen, par = mesh.shape["sen"], mesh.shape["par"]
    rows, sensors, length = vectors.shape
    half = length // 2
    if half % (sen * par) or sensors % sen or coefficient.shape[0] != par:
        return False
    each, pair = half // (sen * par), 2 * (sensors // sen)
    return 2 * each * pair == 128 and 2 * each == 8 and 3 * rows * pair <= 128 and sen * pair % 128 == 0 and coefficient.shape[1] % 128 == 0


def solution(mesh):
    placed = (
        P(None, "sen", None),
        P(None, "sen", None),
        P(None, None, "sen", "par"),
        P("sen"),
        P("par", None),
        P("par", None),
    )

    def whole(*args):
        return jax.shard_map(
            body_fast if fits(mesh, args) else body_plain,
            mesh=mesh,
            in_specs=placed,
            out_specs=(P(None, "sen", None), P(None, "sen", None)),
            check_vma=False,
        )(*args)

    return whole
```

```python
import functools
import math

import jax
import jax.numpy as jnp
import numpy as np
from jax import lax
from jax.experimental import pallas as pl
from jax.experimental.pallas import tpu as pltpu
from jax.sharding import Mesh
from jax.sharding import PartitionSpec as P

SWEEPS = 4
REACH = 3
LANES = 128
DEPTH = 256


def make_basis(length):
    half = length // 2
    times = np.arange(length)[:, None]
    freqs = np.arange(half)[None, :]
    phase = (2 * freqs + 1) * times % (2 * length)
    angle = phase.astype(np.float64) * (math.pi / length)
    scale = math.sqrt(2.0 / length)
    return (np.concatenate([np.cos(angle), np.sin(angle)], axis=1) * scale).astype(np.float32)


def halo(field, axis, dim):
    count = lax.axis_size(axis)
    if count == 1:
        edge = jnp.zeros_like(lax.slice_in_dim(field, 0, 1, axis=dim))
        return jnp.concatenate([edge, field, edge], axis=dim)
    ends = count - 1
    head = lax.slice_in_dim(field, 0, 1, axis=dim)
    tail = lax.slice_in_dim(field, field.shape[dim] - 1, field.shape[dim], axis=dim)
    return jnp.concatenate(
        [
            lax.ppermute(tail, axis, [(i, i + 1) for i in range(ends)]),
            field,
            lax.ppermute(head, axis, [(i + 1, i) for i in range(ends)]),
        ],
        axis=dim,
    )


def zero_halo(field):
    return jnp.pad(field, [(0, 0)] * (field.ndim - 2) + [(1, 1), (0, 0)])


def smooth(field, coefficient, offsets, extend):
    width = field.shape[-1]
    lead = [(0, 0)] * (field.ndim - 1)
    for _ in range(SWEEPS):
        padded = extend(field)
        upper = padded[..., :-2, :]
        lower = jnp.pad(padded[..., 2:, :], lead + [(REACH, REACH)])
        linked = jnp.zeros_like(field)
        for shift in range(-REACH, REACH + 1):
            start = REACH + shift
            linked = linked + jnp.where(offsets == shift, lower[..., start : start + width], 0.0)
        sides = jnp.pad(field, lead + [(1, 1)])
        field = field + coefficient * (
            sides[..., :-2] + sides[..., 2:] + upper + linked - 4.0 * field
        )
    return field


def apply_part(spectrum, operator, coefficient, offsets, extend):
    low = spectrum.astype(jnp.bfloat16)

    def adjoint_of(spec, resp):
        return jnp.einsum("frs,fsp->frp", spec, resp, preferred_element_type=jnp.float32)

    def forward_of(par, resp):
        return jnp.einsum("frp,fsp->frs", par, resp, preferred_element_type=jnp.float32)

    real = adjoint_of(low[0], operator[0]) + adjoint_of(low[1], operator[1])
    imag = adjoint_of(low[1], operator[0]) - adjoint_of(low[0], operator[1])
    adjoint = jnp.stack([real, imag])
    grid = adjoint.reshape(adjoint.shape[:3] + coefficient.shape)
    prior = smooth(grid, coefficient, offsets, extend).astype(jnp.bfloat16)
    prior = prior.reshape(adjoint.shape)
    real = forward_of(prior[0], operator[0]) - forward_of(prior[1], operator[1])
    imag = forward_of(prior[1], operator[0]) + forward_of(prior[0], operator[1])
    return jnp.stack([real, imag])


def body_plain(vectors, observed, operator, noise, coefficient, offsets):
    sen, par = lax.axis_size("sen"), lax.axis_size("par")
    rows, sensors, length = vectors.shape
    half = length // 2
    grid_rows, width = coefficient.shape
    basis = jnp.asarray(make_basis(length))
    both = jnp.stack([vectors, observed])
    spectra = jnp.dot(
        both.reshape(2 * rows * sensors, length), basis, precision=lax.Precision.HIGHEST
    )
    spectra = spectra.reshape(2, rows, sensors, 2, half)
    whole_cells = half % (sen * par) == 0
    axes = ("sen", "par") if whole_cells else "sen"
    shares = sen * par if whole_cells else sen
    each = half // shares

    cut = operator.reshape(2, shares, each, sensors, grid_rows, width)
    cut = lax.all_to_all(cut, axes, 1, 1, tiled=True)
    if whole_cells:
        resp = cut.reshape(2, sen, par, each, sensors, grid_rows, width)
        resp = resp.transpose(0, 3, 1, 4, 2, 5, 6)
        resp = resp.reshape(2, each, sen * sensors, par * grid_rows * width)
        coefficient = lax.all_gather(coefficient, "par", tiled=True)
        offsets = lax.all_gather(offsets, "par", tiled=True)
        extend = zero_halo
    else:
        resp = cut.transpose(0, 2, 1, 3, 4, 5)
        resp = resp.reshape(2, each, sen * sensors, grid_rows * width)
        extend = lambda field: halo(field, "par", field.ndim - 2)

    def to_frequencies(spec):
        parts = spec.shape[0]
        cut = spec.reshape(parts, rows, sensors, 2, shares, each)
        cut = lax.all_to_all(cut.transpose(4, 0, 3, 5, 1, 2), axes, 0, 0, tiled=True)
        if whole_cells:
            cut = cut.reshape((sen, par) + cut.shape[1:])[:, 0]
        return cut.transpose(1, 2, 3, 4, 0, 5).reshape(parts, 2, each, rows, sen * sensors)

    def to_sensors(spec):
        parts = spec.shape[0]
        cut = spec.reshape(parts, 2, each, rows, sen, sensors).transpose(4, 0, 3, 5, 1, 2)
        if whole_cells:
            cut = jnp.repeat(cut, par, axis=0)
        cut = lax.all_to_all(cut, axes, 0, 0, tiled=True)
        return cut.transpose(1, 2, 3, 4, 0, 5).reshape(parts, rows, sensors, 2 * half)

    def hessian(spectrum):
        forward = apply_part(spectrum, resp, coefficient, offsets, extend)
        return forward if whole_cells else lax.psum(forward, "par")

    rest = spectra[1] - noise[None, :, None, None] * spectra[0]
    own, rest = to_frequencies(jnp.stack([spectra[0], rest]))
    left = rest - hessian(own)
    again = hessian(left)
    home = to_sensors(jnp.stack([left, again]))
    back = jnp.dot(
        home.reshape(2 * rows * sensors, length), basis.T, precision=lax.Precision.HIGHEST
    ).reshape(2, rows, sensors, length)
    residual = back[0]
    applied = back[1] + noise[None, :, None] * residual
    return (residual, applied)


def roll(x, shift, axis):
    size = x.shape[axis]
    return x if shift % size == 0 else pltpu.roll(x, shift % size, axis)


def iota(shape, axis):
    return lax.broadcasted_iota(jnp.int32, shape, axis)


def upright(line):
    count = line.shape[1]
    square = jnp.broadcast_to(line, (count, count))
    square = jnp.where(iota((count, count), 0) == iota((count, count), 1), square, 0.0)
    return jnp.sum(square, axis=1, keepdims=True)


def outbound_kernel(resp_ref, vectors_ref, observed_ref, noise_ref, basis_ref, out_ref, spectra_ref):
    _, devices, each, sensors, width = resp_ref.shape
    pair, lines = 2 * sensors, 2 * each
    wide = out_ref.shape[2]
    tiles = width // wide

    @pl.when(pl.program_id(0) == 0)
    def _():
        rows = vectors_ref.shape[0]
        noise = upright(noise_ref[...])
        records = []
        for r in range(rows):
            record = vectors_ref[r]
            records += [record, observed_ref[r] - noise * record]
        filled = rows * pair
        records.append(jnp.zeros((wide - filled, records[0].shape[1]), jnp.float32))
        spectra = lax.dot_general(
            basis_ref[...],
            jnp.concatenate(records, axis=0),
            (((1,), (1,)), ((), ())),
            precision=lax.Precision.HIGHEST,
            preferred_element_type=jnp.float32,
        )
        exact = iota(spectra.shape, 1) // sensors % 2 == 1
        high = spectra.astype(jnp.bfloat16).astype(jnp.float32)
        rest = jnp.where(exact, spectra - high, 0.0)
        middle = rest.astype(jnp.bfloat16).astype(jnp.float32)
        low = (rest - middle).astype(jnp.bfloat16).astype(jnp.float32)
        packed = high + roll(middle, filled, 1) + roll(low, 2 * filled, 1)
        spectra_ref[...] = packed.reshape(spectra_ref.shape)

    for f in range(each):
        for j in range(tiles):
            lanes = pl.ds(j * wide, wide)
            part = jnp.concatenate([resp_ref[0, :, f, :, lanes], resp_ref[1, :, f, :, lanes]], axis=1)
            out_ref[:, pl.ds((f * tiles + j) * pair, pair), :] = part
    first = pl.multiple_of(pl.program_id(0) * devices, devices)
    out_ref[:, pl.ds(each * tiles * pair, lines), :] = spectra_ref[pl.ds(first, devices)].astype(
        jnp.bfloat16
    )


class Share:
    def __init__(self, got_ref, rows, each, width):
        self.got = got_ref
        self.low, self.par = got_ref.shape[:2]
        self.rows, self.each, self.width = rows, each, width
        self.lines = 2 * each
        self.tiles = width // LANES
        self.pair = (got_ref.shape[2] - self.lines) // (each * self.tiles)
        self.sensors = self.pair // 2
        self.lanes = self.low * self.pair
        self.held = rows * self.lines
        shape = (self.held, self.lanes)
        row = iota(shape, 0)
        self.real_row = row % 2 == 0
        self.real_lane = iota(shape, 1) // self.sensors % 2 == 0
        self.freq = row // 2 % each
        self.joint = max(1, min(each, DEPTH // self.lanes))

    def swapped(self, x):
        return jnp.where(self.real_row, roll(x, -1, 0), roll(x, 1, 0))

    def block(self, first, p):
        return jnp.concatenate(
            [
                jnp.concatenate(
                    [
                        self.got[
                            :, p, pl.ds((f * self.tiles + j) * self.pair, self.pair), :
                        ].reshape(self.lanes, LANES)
                        for j in range(self.tiles)
                    ],
                    axis=1,
                )
                for f in range(first, first + self.joint)
            ],
            axis=0,
        )

    def spectra(self):
        tail = self.got[:, 0, pl.ds(self.got.shape[2] - self.lines, self.lines), :]
        tail = tail.astype(jnp.float32)
        filled = self.rows * self.pair
        shape = (self.lines, LANES)
        at = iota(shape, 1) // self.pair
        per = LANES // self.pair
        found = [
            [jnp.zeros(shape, jnp.float32) for _ in range(self.lanes // LANES)]
            for _ in range(self.rows)
        ]
        for i in range(self.low):
            packed = tail[i]
            packed = packed + roll(packed, -filled, 1) + roll(packed, -2 * filled, 1)
            h, place = divmod(i, per)
            for r in range(self.rows):
                moved = roll(packed, (place - r) * self.pair, 1)
                found[r][h] = jnp.where(at == place, moved, found[r][h])
        return jnp.concatenate([jnp.concatenate(line, axis=1) for line in found], axis=0)

    def adjoint(self, record):
        crossed = self.swapped(record)
        crossed = roll(jnp.where(self.real_row, crossed, -crossed), self.sensors, 1)
        left = jnp.where(self.real_lane, record, crossed)
        sums = [jnp.zeros((self.held, self.width), jnp.float32) for _ in range(self.par)]
        for first in range(0, self.each, self.joint):
            part = [
                jnp.where(self.freq == f, left, 0.0) for f in range(first, first + self.joint)
            ]
            part = jnp.concatenate(part, axis=1).astype(jnp.bfloat16)
            for p in range(self.par):
                sums[p] += jnp.dot(
                    part, self.block(first, p), preferred_element_type=jnp.float32
                )
        return sums

    def smoothed(self, field, coef_ref, link_ref):
        shape = (self.held, self.width)
        column = iota((1, self.width), 1)
        coefs, links = [], []
        for x in range(self.par):
            coefs.append(jnp.broadcast_to(coef_ref[x : x + 1, :], shape))
            offset = link_ref[x : x + 1, :]
            masks = []
            for shift in range(-REACH, REACH + 1):
                inside = (column + shift >= 0) & (column + shift < self.width)
                mask = jnp.where((offset == shift) & inside, 1.0, 0.0)
                masks.append(jnp.broadcast_to(mask, shape))
            links.append(masks)
        after_first = jnp.broadcast_to(jnp.where(column > 0, 1.0, 0.0), shape)
        before_last = jnp.broadcast_to(jnp.where(column < self.width - 1, 1.0, 0.0), shape)
        for _ in range(SWEEPS):
            after = []
            for x, u in enumerate(field):
                around = roll(u, 1, 1) * after_first + roll(u, -1, 1) * before_last
                if x > 0:
                    around += field[x - 1]
                if x < self.par - 1:
                    linked = jnp.zeros(shape, jnp.float32)
                    for mask, shift in zip(links[x], range(-REACH, REACH + 1)):
                        linked += mask * roll(field[x + 1], -shift, 1)
                    around += linked
                after.append(u + coefs[x] * (around - 4.0 * u))
            field = after
        return field

    def forward(self, field):
        prior = [u.astype(jnp.bfloat16) for u in field]
        out = jnp.zeros((self.held, self.lanes), jnp.float32)
        for first in range(0, self.each, self.joint):
            part = jnp.zeros((self.held, self.joint * self.lanes), jnp.float32)
            for p in range(self.par):
                part += lax.dot_general(
                    prior[p],
                    self.block(first, p),
                    (((1,), (1,)), ((), ())),
                    preferred_element_type=jnp.float32,
                )
            for i in range(self.joint):
                own = part[:, i * self.lanes : (i + 1) * self.lanes]
                out = jnp.where(self.freq == first + i, own, out)
        crossed = self.swapped(roll(out, -self.sensors, 1))
        return out + jnp.where(self.real_row, -crossed, crossed)

    def messages(self, residual, applied, out_ref):
        both = jnp.where(self.real_lane, residual, roll(applied, self.sensors, 1))
        per = LANES // self.pair
        to, group = iota((per, LANES), 0), iota((per, LANES), 1) // self.pair
        for g in range(self.held // per):
            for h in range(self.lanes // LANES):
                tile = both[g * per : (g + 1) * per, h * LANES : (h + 1) * LANES]
                moved = tile
                for turn in range(1, per):
                    turned = roll(roll(tile, -turn, 0), turn * self.pair, 1)
                    moved = jnp.where((group - to + per) % per == turn, turned, moved)
                for i in range(per):
                    for p in range(self.par):
                        out_ref[(h * per + i) * self.par + p, g : g + 1, :] = moved[i : i + 1, :]


def first_kernel(share, got_ref, spectra_ref, sums_ref):
    share = share(got_ref)
    spectra = share.spectra()
    spectra_ref[...] = spectra
    for p, part in enumerate(share.adjoint(spectra)):
        sums_ref[p] = part


def summed(one_ref, other_ref):
    return [one_ref[x] + other_ref[x] for x in range(one_ref.shape[0])]


def middle_kernel(
    share, got_ref, one_ref, other_ref, spectra_ref, coef_ref, link_ref, residual_ref, sums_ref
):
    share = share(got_ref)
    rest = roll(spectra_ref[...], -share.sensors, 1)
    field = share.smoothed(summed(one_ref, other_ref), coef_ref, link_ref)
    residual = rest - share.forward(field)
    residual_ref[...] = residual
    for p, part in enumerate(share.adjoint(residual)):
        sums_ref[p] = part


def last_kernel(share, got_ref, one_ref, other_ref, residual_ref, coef_ref, link_ref, out_ref):
    share = share(got_ref)
    field = share.smoothed(summed(one_ref, other_ref), coef_ref, link_ref)
    share.messages(residual_ref[...], share.forward(field), out_ref)


def home_kernel(got_ref, basis_ref, noise_ref, residual_ref, applied_ref):
    sensors = noise_ref.shape[1]
    rows = residual_ref.shape[0]
    pair = 2 * sensors
    noise = upright(noise_ref[...])
    groups = got_ref.shape[1] // rows
    lines = []
    for r in range(rows):
        parts = []
        for g in range(groups):
            turned = got_ref[:, r * groups + g, :].T
            parts += [turned[i : i + pair, :] for i in range(0, LANES, pair)]
        lines.append(jnp.concatenate(parts, axis=1))
    back = jnp.dot(
        jnp.concatenate(lines, axis=0),
        basis_ref[...],
        precision=lax.Precision.HIGHEST,
        preferred_element_type=jnp.float32,
    )
    for r in range(rows):
        residual = back[r * pair : r * pair + sensors]
        residual_ref[r] = residual
        applied_ref[r] = back[r * pair + sensors : (r + 1) * pair] + noise * residual


def body_fast(vectors, observed, operator, noise, coefficient, offsets):
    top, low, par = (lax.axis_size(axis) for axis in ("top", "low", "par"))
    rows, sensors, length = vectors.shape
    width = coefficient.shape[1]
    shares = low * par
    each = length // 2 // shares
    pair = 2 * sensors
    axes = ("low", "par")
    basis = make_basis(length).reshape(length, 2, shares, each)
    noise = noise[None, :]
    whole = lambda shape: pl.BlockSpec(shape, lambda i: (0,) * len(shape))
    f32 = lambda *shape: jax.ShapeDtypeStruct(shape, jnp.float32)
    room = lambda mib: pltpu.CompilerParams(vmem_limit_bytes=mib * 2**20)

    steps = 4 if shares % 4 == 0 else 1
    some = shares // steps
    tall = each * width // LANES * pair + 2 * each
    message = pl.pallas_call(
        outbound_kernel,
        grid=(steps,),
        in_specs=[
            pl.BlockSpec((2, some, each, sensors, width), lambda i: (0, i, 0, 0, 0)),
            whole(vectors.shape),
            whole(observed.shape),
            whole(noise.shape),
            whole((length, length)),
        ],
        out_specs=pl.BlockSpec((some, tall, LANES), lambda i: (i, 0, 0)),
        out_shape=jax.ShapeDtypeStruct((shares, tall, LANES), jnp.bfloat16),
        scratch_shapes=[pltpu.VMEM((shares, 2 * each, LANES), jnp.float32)],
        compiler_params=room(60),
        name="outbound",
    )(
        operator.reshape(2, shares, each, sensors, width),
        vectors,
        observed,
        noise,
        jnp.asarray(basis.transpose(2, 3, 1, 0).reshape(length, length)),
    )
    got = lax.all_to_all(message, axes, 0, 0, tiled=True).reshape(low, par, tall, LANES)

    grid = jnp.concatenate([coefficient, offsets.astype(jnp.float32)])
    grid = lax.all_gather(grid, "par").transpose(1, 0, 2)
    coefs, links = grid[0], grid[1].astype(jnp.int32)

    def across(sums):
        return lax.ppermute(sums, "top", [(i, (i + 1) % top) for i in range(top)])

    share = functools.partial(Share, rows=rows, each=each, width=width)
    held, lanes = rows * 2 * each, low * pair
    sums = f32(par, held, width)
    spectra, one = pl.pallas_call(
        functools.partial(first_kernel, share),
        out_shape=[f32(held, lanes), sums],
        compiler_params=room(32),
        name="first_adjoint",
    )(got)
    residual, two = pl.pallas_call(
        functools.partial(middle_kernel, share),
        out_shape=[f32(held, lanes), sums],
        compiler_params=room(32),
        name="forward_adjoint",
    )(got, one, across(one), spectra, coefs, links)
    message = pl.pallas_call(
        functools.partial(last_kernel, share),
        out_shape=f32(shares, held * pair // LANES, LANES),
        compiler_params=room(32),
        name="last_forward",
    )(got, two, across(two), residual, coefs, links)
    got = lax.all_to_all(message, axes, 0, 0, tiled=True)
    return pl.pallas_call(
        home_kernel,
        out_shape=[f32(rows, sensors, length)] * 2,
        compiler_params=room(16),
        name="to_time",
    )(got, jnp.asarray(basis.transpose(3, 1, 2, 0).reshape(length, length)), noise)


def fits(mesh, args):
    vectors, _, _, _, coefficient, _ = args
    sen, par = mesh.shape["sen"], mesh.shape["par"]
    rows, sensors, length = vectors.shape
    half, low = length // 2, sen // 2
    if sen % 2 or half % (low * par) or sensors % sen or coefficient.shape[0] != par:
        return False
    each, pair = half // (low * par), 2 * (sensors // sen)
    return (
        pair == 16
        and each % 8 == 0
        and 3 * rows * pair <= LANES
        and low * pair % LANES == 0
        and coefficient.shape[1] % LANES == 0
    )


def solution(mesh):
    def whole(*args):
        if fits(mesh, args):
            body, sen = body_fast, ("top", "low")
            shape = (2, mesh.shape["sen"] // 2, mesh.shape["par"])
            within = Mesh(mesh.devices.reshape(shape), sen + ("par",))
        else:
            body, sen, within = body_plain, "sen", mesh
        record = P(None, sen, None)
        return jax.shard_map(
            body,
            mesh=within,
            in_specs=(
                record,
                record,
                P(None, None, sen, "par"),
                P(sen),
                P("par", None),
                P("par", None),
            ),
            out_specs=(record, record),
            check_vma=False,
        )(*args)

    return whole
```

```python
import functools
import math

import jax
import jax.numpy as jnp
import numpy as np
from jax import lax
from jax.experimental import pallas as pl
from jax.experimental.pallas import tpu as pltpu
from jax.sharding import Mesh
from jax.sharding import PartitionSpec as P

SWEEPS = 4
REACH = 3
LANES = 128
DEPTH = 256


def make_basis(length):
    half = length // 2
    times = np.arange(length)[:, None]
    freqs = np.arange(half)[None, :]
    phase = (2 * freqs + 1) * times % (2 * length)
    angle = phase.astype(np.float64) * (math.pi / length)
    scale = math.sqrt(2.0 / length)
    return (np.concatenate([np.cos(angle), np.sin(angle)], axis=1) * scale).astype(np.float32)


def halo(field, axis, dim):
    count = lax.axis_size(axis)
    if count == 1:
        edge = jnp.zeros_like(lax.slice_in_dim(field, 0, 1, axis=dim))
        return jnp.concatenate([edge, field, edge], axis=dim)
    ends = count - 1
    head = lax.slice_in_dim(field, 0, 1, axis=dim)
    tail = lax.slice_in_dim(field, field.shape[dim] - 1, field.shape[dim], axis=dim)
    return jnp.concatenate(
        [
            lax.ppermute(tail, axis, [(i, i + 1) for i in range(ends)]),
            field,
            lax.ppermute(head, axis, [(i + 1, i) for i in range(ends)]),
        ],
        axis=dim,
    )


def zero_halo(field):
    return jnp.pad(field, [(0, 0)] * (field.ndim - 2) + [(1, 1), (0, 0)])


def smooth(field, coefficient, offsets, extend):
    width = field.shape[-1]
    lead = [(0, 0)] * (field.ndim - 1)
    for _ in range(SWEEPS):
        padded = extend(field)
        upper = padded[..., :-2, :]
        lower = jnp.pad(padded[..., 2:, :], lead + [(REACH, REACH)])
        linked = jnp.zeros_like(field)
        for shift in range(-REACH, REACH + 1):
            start = REACH + shift
            linked = linked + jnp.where(offsets == shift, lower[..., start : start + width], 0.0)
        sides = jnp.pad(field, lead + [(1, 1)])
        field = field + coefficient * (
            sides[..., :-2] + sides[..., 2:] + upper + linked - 4.0 * field
        )
    return field


def apply_part(spectrum, operator, coefficient, offsets, extend):
    low = spectrum.astype(jnp.bfloat16)

    def adjoint_of(spec, resp):
        return jnp.einsum("frs,fsp->frp", spec, resp, preferred_element_type=jnp.float32)

    def forward_of(par, resp):
        return jnp.einsum("frp,fsp->frs", par, resp, preferred_element_type=jnp.float32)

    real = adjoint_of(low[0], operator[0]) + adjoint_of(low[1], operator[1])
    imag = adjoint_of(low[1], operator[0]) - adjoint_of(low[0], operator[1])
    adjoint = jnp.stack([real, imag])
    grid = adjoint.reshape(adjoint.shape[:3] + coefficient.shape)
    prior = smooth(grid, coefficient, offsets, extend).astype(jnp.bfloat16)
    prior = prior.reshape(adjoint.shape)
    real = forward_of(prior[0], operator[0]) - forward_of(prior[1], operator[1])
    imag = forward_of(prior[1], operator[0]) + forward_of(prior[0], operator[1])
    return jnp.stack([real, imag])


def body_plain(vectors, observed, operator, noise, coefficient, offsets):
    sen, par = lax.axis_size("sen"), lax.axis_size("par")
    rows, sensors, length = vectors.shape
    half = length // 2
    grid_rows, width = coefficient.shape
    basis = jnp.asarray(make_basis(length))
    both = jnp.stack([vectors, observed])
    spectra = jnp.dot(
        both.reshape(2 * rows * sensors, length), basis, precision=lax.Precision.HIGHEST
    )
    spectra = spectra.reshape(2, rows, sensors, 2, half)
    whole_cells = half % (sen * par) == 0
    axes = ("sen", "par") if whole_cells else "sen"
    shares = sen * par if whole_cells else sen
    each = half // shares

    cut = operator.reshape(2, shares, each, sensors, grid_rows, width)
    cut = lax.all_to_all(cut, axes, 1, 1, tiled=True)
    if whole_cells:
        resp = cut.reshape(2, sen, par, each, sensors, grid_rows, width)
        resp = resp.transpose(0, 3, 1, 4, 2, 5, 6)
        resp = resp.reshape(2, each, sen * sensors, par * grid_rows * width)
        coefficient = lax.all_gather(coefficient, "par", tiled=True)
        offsets = lax.all_gather(offsets, "par", tiled=True)
        extend = zero_halo
    else:
        resp = cut.transpose(0, 2, 1, 3, 4, 5)
        resp = resp.reshape(2, each, sen * sensors, grid_rows * width)
        extend = lambda field: halo(field, "par", field.ndim - 2)

    def to_frequencies(spec):
        parts = spec.shape[0]
        cut = spec.reshape(parts, rows, sensors, 2, shares, each)
        cut = lax.all_to_all(cut.transpose(4, 0, 3, 5, 1, 2), axes, 0, 0, tiled=True)
        if whole_cells:
            cut = cut.reshape((sen, par) + cut.shape[1:])[:, 0]
        return cut.transpose(1, 2, 3, 4, 0, 5).reshape(parts, 2, each, rows, sen * sensors)

    def to_sensors(spec):
        parts = spec.shape[0]
        cut = spec.reshape(parts, 2, each, rows, sen, sensors).transpose(4, 0, 3, 5, 1, 2)
        if whole_cells:
            cut = jnp.repeat(cut, par, axis=0)
        cut = lax.all_to_all(cut, axes, 0, 0, tiled=True)
        return cut.transpose(1, 2, 3, 4, 0, 5).reshape(parts, rows, sensors, 2 * half)

    def hessian(spectrum):
        forward = apply_part(spectrum, resp, coefficient, offsets, extend)
        return forward if whole_cells else lax.psum(forward, "par")

    rest = spectra[1] - noise[None, :, None, None] * spectra[0]
    own, rest = to_frequencies(jnp.stack([spectra[0], rest]))
    left = rest - hessian(own)
    again = hessian(left)
    home = to_sensors(jnp.stack([left, again]))
    back = jnp.dot(
        home.reshape(2 * rows * sensors, length), basis.T, precision=lax.Precision.HIGHEST
    ).reshape(2, rows, sensors, length)
    residual = back[0]
    applied = back[1] + noise[None, :, None] * residual
    return (residual, applied)


def roll(x, shift, axis):
    size = x.shape[axis]
    return x if shift % size == 0 else pltpu.roll(x, shift % size, axis)


def iota(shape, axis):
    return lax.broadcasted_iota(jnp.int32, shape, axis)


def upright(line):
    count = line.shape[1]
    square = jnp.broadcast_to(line, (count, count))
    square = jnp.where(iota((count, count), 0) == iota((count, count), 1), square, 0.0)
    return jnp.sum(square, axis=1, keepdims=True)


def outbound_kernel(
    resp_hbm, vectors_hbm, observed_hbm, noise_hbm, basis_hbm, out_hbm,
    resp_ref, vectors_ref, observed_ref, noise_ref, basis_ref, out_ref, small_sems, in_sems, out_sems,
):
    _, devices, each, sensors, width = resp_ref.shape
    pair, lines = 2 * sensors, 2 * each
    tiles = width // LANES
    steps = in_sems.shape[0]
    some = devices // steps
    pieces = [pl.ds(i * some, some) for i in range(steps)]
    small = [
        pltpu.make_async_copy(src, dst, small_sems.at[i])
        for i, (src, dst) in enumerate(
            [
                (basis_hbm, basis_ref),
                (vectors_hbm, vectors_ref),
                (observed_hbm, observed_ref),
                (noise_hbm, noise_ref),
            ]
        )
    ]
    loads = [
        pltpu.make_async_copy(resp_hbm.at[:, piece], resp_ref.at[:, piece], in_sems.at[i])
        for i, piece in enumerate(pieces)
    ]
    body = each * tiles * pair
    parts = [(piece, pl.ds(0, body)) for piece in pieces] + [(pl.ds(0, devices), pl.ds(body, lines))]
    stores = [
        pltpu.make_async_copy(out_ref.at[part], out_hbm.at[part], out_sems.at[i])
        for i, part in enumerate(parts)
    ]
    for copy in loads + small:
        copy.start()

    for i, piece in enumerate(pieces):
        loads[i].wait()
        for f in range(each):
            for j in range(tiles):
                lanes = pl.ds(j * LANES, LANES)
                both = [resp_ref[c, piece, f, :, lanes] for c in range(2)]
                lane_rows = pl.ds((f * tiles + j) * pair, pair)
                out_ref[piece, lane_rows, :] = jnp.concatenate(both, axis=1)
        stores[i].start()

    for copy in small:
        copy.wait()
    rows = vectors_ref.shape[0]
    noise = upright(noise_ref[...])
    records = []
    for r in range(rows):
        record = vectors_ref[r]
        records += [record, observed_ref[r] - noise * record]
    filled = rows * pair
    records.append(jnp.zeros((LANES - filled, records[0].shape[1]), jnp.float32))
    spectra = lax.dot_general(
        basis_ref[...],
        jnp.concatenate(records, axis=0),
        (((1,), (1,)), ((), ())),
        precision=lax.Precision.HIGHEST,
        preferred_element_type=jnp.float32,
    )
    exact = iota(spectra.shape, 1) // sensors % 2 == 1
    high = spectra.astype(jnp.bfloat16).astype(jnp.float32)
    rest = jnp.where(exact, spectra - high, 0.0)
    middle = rest.astype(jnp.bfloat16).astype(jnp.float32)
    low = (rest - middle).astype(jnp.bfloat16).astype(jnp.float32)
    packed = high + roll(middle, filled, 1) + roll(low, 2 * filled, 1)
    packed = packed.reshape(devices, lines, LANES).astype(jnp.bfloat16)
    out_ref[:, pl.ds(body, lines), :] = packed
    stores[-1].start()
    for copy in stores:
        copy.wait()


class Share:
    def __init__(self, got_ref, rows, each, width):
        self.got = got_ref
        self.low, self.par = got_ref.shape[:2]
        self.rows, self.each, self.width = rows, each, width
        self.lines = 2 * each
        self.tiles = width // LANES
        self.pair = (got_ref.shape[2] - self.lines) // (each * self.tiles)
        self.sensors = self.pair // 2
        self.lanes = self.low * self.pair
        self.held = rows * self.lines
        shape = (self.held, self.lanes)
        row = iota(shape, 0)
        self.real_row = row % 2 == 0
        self.real_lane = iota(shape, 1) // self.sensors % 2 == 0
        self.freq = row // 2 % each
        self.joint = max(1, min(each, DEPTH // self.lanes))

    def swapped(self, x):
        return jnp.where(self.real_row, roll(x, -1, 0), roll(x, 1, 0))

    def block(self, first, p):
        return jnp.concatenate(
            [
                jnp.concatenate(
                    [
                        self.got[
                            :, p, pl.ds((f * self.tiles + j) * self.pair, self.pair), :
                        ].reshape(self.lanes, LANES)
                        for j in range(self.tiles)
                    ],
                    axis=1,
                )
                for f in range(first, first + self.joint)
            ],
            axis=0,
        )

    def spectra(self):
        tail = self.got[:, 0, pl.ds(self.got.shape[2] - self.lines, self.lines), :]
        tail = tail.astype(jnp.float32)
        filled = self.rows * self.pair
        shape = (self.lines, LANES)
        at = iota(shape, 1) // self.pair
        per = LANES // self.pair
        found = [
            [jnp.zeros(shape, jnp.float32) for _ in range(self.lanes // LANES)]
            for _ in range(self.rows)
        ]
        for i in range(self.low):
            packed = tail[i]
            packed = packed + roll(packed, -filled, 1) + roll(packed, -2 * filled, 1)
            h, place = divmod(i, per)
            for r in range(self.rows):
                moved = roll(packed, (place - r) * self.pair, 1)
                found[r][h] = jnp.where(at == place, moved, found[r][h])
        return jnp.concatenate([jnp.concatenate(line, axis=1) for line in found], axis=0)

    def adjoint(self, record):
        crossed = self.swapped(record)
        crossed = roll(jnp.where(self.real_row, crossed, -crossed), self.sensors, 1)
        left = jnp.where(self.real_lane, record, crossed)
        sums = [jnp.zeros((self.held, self.width), jnp.float32) for _ in range(self.par)]
        for first in range(0, self.each, self.joint):
            part = [
                jnp.where(self.freq == f, left, 0.0) for f in range(first, first + self.joint)
            ]
            part = jnp.concatenate(part, axis=1).astype(jnp.bfloat16)
            for p in range(self.par):
                sums[p] += jnp.dot(
                    part, self.block(first, p), preferred_element_type=jnp.float32
                )
        return sums

    def smoothed(self, field, coef_ref, link_ref):
        shape = (self.held, self.width)
        column = iota((1, self.width), 1)
        coefs, links = [], []
        for x in range(self.par):
            coefs.append(jnp.broadcast_to(coef_ref[x : x + 1, :], shape))
            offset = link_ref[x : x + 1, :]
            masks = []
            for shift in range(-REACH, REACH + 1):
                inside = (column + shift >= 0) & (column + shift < self.width)
                mask = jnp.where((offset == shift) & inside, 1.0, 0.0)
                masks.append(jnp.broadcast_to(mask, shape))
            links.append(masks)
        after_first = jnp.broadcast_to(jnp.where(column > 0, 1.0, 0.0), shape)
        before_last = jnp.broadcast_to(jnp.where(column < self.width - 1, 1.0, 0.0), shape)
        for _ in range(SWEEPS):
            after = []
            for x, u in enumerate(field):
                around = roll(u, 1, 1) * after_first + roll(u, -1, 1) * before_last
                if x > 0:
                    around += field[x - 1]
                if x < self.par - 1:
                    linked = jnp.zeros(shape, jnp.float32)
                    for mask, shift in zip(links[x], range(-REACH, REACH + 1)):
                        linked += mask * roll(field[x + 1], -shift, 1)
                    around += linked
                after.append(u + coefs[x] * (around - 4.0 * u))
            field = after
        return field

    def forward(self, field):
        prior = [u.astype(jnp.bfloat16) for u in field]
        out = jnp.zeros((self.held, self.lanes), jnp.float32)
        for first in range(0, self.each, self.joint):
            part = jnp.zeros((self.held, self.joint * self.lanes), jnp.float32)
            for p in range(self.par):
                part += lax.dot_general(
                    prior[p],
                    self.block(first, p),
                    (((1,), (1,)), ((), ())),
                    preferred_element_type=jnp.float32,
                )
            for i in range(self.joint):
                own = part[:, i * self.lanes : (i + 1) * self.lanes]
                out = jnp.where(self.freq == first + i, own, out)
        crossed = self.swapped(roll(out, -self.sensors, 1))
        return out + jnp.where(self.real_row, -crossed, crossed)

    def messages(self, residual, applied, out_ref):
        both = jnp.where(self.real_lane, residual, roll(applied, self.sensors, 1))
        per = LANES // self.pair
        to, group = iota((per, LANES), 0), iota((per, LANES), 1) // self.pair
        for g in range(self.held // per):
            for h in range(self.lanes // LANES):
                tile = both[g * per : (g + 1) * per, h * LANES : (h + 1) * LANES]
                moved = tile
                for turn in range(1, per):
                    turned = roll(roll(tile, -turn, 0), turn * self.pair, 1)
                    moved = jnp.where((group - to + per) % per == turn, turned, moved)
                for i in range(per):
                    for p in range(self.par):
                        out_ref[(h * per + i) * self.par + p, g : g + 1, :] = moved[i : i + 1, :]


def first_kernel(share, got_ref, spectra_ref, sums_ref):
    share = share(got_ref)
    spectra = share.spectra()
    spectra_ref[...] = spectra
    for p, part in enumerate(share.adjoint(spectra)):
        sums_ref[p] = part


def summed(one_ref, other_ref):
    return [one_ref[x] + other_ref[x] for x in range(one_ref.shape[0])]


def middle_kernel(
    share, got_ref, one_ref, other_ref, spectra_ref, coef_ref, link_ref, residual_ref, sums_ref
):
    share = share(got_ref)
    rest = roll(spectra_ref[...], -share.sensors, 1)
    field = share.smoothed(summed(one_ref, other_ref), coef_ref, link_ref)
    residual = rest - share.forward(field)
    residual_ref[...] = residual
    for p, part in enumerate(share.adjoint(residual)):
        sums_ref[p] = part


def last_kernel(share, got_ref, one_ref, other_ref, residual_ref, coef_ref, link_ref, out_ref):
    share = share(got_ref)
    field = share.smoothed(summed(one_ref, other_ref), coef_ref, link_ref)
    share.messages(residual_ref[...], share.forward(field), out_ref)


def home_kernel(got_ref, basis_ref, noise_ref, residual_ref, applied_ref):
    sensors = noise_ref.shape[1]
    rows = residual_ref.shape[0]
    pair = 2 * sensors
    noise = upright(noise_ref[...])
    groups = got_ref.shape[1] // rows
    lines = []
    for r in range(rows):
        parts = []
        for g in range(groups):
            turned = got_ref[:, r * groups + g, :].T
            parts += [turned[i : i + pair, :] for i in range(0, LANES, pair)]
        lines.append(jnp.concatenate(parts, axis=1))
    back = jnp.dot(
        jnp.concatenate(lines, axis=0),
        basis_ref[...],
        precision=lax.Precision.HIGHEST,
        preferred_element_type=jnp.float32,
    )
    for r in range(rows):
        residual = back[r * pair : r * pair + sensors]
        residual_ref[r] = residual
        applied_ref[r] = back[r * pair + sensors : (r + 1) * pair] + noise * residual


def body_fast(vectors, observed, operator, noise, coefficient, offsets):
    top, low, par = (lax.axis_size(axis) for axis in ("top", "low", "par"))
    rows, sensors, length = vectors.shape
    width = coefficient.shape[1]
    shares = low * par
    each = length // 2 // shares
    pair = 2 * sensors
    axes = ("low", "par")
    basis = make_basis(length).reshape(length, 2, shares, each)
    noise = noise[None, :]
    f32 = lambda *shape: jax.ShapeDtypeStruct(shape, jnp.float32)
    room = lambda mib: pltpu.CompilerParams(vmem_limit_bytes=mib * 2**20)

    steps = 4 if shares % 4 == 0 else 1
    tall = each * width // LANES * pair + 2 * each
    operator = operator.reshape(2, shares, each, sensors, width)
    scratch = [
        pltpu.VMEM(array.shape, array.dtype) for array in (operator, vectors, observed, noise)
    ]
    message = pl.pallas_call(
        outbound_kernel,
        in_specs=[pl.BlockSpec(memory_space=pl.ANY)] * 5,
        out_specs=pl.BlockSpec(memory_space=pl.ANY),
        out_shape=jax.ShapeDtypeStruct((shares, tall, LANES), jnp.bfloat16),
        scratch_shapes=scratch
        + [
            pltpu.VMEM((length, length), jnp.float32),
            pltpu.VMEM((shares, tall, LANES), jnp.bfloat16),
            pltpu.SemaphoreType.DMA((4,)),
            pltpu.SemaphoreType.DMA((steps,)),
            pltpu.SemaphoreType.DMA((steps + 1,)),
        ],
        compiler_params=room(60),
        name="outbound",
    )(
        operator,
        vectors,
        observed,
        noise,
        jnp.asarray(basis.transpose(2, 3, 1, 0).reshape(length, length)),
    )
    got = lax.all_to_all(message, axes, 0, 0, tiled=True).reshape(low, par, tall, LANES)

    grid = jnp.concatenate([coefficient, offsets.astype(jnp.float32)])
    grid = lax.all_gather(grid, "par").transpose(1, 0, 2)
    coefs, links = grid[0], grid[1].astype(jnp.int32)

    def across(sums):
        return lax.ppermute(sums, "top", [(i, (i + 1) % top) for i in range(top)])

    share = functools.partial(Share, rows=rows, each=each, width=width)
    held, lanes = rows * 2 * each, low * pair
    sums = f32(par, held, width)
    spectra, one = pl.pallas_call(
        functools.partial(first_kernel, share),
        out_shape=[f32(held, lanes), sums],
        compiler_params=room(32),
        name="first_adjoint",
    )(got)
    residual, two = pl.pallas_call(
        functools.partial(middle_kernel, share),
        out_shape=[f32(held, lanes), sums],
        compiler_params=room(32),
        name="forward_adjoint",
    )(got, one, across(one), spectra, coefs, links)
    message = pl.pallas_call(
        functools.partial(last_kernel, share),
        out_shape=f32(shares, held * pair // LANES, LANES),
        compiler_params=room(32),
        name="last_forward",
    )(got, two, across(two), residual, coefs, links)
    got = lax.all_to_all(message, axes, 0, 0, tiled=True)
    return pl.pallas_call(
        home_kernel,
        out_shape=[f32(rows, sensors, length)] * 2,
        compiler_params=room(16),
        name="to_time",
    )(got, jnp.asarray(basis.transpose(3, 1, 2, 0).reshape(length, length)), noise)


def fits(mesh, args):
    vectors, _, _, _, coefficient, _ = args
    sen, par = mesh.shape["sen"], mesh.shape["par"]
    rows, sensors, length = vectors.shape
    half, low = length // 2, sen // 2
    if sen % 2 or half % (low * par) or sensors % sen or coefficient.shape[0] != par:
        return False
    each, pair = half // (low * par), 2 * (sensors // sen)
    return (
        pair == 16
        and each % 8 == 0
        and 3 * rows * pair <= LANES
        and low * pair % LANES == 0
        and coefficient.shape[1] % LANES == 0
    )


def solution(mesh):
    def whole(*args):
        if fits(mesh, args):
            body, sen = body_fast, ("top", "low")
            shape = (2, mesh.shape["sen"] // 2, mesh.shape["par"])
            within = Mesh(mesh.devices.reshape(shape), sen + ("par",))
        else:
            body, sen, within = body_plain, "sen", mesh
        record = P(None, sen, None)
        return jax.shard_map(
            body,
            mesh=within,
            in_specs=(
                record,
                record,
                P(None, None, sen, "par"),
                P(sen),
                P("par", None),
                P("par", None),
            ),
            out_specs=(record, record),
            check_vma=False,
        )(*args)

    return whole
```

```python
import functools
import math

import jax
import jax.numpy as jnp
import numpy as np
from jax import lax
from jax.experimental import pallas as pl
from jax.experimental.pallas import tpu as pltpu
from jax.sharding import Mesh
from jax.sharding import PartitionSpec as P

SWEEPS = 4
REACH = 3
LANES = 128
DEPTH = 256


def make_basis(length):
    half = length // 2
    times = np.arange(length)[:, None]
    freqs = np.arange(half)[None, :]
    phase = (2 * freqs + 1) * times % (2 * length)
    angle = phase.astype(np.float64) * (math.pi / length)
    scale = math.sqrt(2.0 / length)
    return (np.concatenate([np.cos(angle), np.sin(angle)], axis=1) * scale).astype(np.float32)


def halo(field, axis, dim):
    count = lax.axis_size(axis)
    if count == 1:
        edge = jnp.zeros_like(lax.slice_in_dim(field, 0, 1, axis=dim))
        return jnp.concatenate([edge, field, edge], axis=dim)
    ends = count - 1
    head = lax.slice_in_dim(field, 0, 1, axis=dim)
    tail = lax.slice_in_dim(field, field.shape[dim] - 1, field.shape[dim], axis=dim)
    return jnp.concatenate(
        [
            lax.ppermute(tail, axis, [(i, i + 1) for i in range(ends)]),
            field,
            lax.ppermute(head, axis, [(i + 1, i) for i in range(ends)]),
        ],
        axis=dim,
    )


def zero_halo(field):
    return jnp.pad(field, [(0, 0)] * (field.ndim - 2) + [(1, 1), (0, 0)])


def smooth(field, coefficient, offsets, extend):
    width = field.shape[-1]
    lead = [(0, 0)] * (field.ndim - 1)
    for _ in range(SWEEPS):
        padded = extend(field)
        upper = padded[..., :-2, :]
        lower = jnp.pad(padded[..., 2:, :], lead + [(REACH, REACH)])
        linked = jnp.zeros_like(field)
        for shift in range(-REACH, REACH + 1):
            start = REACH + shift
            linked = linked + jnp.where(offsets == shift, lower[..., start : start + width], 0.0)
        sides = jnp.pad(field, lead + [(1, 1)])
        field = field + coefficient * (
            sides[..., :-2] + sides[..., 2:] + upper + linked - 4.0 * field
        )
    return field


def apply_part(spectrum, operator, coefficient, offsets, extend):
    low = spectrum.astype(jnp.bfloat16)

    def adjoint_of(spec, resp):
        return jnp.einsum("frs,fsp->frp", spec, resp, preferred_element_type=jnp.float32)

    def forward_of(par, resp):
        return jnp.einsum("frp,fsp->frs", par, resp, preferred_element_type=jnp.float32)

    real = adjoint_of(low[0], operator[0]) + adjoint_of(low[1], operator[1])
    imag = adjoint_of(low[1], operator[0]) - adjoint_of(low[0], operator[1])
    adjoint = jnp.stack([real, imag])
    grid = adjoint.reshape(adjoint.shape[:3] + coefficient.shape)
    prior = smooth(grid, coefficient, offsets, extend).astype(jnp.bfloat16)
    prior = prior.reshape(adjoint.shape)
    real = forward_of(prior[0], operator[0]) - forward_of(prior[1], operator[1])
    imag = forward_of(prior[1], operator[0]) + forward_of(prior[0], operator[1])
    return jnp.stack([real, imag])


def body_plain(vectors, observed, operator, noise, coefficient, offsets):
    sen, par = lax.axis_size("sen"), lax.axis_size("par")
    rows, sensors, length = vectors.shape
    half = length // 2
    grid_rows, width = coefficient.shape
    basis = jnp.asarray(make_basis(length))
    both = jnp.stack([vectors, observed])
    spectra = jnp.dot(
        both.reshape(2 * rows * sensors, length), basis, precision=lax.Precision.HIGHEST
    )
    spectra = spectra.reshape(2, rows, sensors, 2, half)
    whole_cells = half % (sen * par) == 0
    axes = ("sen", "par") if whole_cells else "sen"
    shares = sen * par if whole_cells else sen
    each = half // shares

    cut = operator.reshape(2, shares, each, sensors, grid_rows, width)
    cut = lax.all_to_all(cut, axes, 1, 1, tiled=True)
    if whole_cells:
        resp = cut.reshape(2, sen, par, each, sensors, grid_rows, width)
        resp = resp.transpose(0, 3, 1, 4, 2, 5, 6)
        resp = resp.reshape(2, each, sen * sensors, par * grid_rows * width)
        coefficient = lax.all_gather(coefficient, "par", tiled=True)
        offsets = lax.all_gather(offsets, "par", tiled=True)
        extend = zero_halo
    else:
        resp = cut.transpose(0, 2, 1, 3, 4, 5)
        resp = resp.reshape(2, each, sen * sensors, grid_rows * width)
        extend = lambda field: halo(field, "par", field.ndim - 2)

    def to_frequencies(spec):
        parts = spec.shape[0]
        cut = spec.reshape(parts, rows, sensors, 2, shares, each)
        cut = lax.all_to_all(cut.transpose(4, 0, 3, 5, 1, 2), axes, 0, 0, tiled=True)
        if whole_cells:
            cut = cut.reshape((sen, par) + cut.shape[1:])[:, 0]
        return cut.transpose(1, 2, 3, 4, 0, 5).reshape(parts, 2, each, rows, sen * sensors)

    def to_sensors(spec):
        parts = spec.shape[0]
        cut = spec.reshape(parts, 2, each, rows, sen, sensors).transpose(4, 0, 3, 5, 1, 2)
        if whole_cells:
            cut = jnp.repeat(cut, par, axis=0)
        cut = lax.all_to_all(cut, axes, 0, 0, tiled=True)
        return cut.transpose(1, 2, 3, 4, 0, 5).reshape(parts, rows, sensors, 2 * half)

    def hessian(spectrum):
        forward = apply_part(spectrum, resp, coefficient, offsets, extend)
        return forward if whole_cells else lax.psum(forward, "par")

    rest = spectra[1] - noise[None, :, None, None] * spectra[0]
    own, rest = to_frequencies(jnp.stack([spectra[0], rest]))
    left = rest - hessian(own)
    again = hessian(left)
    home = to_sensors(jnp.stack([left, again]))
    back = jnp.dot(
        home.reshape(2 * rows * sensors, length), basis.T, precision=lax.Precision.HIGHEST
    ).reshape(2, rows, sensors, length)
    residual = back[0]
    applied = back[1] + noise[None, :, None] * residual
    return (residual, applied)


def roll(x, shift, axis):
    size = x.shape[axis]
    return x if shift % size == 0 else pltpu.roll(x, shift % size, axis)


def iota(shape, axis):
    return lax.broadcasted_iota(jnp.int32, shape, axis)


def upright(line):
    count = line.shape[1]
    square = jnp.broadcast_to(line, (count, count))
    square = jnp.where(iota((count, count), 0) == iota((count, count), 1), square, 0.0)
    return jnp.sum(square, axis=1, keepdims=True)


def outbound_kernel(
    resp_hbm, vectors_hbm, observed_hbm, noise_hbm, basis_hbm, out_hbm,
    resp_ref, vectors_ref, observed_ref, noise_ref, basis_ref, out_ref, small_sems, in_sems, out_sems,
):
    _, devices, each, sensors, width = resp_ref.shape
    pair, lines = 2 * sensors, 2 * each
    tiles = width // LANES
    steps = in_sems.shape[0]
    some = devices // steps
    pieces = [pl.ds(i * some, some) for i in range(steps)]
    small = [
        pltpu.make_async_copy(src, dst, small_sems.at[i])
        for i, (src, dst) in enumerate(
            [
                (basis_hbm, basis_ref),
                (vectors_hbm, vectors_ref),
                (observed_hbm, observed_ref),
                (noise_hbm, noise_ref),
            ]
        )
    ]
    loads = [
        pltpu.make_async_copy(resp_hbm.at[:, piece], resp_ref.at[:, piece], in_sems.at[i])
        for i, piece in enumerate(pieces)
    ]
    body = each * tiles * pair
    parts = [(piece, pl.ds(0, body)) for piece in pieces] + [(pl.ds(0, devices), pl.ds(body, lines))]
    stores = [
        pltpu.make_async_copy(out_ref.at[part], out_hbm.at[part], out_sems.at[i])
        for i, part in enumerate(parts)
    ]
    for copy in loads + small:
        copy.start()

    for i, piece in enumerate(pieces):
        loads[i].wait()
        for f in range(each):
            for j in range(tiles):
                lanes = pl.ds(j * LANES, LANES)
                both = [resp_ref[c, piece, f, :, lanes] for c in range(2)]
                lane_rows = pl.ds((f * tiles + j) * pair, pair)
                out_ref[piece, lane_rows, :] = jnp.concatenate(both, axis=1)
        stores[i].start()

    for copy in small:
        copy.wait()
    rows = vectors_ref.shape[0]
    noise = upright(noise_ref[...])
    records = []
    for r in range(rows):
        record = vectors_ref[r]
        records += [record, observed_ref[r] - noise * record]
    filled = rows * pair
    records.append(jnp.zeros((LANES - filled, records[0].shape[1]), jnp.float32))
    spectra = lax.dot_general(
        basis_ref[...],
        jnp.concatenate(records, axis=0),
        (((1,), (1,)), ((), ())),
        precision=lax.Precision.HIGHEST,
        preferred_element_type=jnp.float32,
    )
    exact = iota(spectra.shape, 1) // sensors % 2 == 1
    high = spectra.astype(jnp.bfloat16).astype(jnp.float32)
    rest = jnp.where(exact, spectra - high, 0.0)
    middle = rest.astype(jnp.bfloat16).astype(jnp.float32)
    low = (rest - middle).astype(jnp.bfloat16).astype(jnp.float32)
    packed = high + roll(middle, filled, 1) + roll(low, 2 * filled, 1)
    packed = packed.reshape(devices, lines, LANES).astype(jnp.bfloat16)
    out_ref[:, pl.ds(body, lines), :] = packed
    stores[-1].start()
    for copy in stores:
        copy.wait()


class Share:
    def __init__(self, got_ref, rows, each, width):
        self.got = got_ref
        self.low, self.par = got_ref.shape[:2]
        self.rows, self.each, self.width = rows, each, width
        self.lines = 2 * each
        self.tiles = width // LANES
        self.pair = (got_ref.shape[2] - self.lines) // (each * self.tiles)
        self.sensors = self.pair // 2
        self.lanes = self.low * self.pair
        self.held = rows * self.lines
        shape = (self.held, self.lanes)
        row = iota(shape, 0)
        self.real_row = row % 2 == 0
        self.real_lane = iota(shape, 1) // self.sensors % 2 == 0
        self.freq = row // 2 % each
        self.joint = max(1, min(each, DEPTH // self.lanes))

    def swapped(self, x):
        return jnp.where(self.real_row, roll(x, -1, 0), roll(x, 1, 0))

    def block(self, first, p):
        return jnp.concatenate(
            [
                jnp.concatenate(
                    [
                        self.got[
                            :, p, pl.ds((f * self.tiles + j) * self.pair, self.pair), :
                        ].reshape(self.lanes, LANES)
                        for j in range(self.tiles)
                    ],
                    axis=1,
                )
                for f in range(first, first + self.joint)
            ],
            axis=0,
        )

    def spectra(self):
        tail = self.got[:, 0, pl.ds(self.got.shape[2] - self.lines, self.lines), :]
        tail = tail.astype(jnp.float32)
        filled = self.rows * self.pair
        shape = (self.lines, LANES)
        at = iota(shape, 1) // self.pair
        per = LANES // self.pair
        found = [
            [jnp.zeros(shape, jnp.float32) for _ in range(self.lanes // LANES)]
            for _ in range(self.rows)
        ]
        for i in range(self.low):
            packed = tail[i]
            packed = packed + roll(packed, -filled, 1) + roll(packed, -2 * filled, 1)
            h, place = divmod(i, per)
            for r in range(self.rows):
                moved = roll(packed, (place - r) * self.pair, 1)
                found[r][h] = jnp.where(at == place, moved, found[r][h])
        return jnp.concatenate([jnp.concatenate(line, axis=1) for line in found], axis=0)

    def adjoint(self, record):
        crossed = self.swapped(record)
        crossed = roll(jnp.where(self.real_row, crossed, -crossed), self.sensors, 1)
        left = jnp.where(self.real_lane, record, crossed)
        sums = [jnp.zeros((self.held, self.width), jnp.float32) for _ in range(self.par)]
        for first in range(0, self.each, self.joint):
            part = [
                jnp.where(self.freq == f, left, 0.0) for f in range(first, first + self.joint)
            ]
            part = jnp.concatenate(part, axis=1).astype(jnp.bfloat16)
            for p in range(self.par):
                sums[p] += jnp.dot(
                    part, self.block(first, p), preferred_element_type=jnp.float32
                )
        return sums

    def smoothed(self, field, coef_ref, link_ref):
        shape = (self.held, self.width)
        column = iota((1, self.width), 1)
        coefs, links = [], []
        for x in range(self.par):
            coefs.append(jnp.broadcast_to(coef_ref[x : x + 1, :], shape))
            offset = link_ref[x : x + 1, :]
            masks = []
            for shift in range(-REACH, REACH + 1):
                inside = (column + shift >= 0) & (column + shift < self.width)
                mask = jnp.where((offset == shift) & inside, 1.0, 0.0)
                masks.append(jnp.broadcast_to(mask, shape))
            links.append(masks)
        after_first = jnp.broadcast_to(jnp.where(column > 0, 1.0, 0.0), shape)
        before_last = jnp.broadcast_to(jnp.where(column < self.width - 1, 1.0, 0.0), shape)
        for _ in range(SWEEPS):
            after = []
            for x, u in enumerate(field):
                around = roll(u, 1, 1) * after_first + roll(u, -1, 1) * before_last
                if x > 0:
                    around += field[x - 1]
                if x < self.par - 1:
                    linked = jnp.zeros(shape, jnp.float32)
                    for mask, shift in zip(links[x], range(-REACH, REACH + 1)):
                        linked += mask * roll(field[x + 1], -shift, 1)
                    around += linked
                after.append(u + coefs[x] * (around - 4.0 * u))
            field = after
        return field

    def forward(self, field):
        prior = [u.astype(jnp.bfloat16) for u in field]
        out = jnp.zeros((self.held, self.lanes), jnp.float32)
        for first in range(0, self.each, self.joint):
            part = jnp.zeros((self.held, self.joint * self.lanes), jnp.float32)
            for p in range(self.par):
                part += lax.dot_general(
                    prior[p],
                    self.block(first, p),
                    (((1,), (1,)), ((), ())),
                    preferred_element_type=jnp.float32,
                )
            for i in range(self.joint):
                own = part[:, i * self.lanes : (i + 1) * self.lanes]
                out = jnp.where(self.freq == first + i, own, out)
        crossed = self.swapped(roll(out, -self.sensors, 1))
        return out + jnp.where(self.real_row, -crossed, crossed)

    def messages(self, residual, applied, out_ref):
        both = jnp.where(self.real_lane, residual, roll(applied, self.sensors, 1))
        per = LANES // self.pair
        to, group = iota((per, LANES), 0), iota((per, LANES), 1) // self.pair
        for g in range(self.held // per):
            for h in range(self.lanes // LANES):
                tile = both[g * per : (g + 1) * per, h * LANES : (h + 1) * LANES]
                moved = tile
                for turn in range(1, per):
                    turned = roll(roll(tile, -turn, 0), turn * self.pair, 1)
                    moved = jnp.where((group - to + per) % per == turn, turned, moved)
                for i in range(per):
                    for p in range(self.par):
                        out_ref[(h * per + i) * self.par + p, g : g + 1, :] = moved[i : i + 1, :]


def give(sums, own_ref, sent_ref):
    for p, part in enumerate(sums):
        own_ref[p] = part
        sent_ref[p] = part.astype(sent_ref.dtype)


def first_kernel(share, got_ref, spectra_ref, own_ref, sent_ref):
    share = share(got_ref)
    spectra = share.spectra()
    spectra_ref[...] = spectra
    give(share.adjoint(spectra), own_ref, sent_ref)


def summed(one_ref, other_ref):
    return [one_ref[x] + other_ref[x].astype(jnp.float32) for x in range(one_ref.shape[0])]


def middle_kernel(
    share, got_ref, one_ref, other_ref, spectra_ref, coef_ref, link_ref, residual_ref, own_ref, sent_ref
):
    share = share(got_ref)
    rest = roll(spectra_ref[...], -share.sensors, 1)
    field = share.smoothed(summed(one_ref, other_ref), coef_ref, link_ref)
    residual = rest - share.forward(field)
    residual_ref[...] = residual
    give(share.adjoint(residual), own_ref, sent_ref)


def last_kernel(share, got_ref, one_ref, other_ref, residual_ref, coef_ref, link_ref, out_ref):
    share = share(got_ref)
    field = share.smoothed(summed(one_ref, other_ref), coef_ref, link_ref)
    share.messages(residual_ref[...], share.forward(field), out_ref)


def home_kernel(got_ref, basis_ref, noise_ref, residual_ref, applied_ref):
    sensors = noise_ref.shape[1]
    rows = residual_ref.shape[0]
    pair = 2 * sensors
    noise = upright(noise_ref[...])
    groups = got_ref.shape[1] // rows
    lines = []
    for r in range(rows):
        parts = []
        for g in range(groups):
            turned = got_ref[:, r * groups + g, :].T
            parts += [turned[i : i + pair, :] for i in range(0, LANES, pair)]
        lines.append(jnp.concatenate(parts, axis=1))
    back = jnp.dot(
        jnp.concatenate(lines, axis=0),
        basis_ref[...],
        precision=lax.Precision.HIGHEST,
        preferred_element_type=jnp.float32,
    )
    for r in range(rows):
        residual = back[r * pair : r * pair + sensors]
        residual_ref[r] = residual
        applied_ref[r] = back[r * pair + sensors : (r + 1) * pair] + noise * residual


def body_fast(vectors, observed, operator, noise, coefficient, offsets):
    top, low, par = (lax.axis_size(axis) for axis in ("top", "low", "par"))
    rows, sensors, length = vectors.shape
    width = coefficient.shape[1]
    shares = low * par
    each = length // 2 // shares
    pair = 2 * sensors
    axes = ("low", "par")
    basis = make_basis(length).reshape(length, 2, shares, each)
    noise = noise[None, :]
    f32 = lambda *shape: jax.ShapeDtypeStruct(shape, jnp.float32)
    room = lambda mib: pltpu.CompilerParams(vmem_limit_bytes=mib * 2**20)

    steps = 4 if shares % 4 == 0 else 1
    tall = each * width // LANES * pair + 2 * each
    operator = operator.reshape(2, shares, each, sensors, width)
    scratch = [
        pltpu.VMEM(array.shape, array.dtype) for array in (operator, vectors, observed, noise)
    ]
    message = pl.pallas_call(
        outbound_kernel,
        in_specs=[pl.BlockSpec(memory_space=pl.ANY)] * 5,
        out_specs=pl.BlockSpec(memory_space=pl.ANY),
        out_shape=jax.ShapeDtypeStruct((shares, tall, LANES), jnp.bfloat16),
        scratch_shapes=scratch
        + [
            pltpu.VMEM((length, length), jnp.float32),
            pltpu.VMEM((shares, tall, LANES), jnp.bfloat16),
            pltpu.SemaphoreType.DMA((4,)),
            pltpu.SemaphoreType.DMA((steps,)),
            pltpu.SemaphoreType.DMA((steps + 1,)),
        ],
        compiler_params=room(60),
        name="outbound",
    )(
        operator,
        vectors,
        observed,
        noise,
        jnp.asarray(basis.transpose(2, 3, 1, 0).reshape(length, length)),
    )
    got = lax.all_to_all(message, axes, 0, 0, tiled=True).reshape(low, par, tall, LANES)

    grid = jnp.concatenate([coefficient, offsets.astype(jnp.float32)])
    grid = lax.all_gather(grid, "par").transpose(1, 0, 2)
    coefs, links = grid[0], grid[1].astype(jnp.int32)

    def across(sums):
        return lax.ppermute(sums, "top", [(i, (i + 1) % top) for i in range(top)])

    share = functools.partial(Share, rows=rows, each=each, width=width)
    held, lanes = rows * 2 * each, low * pair
    sums = [f32(par, held, width), jax.ShapeDtypeStruct((par, held, width), jnp.bfloat16)]
    spectra, one, sent = pl.pallas_call(
        functools.partial(first_kernel, share),
        out_shape=[f32(held, lanes)] + sums,
        compiler_params=room(32),
        name="first_adjoint",
    )(got)
    residual, two, sent_too = pl.pallas_call(
        functools.partial(middle_kernel, share),
        out_shape=[f32(held, lanes)] + sums,
        compiler_params=room(32),
        name="forward_adjoint",
    )(got, one, across(sent), spectra, coefs, links)
    message = pl.pallas_call(
        functools.partial(last_kernel, share),
        out_shape=f32(shares, held * pair // LANES, LANES),
        compiler_params=room(32),
        name="last_forward",
    )(got, two, across(sent_too), residual, coefs, links)
    got = lax.all_to_all(message, axes, 0, 0, tiled=True)
    return pl.pallas_call(
        home_kernel,
        out_shape=[f32(rows, sensors, length)] * 2,
        compiler_params=room(16),
        name="to_time",
    )(got, jnp.asarray(basis.transpose(3, 1, 2, 0).reshape(length, length)), noise)


def fits(mesh, args):
    vectors, _, _, _, coefficient, _ = args
    sen, par = mesh.shape["sen"], mesh.shape["par"]
    rows, sensors, length = vectors.shape
    half, low = length // 2, sen // 2
    if sen % 2 or half % (low * par) or sensors % sen or coefficient.shape[0] != par:
        return False
    each, pair = half // (low * par), 2 * (sensors // sen)
    return (
        pair == 16
        and each % 8 == 0
        and 3 * rows * pair <= LANES
        and low * pair % LANES == 0
        and coefficient.shape[1] % LANES == 0
    )


def solution(mesh):
    def whole(*args):
        if fits(mesh, args):
            body, sen = body_fast, ("top", "low")
            shape = (2, mesh.shape["sen"] // 2, mesh.shape["par"])
            within = Mesh(mesh.devices.reshape(shape), sen + ("par",))
        else:
            body, sen, within = body_plain, "sen", mesh
        record = P(None, sen, None)
        return jax.shard_map(
            body,
            mesh=within,
            in_specs=(
                record,
                record,
                P(None, None, sen, "par"),
                P(sen),
                P("par", None),
                P("par", None),
            ),
            out_specs=(record, record),
            check_vma=False,
        )(*args)

    return whole
```

```python
import functools
import math

import jax
import jax.numpy as jnp
import numpy as np
from jax import lax
from jax.experimental import pallas as pl
from jax.experimental.pallas import tpu as pltpu
from jax.sharding import Mesh
from jax.sharding import PartitionSpec as P

SWEEPS = 4
REACH = 3
LANES = 128
DEPTH = 256


def make_basis(length):
    half = length // 2
    times = np.arange(length)[:, None]
    freqs = np.arange(half)[None, :]
    phase = (2 * freqs + 1) * times % (2 * length)
    angle = phase.astype(np.float64) * (math.pi / length)
    scale = math.sqrt(2.0 / length)
    return (np.concatenate([np.cos(angle), np.sin(angle)], axis=1) * scale).astype(np.float32)


def halo(field, axis, dim):
    count = lax.axis_size(axis)
    if count == 1:
        edge = jnp.zeros_like(lax.slice_in_dim(field, 0, 1, axis=dim))
        return jnp.concatenate([edge, field, edge], axis=dim)
    ends = count - 1
    head = lax.slice_in_dim(field, 0, 1, axis=dim)
    tail = lax.slice_in_dim(field, field.shape[dim] - 1, field.shape[dim], axis=dim)
    return jnp.concatenate(
        [
            lax.ppermute(tail, axis, [(i, i + 1) for i in range(ends)]),
            field,
            lax.ppermute(head, axis, [(i + 1, i) for i in range(ends)]),
        ],
        axis=dim,
    )


def zero_halo(field):
    return jnp.pad(field, [(0, 0)] * (field.ndim - 2) + [(1, 1), (0, 0)])


def smooth(field, coefficient, offsets, extend):
    width = field.shape[-1]
    lead = [(0, 0)] * (field.ndim - 1)
    for _ in range(SWEEPS):
        padded = extend(field)
        upper = padded[..., :-2, :]
        lower = jnp.pad(padded[..., 2:, :], lead + [(REACH, REACH)])
        linked = jnp.zeros_like(field)
        for shift in range(-REACH, REACH + 1):
            start = REACH + shift
            linked = linked + jnp.where(offsets == shift, lower[..., start : start + width], 0.0)
        sides = jnp.pad(field, lead + [(1, 1)])
        field = field + coefficient * (
            sides[..., :-2] + sides[..., 2:] + upper + linked - 4.0 * field
        )
    return field


def apply_part(spectrum, operator, coefficient, offsets, extend):
    low = spectrum.astype(jnp.bfloat16)

    def adjoint_of(spec, resp):
        return jnp.einsum("frs,fsp->frp", spec, resp, preferred_element_type=jnp.float32)

    def forward_of(par, resp):
        return jnp.einsum("frp,fsp->frs", par, resp, preferred_element_type=jnp.float32)

    real = adjoint_of(low[0], operator[0]) + adjoint_of(low[1], operator[1])
    imag = adjoint_of(low[1], operator[0]) - adjoint_of(low[0], operator[1])
    adjoint = jnp.stack([real, imag])
    grid = adjoint.reshape(adjoint.shape[:3] + coefficient.shape)
    prior = smooth(grid, coefficient, offsets, extend).astype(jnp.bfloat16)
    prior = prior.reshape(adjoint.shape)
    real = forward_of(prior[0], operator[0]) - forward_of(prior[1], operator[1])
    imag = forward_of(prior[1], operator[0]) + forward_of(prior[0], operator[1])
    return jnp.stack([real, imag])


def body_plain(vectors, observed, operator, noise, coefficient, offsets):
    sen, par = lax.axis_size("sen"), lax.axis_size("par")
    rows, sensors, length = vectors.shape
    half = length // 2
    grid_rows, width = coefficient.shape
    basis = jnp.asarray(make_basis(length))
    both = jnp.stack([vectors, observed])
    spectra = jnp.dot(
        both.reshape(2 * rows * sensors, length), basis, precision=lax.Precision.HIGHEST
    )
    spectra = spectra.reshape(2, rows, sensors, 2, half)
    whole_cells = half % (sen * par) == 0
    axes = ("sen", "par") if whole_cells else "sen"
    shares = sen * par if whole_cells else sen
    each = half // shares

    cut = operator.reshape(2, shares, each, sensors, grid_rows, width)
    cut = lax.all_to_all(cut, axes, 1, 1, tiled=True)
    if whole_cells:
        resp = cut.reshape(2, sen, par, each, sensors, grid_rows, width)
        resp = resp.transpose(0, 3, 1, 4, 2, 5, 6)
        resp = resp.reshape(2, each, sen * sensors, par * grid_rows * width)
        coefficient = lax.all_gather(coefficient, "par", tiled=True)
        offsets = lax.all_gather(offsets, "par", tiled=True)
        extend = zero_halo
    else:
        resp = cut.transpose(0, 2, 1, 3, 4, 5)
        resp = resp.reshape(2, each, sen * sensors, grid_rows * width)
        extend = lambda field: halo(field, "par", field.ndim - 2)

    def to_frequencies(spec):
        parts = spec.shape[0]
        cut = spec.reshape(parts, rows, sensors, 2, shares, each)
        cut = lax.all_to_all(cut.transpose(4, 0, 3, 5, 1, 2), axes, 0, 0, tiled=True)
        if whole_cells:
            cut = cut.reshape((sen, par) + cut.shape[1:])[:, 0]
        return cut.transpose(1, 2, 3, 4, 0, 5).reshape(parts, 2, each, rows, sen * sensors)

    def to_sensors(spec):
        parts = spec.shape[0]
        cut = spec.reshape(parts, 2, each, rows, sen, sensors).transpose(4, 0, 3, 5, 1, 2)
        if whole_cells:
            cut = jnp.repeat(cut, par, axis=0)
        cut = lax.all_to_all(cut, axes, 0, 0, tiled=True)
        return cut.transpose(1, 2, 3, 4, 0, 5).reshape(parts, rows, sensors, 2 * half)

    def hessian(spectrum):
        forward = apply_part(spectrum, resp, coefficient, offsets, extend)
        return forward if whole_cells else lax.psum(forward, "par")

    rest = spectra[1] - noise[None, :, None, None] * spectra[0]
    own, rest = to_frequencies(jnp.stack([spectra[0], rest]))
    left = rest - hessian(own)
    again = hessian(left)
    home = to_sensors(jnp.stack([left, again]))
    back = jnp.dot(
        home.reshape(2 * rows * sensors, length), basis.T, precision=lax.Precision.HIGHEST
    ).reshape(2, rows, sensors, length)
    residual = back[0]
    applied = back[1] + noise[None, :, None] * residual
    return (residual, applied)


def roll(x, shift, axis):
    size = x.shape[axis]
    return x if shift % size == 0 else pltpu.roll(x, shift % size, axis)


def iota(shape, axis):
    return lax.broadcasted_iota(jnp.int32, shape, axis)


def upright(line):
    count = line.shape[1]
    square = jnp.broadcast_to(line, (count, count))
    square = jnp.where(iota((count, count), 0) == iota((count, count), 1), square, 0.0)
    return jnp.sum(square, axis=1, keepdims=True)


def split(x):
    high = x.astype(jnp.bfloat16).astype(jnp.float32)
    middle = (x - high).astype(jnp.bfloat16).astype(jnp.float32)
    return high, middle, (x - high - middle).astype(jnp.bfloat16).astype(jnp.float32)


def tail_lanes(rows, pair):
    start = 3 * rows * pair
    return start, LANES // (LANES - start), LANES - start


def outbound_kernel(
    resp_hbm, vectors_hbm, observed_hbm, noise_hbm, coef_hbm, link_hbm, basis_hbm, out_hbm,
    resp_ref, vectors_ref, observed_ref, noise_ref, coef_ref, link_ref, basis_ref, out_ref,
    small_sems, in_sems, out_sems,
):
    _, devices, each, sensors, width = resp_ref.shape
    pair, lines = 2 * sensors, 2 * each
    tiles = width // LANES
    steps = in_sems.shape[0]
    some = devices // steps
    pieces = [pl.ds(i * some, some) for i in range(steps)]
    small = [
        pltpu.make_async_copy(src, dst, small_sems.at[i])
        for i, (src, dst) in enumerate(
            [
                (basis_hbm, basis_ref),
                (vectors_hbm, vectors_ref),
                (observed_hbm, observed_ref),
                (noise_hbm, noise_ref),
                (coef_hbm, coef_ref),
                (link_hbm, link_ref),
            ]
        )
    ]
    loads = [
        pltpu.make_async_copy(resp_hbm.at[:, piece], resp_ref.at[:, piece], in_sems.at[i])
        for i, piece in enumerate(pieces)
    ]
    body = each * tiles * pair
    parts = [(piece, pl.ds(0, body)) for piece in pieces] + [(pl.ds(0, devices), pl.ds(body, lines))]
    stores = [
        pltpu.make_async_copy(out_ref.at[part], out_hbm.at[part], out_sems.at[i])
        for i, part in enumerate(parts)
    ]
    for copy in loads + small:
        copy.start()

    for i, piece in enumerate(pieces):
        loads[i].wait()
        for f in range(each):
            for j in range(tiles):
                lanes = pl.ds(j * LANES, LANES)
                both = [resp_ref[c, piece, f, :, lanes] for c in range(2)]
                lane_rows = pl.ds((f * tiles + j) * pair, pair)
                out_ref[piece, lane_rows, :] = jnp.concatenate(both, axis=1)
        stores[i].start()

    for copy in small:
        copy.wait()
    rows = vectors_ref.shape[0]
    noise = upright(noise_ref[...])
    records = []
    for r in range(rows):
        record = vectors_ref[r]
        records += [record, observed_ref[r] - noise * record]
    filled = rows * pair
    records.append(jnp.zeros((LANES - filled, records[0].shape[1]), jnp.float32))
    spectra = lax.dot_general(
        basis_ref[...],
        jnp.concatenate(records, axis=0),
        (((1,), (1,)), ((), ())),
        precision=lax.Precision.HIGHEST,
        preferred_element_type=jnp.float32,
    )
    exact = iota(spectra.shape, 1) // sensors % 2 == 1
    high, middle, low = split(spectra)
    packed = high + roll(jnp.where(exact, middle, 0.0), filled, 1)
    packed = packed + roll(jnp.where(exact, low, 0.0), 2 * filled, 1)

    start, chunks, free = tail_lanes(rows, pair)
    turn = lax.axis_index("low") % tiles
    coefs, links = (
        sum(
            jnp.where(turn == j, ref[:, j * LANES : (j + 1) * LANES].astype(jnp.float32), 0.0)
            for j in range(tiles)
        )
        for ref in (coef_ref, link_ref)
    )
    grid = jnp.concatenate([*split(coefs), links], axis=0)
    grid = jnp.concatenate([roll(grid, start - i * free, 1) for i in range(chunks)], axis=0)
    grid = jnp.where(iota(grid.shape, 1) >= start, grid, 0.0)
    packed = packed.reshape(devices, lines, LANES) + grid[None]
    packed = packed.astype(jnp.bfloat16)
    out_ref[:, pl.ds(body, lines), :] = packed
    stores[-1].start()
    for copy in stores:
        copy.wait()


class Share:
    def __init__(self, got_ref, rows, each, width):
        self.got = got_ref
        self.low, self.par = got_ref.shape[:2]
        self.rows, self.each, self.width = rows, each, width
        self.lines = 2 * each
        self.tiles = width // LANES
        self.pair = (got_ref.shape[2] - self.lines) // (each * self.tiles)
        self.sensors = self.pair // 2
        self.lanes = self.low * self.pair
        self.held = rows * self.lines
        shape = (self.held, self.lanes)
        row = iota(shape, 0)
        self.real_row = row % 2 == 0
        self.real_lane = iota(shape, 1) // self.sensors % 2 == 0
        self.freq = row // 2 % each
        self.joint = max(1, min(each, DEPTH // self.lanes))

    def swapped(self, x):
        return jnp.where(self.real_row, roll(x, -1, 0), roll(x, 1, 0))

    def block(self, first, p):
        return jnp.concatenate(
            [
                jnp.concatenate(
                    [
                        self.got[
                            :, p, pl.ds((f * self.tiles + j) * self.pair, self.pair), :
                        ].reshape(self.lanes, LANES)
                        for j in range(self.tiles)
                    ],
                    axis=1,
                )
                for f in range(first, first + self.joint)
            ],
            axis=0,
        )

    def spectra(self):
        tail = self.got[:, 0, pl.ds(self.got.shape[2] - self.lines, self.lines), :]
        tail = tail.astype(jnp.float32)
        filled = self.rows * self.pair
        shape = (self.lines, LANES)
        at = iota(shape, 1) // self.pair
        per = LANES // self.pair
        found = [
            [jnp.zeros(shape, jnp.float32) for _ in range(self.lanes // LANES)]
            for _ in range(self.rows)
        ]
        for i in range(self.low):
            packed = tail[i]
            packed = packed + roll(packed, -filled, 1) + roll(packed, -2 * filled, 1)
            h, place = divmod(i, per)
            for r in range(self.rows):
                moved = roll(packed, (place - r) * self.pair, 1)
                found[r][h] = jnp.where(at == place, moved, found[r][h])
        return jnp.concatenate([jnp.concatenate(line, axis=1) for line in found], axis=0)

    def grid(self):
        start, chunks, free = tail_lanes(self.rows, self.pair)
        kinds = self.lines // chunks
        chunk = iota((kinds, LANES), 1) // free
        coefs, links = [], []
        for p in range(self.par):
            tail = self.got[
                pl.ds(0, self.tiles), p, pl.ds(self.got.shape[2] - self.lines, self.lines), :
            ].astype(jnp.float32)
            found = []
            for j in range(self.tiles):
                line = jnp.zeros((kinds, LANES), jnp.float32)
                for i in range(chunks):
                    part = roll(tail[j, i * kinds : (i + 1) * kinds], i * free - start, 1)
                    line = jnp.where(chunk == i, part, line)
                found.append(line)
            found = jnp.concatenate(found, axis=1)
            coefs.append(found[0:1] + found[1:2] + found[2:3])
            links.append(found[3:4])
        return jnp.concatenate(coefs, axis=0), jnp.concatenate(links, axis=0)

    def adjoint(self, record):
        crossed = self.swapped(record)
        crossed = roll(jnp.where(self.real_row, crossed, -crossed), self.sensors, 1)
        left = jnp.where(self.real_lane, record, crossed)
        sums = [jnp.zeros((self.held, self.width), jnp.float32) for _ in range(self.par)]
        for first in range(0, self.each, self.joint):
            part = [
                jnp.where(self.freq == f, left, 0.0) for f in range(first, first + self.joint)
            ]
            part = jnp.concatenate(part, axis=1).astype(jnp.bfloat16)
            for p in range(self.par):
                sums[p] += jnp.dot(
                    part, self.block(first, p), preferred_element_type=jnp.float32
                )
        return sums

    def smoothed(self, field, coef_ref, link_ref):
        shape = (self.held, self.width)
        column = iota((1, self.width), 1)
        coefs, links = [], []
        for x in range(self.par):
            coefs.append(jnp.broadcast_to(coef_ref[x : x + 1, :], shape))
            offset = link_ref[x : x + 1, :]
            masks = []
            for shift in range(-REACH, REACH + 1):
                inside = (column + shift >= 0) & (column + shift < self.width)
                mask = jnp.where((offset == float(shift)) & inside, 1.0, 0.0)
                masks.append(jnp.broadcast_to(mask, shape))
            links.append(masks)
        after_first = jnp.broadcast_to(jnp.where(column > 0, 1.0, 0.0), shape)
        before_last = jnp.broadcast_to(jnp.where(column < self.width - 1, 1.0, 0.0), shape)
        for _ in range(SWEEPS):
            after = []
            for x, u in enumerate(field):
                around = roll(u, 1, 1) * after_first + roll(u, -1, 1) * before_last
                if x > 0:
                    around += field[x - 1]
                if x < self.par - 1:
                    linked = jnp.zeros(shape, jnp.float32)
                    for mask, shift in zip(links[x], range(-REACH, REACH + 1)):
                        linked += mask * roll(field[x + 1], -shift, 1)
                    around += linked
                after.append(u + coefs[x] * (around - 4.0 * u))
            field = after
        return field

    def forward(self, field):
        prior = [u.astype(jnp.bfloat16) for u in field]
        out = jnp.zeros((self.held, self.lanes), jnp.float32)
        for first in range(0, self.each, self.joint):
            part = jnp.zeros((self.held, self.joint * self.lanes), jnp.float32)
            for p in range(self.par):
                part += lax.dot_general(
                    prior[p],
                    self.block(first, p),
                    (((1,), (1,)), ((), ())),
                    preferred_element_type=jnp.float32,
                )
            for i in range(self.joint):
                own = part[:, i * self.lanes : (i + 1) * self.lanes]
                out = jnp.where(self.freq == first + i, own, out)
        crossed = self.swapped(roll(out, -self.sensors, 1))
        return out + jnp.where(self.real_row, -crossed, crossed)

    def messages(self, residual, applied, out_ref):
        both = jnp.where(self.real_lane, residual, roll(applied, self.sensors, 1))
        per = LANES // self.pair
        to, group = iota((per, LANES), 0), iota((per, LANES), 1) // self.pair
        for g in range(self.held // per):
            for h in range(self.lanes // LANES):
                tile = both[g * per : (g + 1) * per, h * LANES : (h + 1) * LANES]
                moved = tile
                for turn in range(1, per):
                    turned = roll(roll(tile, -turn, 0), turn * self.pair, 1)
                    moved = jnp.where((group - to + per) % per == turn, turned, moved)
                for i in range(per):
                    for p in range(self.par):
                        out_ref[(h * per + i) * self.par + p, g : g + 1, :] = moved[i : i + 1, :]


def give(sums, own_ref, sent_ref):
    for p, part in enumerate(sums):
        own_ref[p] = part
        sent_ref[p] = part.astype(sent_ref.dtype)


def first_kernel(share, got_ref, spectra_ref, coef_ref, link_ref, own_ref, sent_ref):
    share = share(got_ref)
    coef_ref[...], link_ref[...] = share.grid()
    spectra = share.spectra()
    spectra_ref[...] = spectra
    give(share.adjoint(spectra), own_ref, sent_ref)


def summed(one_ref, other_ref):
    return [one_ref[x] + other_ref[x].astype(jnp.float32) for x in range(one_ref.shape[0])]


def middle_kernel(
    share, got_ref, one_ref, other_ref, spectra_ref, coef_ref, link_ref, residual_ref, own_ref, sent_ref
):
    share = share(got_ref)
    rest = roll(spectra_ref[...], -share.sensors, 1)
    field = share.smoothed(summed(one_ref, other_ref), coef_ref, link_ref)
    residual = rest - share.forward(field)
    residual_ref[...] = residual
    give(share.adjoint(residual), own_ref, sent_ref)


def last_kernel(share, got_ref, one_ref, other_ref, residual_ref, coef_ref, link_ref, out_ref):
    share = share(got_ref)
    field = share.smoothed(summed(one_ref, other_ref), coef_ref, link_ref)
    share.messages(residual_ref[...], share.forward(field), out_ref)


def home_kernel(got_ref, basis_ref, noise_ref, residual_ref, applied_ref):
    sensors = noise_ref.shape[1]
    rows = residual_ref.shape[0]
    pair = 2 * sensors
    noise = upright(noise_ref[...])
    groups = got_ref.shape[1] // rows
    lines = []
    for r in range(rows):
        parts = []
        for g in range(groups):
            turned = got_ref[:, r * groups + g, :].T
            parts += [turned[i : i + pair, :] for i in range(0, LANES, pair)]
        lines.append(jnp.concatenate(parts, axis=1))
    back = jnp.dot(
        jnp.concatenate(lines, axis=0),
        basis_ref[...],
        precision=lax.Precision.HIGHEST,
        preferred_element_type=jnp.float32,
    )
    for r in range(rows):
        residual = back[r * pair : r * pair + sensors]
        residual_ref[r] = residual
        applied_ref[r] = back[r * pair + sensors : (r + 1) * pair] + noise * residual


def body_fast(vectors, observed, operator, noise, coefficient, offsets):
    top, low, par = (lax.axis_size(axis) for axis in ("top", "low", "par"))
    rows, sensors, length = vectors.shape
    width = coefficient.shape[1]
    shares = low * par
    each = length // 2 // shares
    pair = 2 * sensors
    axes = ("low", "par")
    basis = make_basis(length).reshape(length, 2, shares, each)
    noise = noise[None, :]
    small = (vectors, observed, noise, coefficient, offsets)
    f32 = lambda *shape: jax.ShapeDtypeStruct(shape, jnp.float32)
    room = lambda mib: pltpu.CompilerParams(vmem_limit_bytes=mib * 2**20)

    steps = 4 if shares % 4 == 0 else 1
    tall = each * width // LANES * pair + 2 * each
    operator = operator.reshape(2, shares, each, sensors, width)
    scratch = [
        pltpu.VMEM(array.shape, array.dtype) for array in (operator, *small)
    ]
    message = pl.pallas_call(
        outbound_kernel,
        in_specs=[pl.BlockSpec(memory_space=pl.ANY)] * 7,
        out_specs=pl.BlockSpec(memory_space=pl.ANY),
        out_shape=jax.ShapeDtypeStruct((shares, tall, LANES), jnp.bfloat16),
        scratch_shapes=scratch
        + [
            pltpu.VMEM((length, length), jnp.float32),
            pltpu.VMEM((shares, tall, LANES), jnp.bfloat16),
            pltpu.SemaphoreType.DMA((6,)),
            pltpu.SemaphoreType.DMA((steps,)),
            pltpu.SemaphoreType.DMA((steps + 1,)),
        ],
        compiler_params=room(60),
        name="outbound",
    )(
        operator,
        *small,
        jnp.asarray(basis.transpose(2, 3, 1, 0).reshape(length, length)),
    )
    got = lax.all_to_all(message, axes, 0, 0, tiled=True).reshape(low, par, tall, LANES)

    def across(sums):
        return lax.ppermute(sums, "top", [(i, (i + 1) % top) for i in range(top)])

    share = functools.partial(Share, rows=rows, each=each, width=width)
    held, lanes = rows * 2 * each, low * pair
    sums = [f32(par, held, width), jax.ShapeDtypeStruct((par, held, width), jnp.bfloat16)]
    grid = [f32(par, width)] * 2
    spectra, coefs, links, one, sent = pl.pallas_call(
        functools.partial(first_kernel, share),
        out_shape=[f32(held, lanes)] + grid + sums,
        compiler_params=room(32),
        name="first_adjoint",
    )(got)
    residual, two, sent_too = pl.pallas_call(
        functools.partial(middle_kernel, share),
        out_shape=[f32(held, lanes)] + sums,
        compiler_params=room(32),
        name="forward_adjoint",
    )(got, one, across(sent), spectra, coefs, links)
    message = pl.pallas_call(
        functools.partial(last_kernel, share),
        out_shape=f32(shares, held * pair // LANES, LANES),
        compiler_params=room(32),
        name="last_forward",
    )(got, two, across(sent_too), residual, coefs, links)
    got = lax.all_to_all(message, axes, 0, 0, tiled=True)
    return pl.pallas_call(
        home_kernel,
        out_shape=[f32(rows, sensors, length)] * 2,
        compiler_params=room(16),
        name="to_time",
    )(got, jnp.asarray(basis.transpose(3, 1, 2, 0).reshape(length, length)), noise)


def fits(mesh, args):
    vectors, _, _, _, coefficient, _ = args
    sen, par = mesh.shape["sen"], mesh.shape["par"]
    rows, sensors, length = vectors.shape
    half, low = length // 2, sen // 2
    if sen % 2 or half % (low * par) or sensors % sen or coefficient.shape[0] != par:
        return False
    each, pair = half // (low * par), 2 * (sensors // sen)
    return (
        pair == 16
        and 3 * rows * pair < LANES
        and each % 8 == 0
        and LANES % (LANES - 3 * rows * pair) == 0
        and 4 * tail_lanes(rows, pair)[1] == 2 * each
        and low * LANES >= coefficient.shape[1]
        and low * pair % LANES == 0
        and coefficient.shape[1] % LANES == 0
    )


def solution(mesh):
    def whole(*args):
        if fits(mesh, args):
            body, sen = body_fast, ("top", "low")
            shape = (2, mesh.shape["sen"] // 2, mesh.shape["par"])
            within = Mesh(mesh.devices.reshape(shape), sen + ("par",))
        else:
            body, sen, within = body_plain, "sen", mesh
        record = P(None, sen, None)
        return jax.shard_map(
            body,
            mesh=within,
            in_specs=(
                record,
                record,
                P(None, None, sen, "par"),
                P(sen),
                P("par", None),
                P("par", None),
            ),
            out_specs=(record, record),
            check_vma=False,
        )(*args)

    return whole
```

```python
import functools
import math

import jax
import jax.numpy as jnp
import numpy as np
from jax import lax
from jax.experimental import pallas as pl
from jax.experimental.pallas import tpu as pltpu
from jax.sharding import Mesh
from jax.sharding import PartitionSpec as P

SWEEPS = 4
REACH = 3
LANES = 128
DEPTH = 256


def make_basis(length):
    half = length // 2
    times = np.arange(length)[:, None]
    freqs = np.arange(half)[None, :]
    phase = (2 * freqs + 1) * times % (2 * length)
    angle = phase.astype(np.float64) * (math.pi / length)
    scale = math.sqrt(2.0 / length)
    return (np.concatenate([np.cos(angle), np.sin(angle)], axis=1) * scale).astype(np.float32)


def halo(field, axis, dim):
    count = lax.axis_size(axis)
    if count == 1:
        edge = jnp.zeros_like(lax.slice_in_dim(field, 0, 1, axis=dim))
        return jnp.concatenate([edge, field, edge], axis=dim)
    ends = count - 1
    head = lax.slice_in_dim(field, 0, 1, axis=dim)
    tail = lax.slice_in_dim(field, field.shape[dim] - 1, field.shape[dim], axis=dim)
    return jnp.concatenate(
        [
            lax.ppermute(tail, axis, [(i, i + 1) for i in range(ends)]),
            field,
            lax.ppermute(head, axis, [(i + 1, i) for i in range(ends)]),
        ],
        axis=dim,
    )


def zero_halo(field):
    return jnp.pad(field, [(0, 0)] * (field.ndim - 2) + [(1, 1), (0, 0)])


def smooth(field, coefficient, offsets, extend):
    width = field.shape[-1]
    lead = [(0, 0)] * (field.ndim - 1)
    for _ in range(SWEEPS):
        padded = extend(field)
        upper = padded[..., :-2, :]
        lower = jnp.pad(padded[..., 2:, :], lead + [(REACH, REACH)])
        linked = jnp.zeros_like(field)
        for shift in range(-REACH, REACH + 1):
            start = REACH + shift
            linked = linked + jnp.where(offsets == shift, lower[..., start : start + width], 0.0)
        sides = jnp.pad(field, lead + [(1, 1)])
        field = field + coefficient * (
            sides[..., :-2] + sides[..., 2:] + upper + linked - 4.0 * field
        )
    return field


def apply_part(spectrum, operator, coefficient, offsets, extend):
    low = spectrum.astype(jnp.bfloat16)

    def adjoint_of(spec, resp):
        return jnp.einsum("frs,fsp->frp", spec, resp, preferred_element_type=jnp.float32)

    def forward_of(par, resp):
        return jnp.einsum("frp,fsp->frs", par, resp, preferred_element_type=jnp.float32)

    real = adjoint_of(low[0], operator[0]) + adjoint_of(low[1], operator[1])
    imag = adjoint_of(low[1], operator[0]) - adjoint_of(low[0], operator[1])
    adjoint = jnp.stack([real, imag])
    grid = adjoint.reshape(adjoint.shape[:3] + coefficient.shape)
    prior = smooth(grid, coefficient, offsets, extend).astype(jnp.bfloat16)
    prior = prior.reshape(adjoint.shape)
    real = forward_of(prior[0], operator[0]) - forward_of(prior[1], operator[1])
    imag = forward_of(prior[1], operator[0]) + forward_of(prior[0], operator[1])
    return jnp.stack([real, imag])


def body_plain(vectors, observed, operator, noise, coefficient, offsets):
    sen, par = lax.axis_size("sen"), lax.axis_size("par")
    rows, sensors, length = vectors.shape
    half = length // 2
    grid_rows, width = coefficient.shape
    basis = jnp.asarray(make_basis(length))
    both = jnp.stack([vectors, observed])
    spectra = jnp.dot(
        both.reshape(2 * rows * sensors, length), basis, precision=lax.Precision.HIGHEST
    )
    spectra = spectra.reshape(2, rows, sensors, 2, half)
    whole_cells = half % (sen * par) == 0
    axes = ("sen", "par") if whole_cells else "sen"
    shares = sen * par if whole_cells else sen
    each = half // shares

    cut = operator.reshape(2, shares, each, sensors, grid_rows, width)
    cut = lax.all_to_all(cut, axes, 1, 1, tiled=True)
    if whole_cells:
        resp = cut.reshape(2, sen, par, each, sensors, grid_rows, width)
        resp = resp.transpose(0, 3, 1, 4, 2, 5, 6)
        resp = resp.reshape(2, each, sen * sensors, par * grid_rows * width)
        coefficient = lax.all_gather(coefficient, "par", tiled=True)
        offsets = lax.all_gather(offsets, "par", tiled=True)
        extend = zero_halo
    else:
        resp = cut.transpose(0, 2, 1, 3, 4, 5)
        resp = resp.reshape(2, each, sen * sensors, grid_rows * width)
        extend = lambda field: halo(field, "par", field.ndim - 2)

    def to_frequencies(spec):
        parts = spec.shape[0]
        cut = spec.reshape(parts, rows, sensors, 2, shares, each)
        cut = lax.all_to_all(cut.transpose(4, 0, 3, 5, 1, 2), axes, 0, 0, tiled=True)
        if whole_cells:
            cut = cut.reshape((sen, par) + cut.shape[1:])[:, 0]
        return cut.transpose(1, 2, 3, 4, 0, 5).reshape(parts, 2, each, rows, sen * sensors)

    def to_sensors(spec):
        parts = spec.shape[0]
        cut = spec.reshape(parts, 2, each, rows, sen, sensors).transpose(4, 0, 3, 5, 1, 2)
        if whole_cells:
            cut = jnp.repeat(cut, par, axis=0)
        cut = lax.all_to_all(cut, axes, 0, 0, tiled=True)
        return cut.transpose(1, 2, 3, 4, 0, 5).reshape(parts, rows, sensors, 2 * half)

    def hessian(spectrum):
        forward = apply_part(spectrum, resp, coefficient, offsets, extend)
        return forward if whole_cells else lax.psum(forward, "par")

    rest = spectra[1] - noise[None, :, None, None] * spectra[0]
    own, rest = to_frequencies(jnp.stack([spectra[0], rest]))
    left = rest - hessian(own)
    again = hessian(left)
    home = to_sensors(jnp.stack([left, again]))
    back = jnp.dot(
        home.reshape(2 * rows * sensors, length), basis.T, precision=lax.Precision.HIGHEST
    ).reshape(2, rows, sensors, length)
    residual = back[0]
    applied = back[1] + noise[None, :, None] * residual
    return (residual, applied)


def roll(x, shift, axis):
    size = x.shape[axis]
    return x if shift % size == 0 else pltpu.roll(x, shift % size, axis)


def iota(shape, axis):
    return lax.broadcasted_iota(jnp.int32, shape, axis)


def upright(line):
    count = line.shape[1]
    square = jnp.broadcast_to(line, (count, count))
    square = jnp.where(iota((count, count), 0) == iota((count, count), 1), square, 0.0)
    return jnp.sum(square, axis=1, keepdims=True)


def split(x):
    high = x.astype(jnp.bfloat16).astype(jnp.float32)
    middle = (x - high).astype(jnp.bfloat16).astype(jnp.float32)
    return high, middle, (x - high - middle).astype(jnp.bfloat16).astype(jnp.float32)


def tail_lanes(rows, pair):
    start = 3 * rows * pair
    return start, LANES // (LANES - start), LANES - start


def outbound_kernel(
    resp_hbm, vectors_hbm, observed_hbm, noise_hbm, coef_hbm, link_hbm, basis_hbm, out_ref,
    resp_ref, vectors_ref, observed_ref, noise_ref, coef_ref, link_ref, basis_ref,
    small_sems, in_sems,
):
    _, devices, each, sensors, width = resp_ref.shape
    pair, lines = 2 * sensors, 2 * each
    tiles = width // LANES
    steps = in_sems.shape[0]
    some = devices // steps
    pieces = [pl.ds(i * some, some) for i in range(steps)]
    small = [
        pltpu.make_async_copy(src, dst, small_sems.at[i])
        for i, (src, dst) in enumerate(
            [
                (basis_hbm, basis_ref),
                (vectors_hbm, vectors_ref),
                (observed_hbm, observed_ref),
                (noise_hbm, noise_ref),
                (coef_hbm, coef_ref),
                (link_hbm, link_ref),
            ]
        )
    ]
    loads = [
        pltpu.make_async_copy(resp_hbm.at[:, piece], resp_ref.at[:, piece], in_sems.at[i])
        for i, piece in enumerate(pieces)
    ]
    body = each * tiles * pair
    for copy in small + loads:
        copy.start()

    for copy in small:
        copy.wait()
    rows = vectors_ref.shape[0]
    noise = upright(noise_ref[...])
    records = []
    for r in range(rows):
        record = vectors_ref[r]
        records += [record, observed_ref[r] - noise * record]
    filled = rows * pair
    records.append(jnp.zeros((LANES - filled, records[0].shape[1]), jnp.float32))
    spectra = lax.dot_general(
        basis_ref[...],
        jnp.concatenate(records, axis=0),
        (((1,), (1,)), ((), ())),
        precision=lax.Precision.HIGHEST,
        preferred_element_type=jnp.float32,
    )
    exact = iota(spectra.shape, 1) // sensors % 2 == 1
    high, middle, low = split(spectra)
    packed = high + roll(jnp.where(exact, middle, 0.0), filled, 1)
    packed = packed + roll(jnp.where(exact, low, 0.0), 2 * filled, 1)

    start, chunks, free = tail_lanes(rows, pair)
    turn = lax.axis_index("low") % tiles
    coefs, links = (
        sum(
            jnp.where(turn == j, ref[:, j * LANES : (j + 1) * LANES].astype(jnp.float32), 0.0)
            for j in range(tiles)
        )
        for ref in (coef_ref, link_ref)
    )
    grid = jnp.concatenate([*split(coefs), links], axis=0)
    grid = jnp.concatenate([roll(grid, start - i * free, 1) for i in range(chunks)], axis=0)
    grid = jnp.where(iota(grid.shape, 1) >= start, grid, 0.0)
    packed = packed.reshape(devices, lines, LANES) + grid[None]
    packed = packed.astype(jnp.bfloat16)
    out_ref[:, pl.ds(body, lines), :] = packed

    for i, piece in enumerate(pieces):
        loads[i].wait()
        for f in range(each):
            for j in range(tiles):
                lanes = pl.ds(j * LANES, LANES)
                both = [resp_ref[c, piece, f, :, lanes] for c in range(2)]
                lane_rows = pl.ds((f * tiles + j) * pair, pair)
                out_ref[piece, lane_rows, :] = jnp.concatenate(both, axis=1)


class Share:
    def __init__(self, got_ref, rows, each, width):
        self.got = got_ref
        self.low, self.par = got_ref.shape[:2]
        self.rows, self.each, self.width = rows, each, width
        self.lines = 2 * each
        self.tiles = width // LANES
        self.pair = (got_ref.shape[2] - self.lines) // (each * self.tiles)
        self.sensors = self.pair // 2
        self.lanes = self.low * self.pair
        self.held = rows * self.lines
        shape = (self.held, self.lanes)
        row = iota(shape, 0)
        self.real_row = row % 2 == 0
        self.real_lane = iota(shape, 1) // self.sensors % 2 == 0
        self.freq = row // 2 % each
        self.joint = max(1, min(each, DEPTH // self.lanes))

    def swapped(self, x):
        return jnp.where(self.real_row, roll(x, -1, 0), roll(x, 1, 0))

    def block(self, first, p):
        return jnp.concatenate(
            [
                jnp.concatenate(
                    [
                        self.got[
                            :, p, pl.ds((f * self.tiles + j) * self.pair, self.pair), :
                        ].reshape(self.lanes, LANES)
                        for j in range(self.tiles)
                    ],
                    axis=1,
                )
                for f in range(first, first + self.joint)
            ],
            axis=0,
        )

    def spectra(self):
        tail = self.got[:, 0, pl.ds(self.got.shape[2] - self.lines, self.lines), :]
        tail = tail.astype(jnp.float32)
        filled = self.rows * self.pair
        shape = (self.lines, LANES)
        at = iota(shape, 1) // self.pair
        per = LANES // self.pair
        found = [
            [jnp.zeros(shape, jnp.float32) for _ in range(self.lanes // LANES)]
            for _ in range(self.rows)
        ]
        for i in range(self.low):
            packed = tail[i]
            packed = packed + roll(packed, -filled, 1) + roll(packed, -2 * filled, 1)
            h, place = divmod(i, per)
            for r in range(self.rows):
                moved = roll(packed, (place - r) * self.pair, 1)
                found[r][h] = jnp.where(at == place, moved, found[r][h])
        return jnp.concatenate([jnp.concatenate(line, axis=1) for line in found], axis=0)

    def grid(self):
        start, chunks, free = tail_lanes(self.rows, self.pair)
        kinds = self.lines // chunks
        chunk = iota((kinds, LANES), 1) // free
        coefs, links = [], []
        for p in range(self.par):
            tail = self.got[
                pl.ds(0, self.tiles), p, pl.ds(self.got.shape[2] - self.lines, self.lines), :
            ].astype(jnp.float32)
            found = []
            for j in range(self.tiles):
                line = jnp.zeros((kinds, LANES), jnp.float32)
                for i in range(chunks):
                    part = roll(tail[j, i * kinds : (i + 1) * kinds], i * free - start, 1)
                    line = jnp.where(chunk == i, part, line)
                found.append(line)
            found = jnp.concatenate(found, axis=1)
            coefs.append(found[0:1] + found[1:2] + found[2:3])
            links.append(found[3:4])
        return jnp.concatenate(coefs, axis=0), jnp.concatenate(links, axis=0)

    def adjoint(self, record):
        crossed = self.swapped(record)
        crossed = roll(jnp.where(self.real_row, crossed, -crossed), self.sensors, 1)
        left = jnp.where(self.real_lane, record, crossed)
        sums = [jnp.zeros((self.held, self.width), jnp.float32) for _ in range(self.par)]
        for first in range(0, self.each, self.joint):
            part = [
                jnp.where(self.freq == f, left, 0.0) for f in range(first, first + self.joint)
            ]
            part = jnp.concatenate(part, axis=1).astype(jnp.bfloat16)
            for p in range(self.par):
                sums[p] += jnp.dot(
                    part, self.block(first, p), preferred_element_type=jnp.float32
                )
        return sums

    def smoothed(self, field, coef_ref, link_ref):
        shape = (self.held, self.width)
        column = iota((1, self.width), 1)
        coefs, links = [], []
        for x in range(self.par):
            coefs.append(jnp.broadcast_to(coef_ref[x : x + 1, :], shape))
            offset = link_ref[x : x + 1, :]
            masks = []
            for shift in range(-REACH, REACH + 1):
                inside = (column + shift >= 0) & (column + shift < self.width)
                mask = jnp.where((offset == float(shift)) & inside, 1.0, 0.0)
                masks.append(jnp.broadcast_to(mask, shape))
            links.append(masks)
        after_first = jnp.broadcast_to(jnp.where(column > 0, 1.0, 0.0), shape)
        before_last = jnp.broadcast_to(jnp.where(column < self.width - 1, 1.0, 0.0), shape)
        for _ in range(SWEEPS):
            after = []
            for x, u in enumerate(field):
                around = roll(u, 1, 1) * after_first + roll(u, -1, 1) * before_last
                if x > 0:
                    around += field[x - 1]
                if x < self.par - 1:
                    linked = jnp.zeros(shape, jnp.float32)
                    for mask, shift in zip(links[x], range(-REACH, REACH + 1)):
                        linked += mask * roll(field[x + 1], -shift, 1)
                    around += linked
                after.append(u + coefs[x] * (around - 4.0 * u))
            field = after
        return field

    def forward(self, field):
        prior = [u.astype(jnp.bfloat16) for u in field]
        out = jnp.zeros((self.held, self.lanes), jnp.float32)
        for first in range(0, self.each, self.joint):
            part = jnp.zeros((self.held, self.joint * self.lanes), jnp.float32)
            for p in range(self.par):
                part += lax.dot_general(
                    prior[p],
                    self.block(first, p),
                    (((1,), (1,)), ((), ())),
                    preferred_element_type=jnp.float32,
                )
            for i in range(self.joint):
                own = part[:, i * self.lanes : (i + 1) * self.lanes]
                out = jnp.where(self.freq == first + i, own, out)
        crossed = self.swapped(roll(out, -self.sensors, 1))
        return out + jnp.where(self.real_row, -crossed, crossed)

    def messages(self, residual, applied, out_ref):
        both = jnp.where(self.real_lane, residual, roll(applied, self.sensors, 1))
        per = LANES // self.pair
        to, group = iota((per, LANES), 0), iota((per, LANES), 1) // self.pair
        for g in range(self.held // per):
            for h in range(self.lanes // LANES):
                tile = both[g * per : (g + 1) * per, h * LANES : (h + 1) * LANES]
                moved = tile
                for turn in range(1, per):
                    turned = roll(roll(tile, -turn, 0), turn * self.pair, 1)
                    moved = jnp.where((group - to + per) % per == turn, turned, moved)
                for i in range(per):
                    for p in range(self.par):
                        out_ref[(h * per + i) * self.par + p, g : g + 1, :] = moved[i : i + 1, :]


def give(sums, own_ref, sent_ref):
    for p, part in enumerate(sums):
        own_ref[p] = part
        sent_ref[p] = part.astype(sent_ref.dtype)


def first_kernel(share, got_ref, spectra_ref, coef_ref, link_ref, own_ref, sent_ref):
    share = share(got_ref)
    coef_ref[...], link_ref[...] = share.grid()
    spectra = share.spectra()
    spectra_ref[...] = spectra
    give(share.adjoint(spectra), own_ref, sent_ref)


def summed(one_ref, other_ref):
    return [one_ref[x] + other_ref[x].astype(jnp.float32) for x in range(one_ref.shape[0])]


def middle_kernel(
    share, got_ref, one_ref, other_ref, spectra_ref, coef_ref, link_ref, residual_ref, own_ref, sent_ref
):
    share = share(got_ref)
    rest = roll(spectra_ref[...], -share.sensors, 1)
    field = share.smoothed(summed(one_ref, other_ref), coef_ref, link_ref)
    residual = rest - share.forward(field)
    residual_ref[...] = residual
    give(share.adjoint(residual), own_ref, sent_ref)


def last_kernel(share, got_ref, one_ref, other_ref, residual_ref, coef_ref, link_ref, out_ref):
    share = share(got_ref)
    field = share.smoothed(summed(one_ref, other_ref), coef_ref, link_ref)
    share.messages(residual_ref[...], share.forward(field), out_ref)


def home_kernel(got_ref, basis_ref, noise_ref, residual_ref, applied_ref):
    sensors = noise_ref.shape[1]
    rows = residual_ref.shape[0]
    pair = 2 * sensors
    noise = upright(noise_ref[...])
    groups = got_ref.shape[1] // rows
    lines = []
    for r in range(rows):
        parts = []
        for g in range(groups):
            turned = got_ref[:, r * groups + g, :].T
            parts += [turned[i : i + pair, :] for i in range(0, LANES, pair)]
        lines.append(jnp.concatenate(parts, axis=1))
    back = jnp.dot(
        jnp.concatenate(lines, axis=0),
        basis_ref[...],
        precision=lax.Precision.HIGHEST,
        preferred_element_type=jnp.float32,
    )
    for r in range(rows):
        residual = back[r * pair : r * pair + sensors]
        residual_ref[r] = residual
        applied_ref[r] = back[r * pair + sensors : (r + 1) * pair] + noise * residual


def body_fast(vectors, observed, operator, noise, coefficient, offsets):
    top, low, par = (lax.axis_size(axis) for axis in ("top", "low", "par"))
    rows, sensors, length = vectors.shape
    width = coefficient.shape[1]
    shares = low * par
    each = length // 2 // shares
    pair = 2 * sensors
    axes = ("low", "par")
    basis = make_basis(length).reshape(length, 2, shares, each)
    noise = noise[None, :]
    small = (vectors, observed, noise, coefficient, offsets)
    f32 = lambda *shape: jax.ShapeDtypeStruct(shape, jnp.float32)
    room = lambda mib: pltpu.CompilerParams(vmem_limit_bytes=mib * 2**20)

    steps = 2 if shares % 2 == 0 else 1
    tall = each * width // LANES * pair + 2 * each
    operator = operator.reshape(2, shares, each, sensors, width)
    scratch = [
        pltpu.VMEM(array.shape, array.dtype) for array in (operator, *small)
    ]
    message = pl.pallas_call(
        outbound_kernel,
        in_specs=[pl.BlockSpec(memory_space=pl.ANY)] * 7,
        out_specs=pl.BlockSpec(memory_space=pltpu.VMEM),
        out_shape=jax.ShapeDtypeStruct((shares, tall, LANES), jnp.bfloat16),
        scratch_shapes=scratch
        + [
            pltpu.VMEM((length, length), jnp.float32),
            pltpu.SemaphoreType.DMA((6,)),
            pltpu.SemaphoreType.DMA((steps,)),
        ],
        compiler_params=room(50),
        name="outbound",
    )(
        *(
            pltpu.with_memory_space_constraint(x, pltpu.HBM)
            for x in (
                operator,
                *small,
                jnp.asarray(basis.transpose(2, 3, 1, 0).reshape(length, length)),
            )
        )
    )
    got = lax.all_to_all(message, axes, 0, 0, tiled=True).reshape(low, par, tall, LANES)

    def across(sums):
        return lax.ppermute(sums, "top", [(i, (i + 1) % top) for i in range(top)])

    share = functools.partial(Share, rows=rows, each=each, width=width)
    held, lanes = rows * 2 * each, low * pair
    sums = [f32(par, held, width), jax.ShapeDtypeStruct((par, held, width), jnp.bfloat16)]
    grid = [f32(par, width)] * 2
    spectra, coefs, links, one, sent = pl.pallas_call(
        functools.partial(first_kernel, share),
        out_shape=[f32(held, lanes)] + grid + sums,
        compiler_params=room(32),
        name="first_adjoint",
    )(got)
    residual, two, sent_too = pl.pallas_call(
        functools.partial(middle_kernel, share),
        out_shape=[f32(held, lanes)] + sums,
        compiler_params=room(32),
        name="forward_adjoint",
    )(got, one, across(sent), spectra, coefs, links)
    message = pl.pallas_call(
        functools.partial(last_kernel, share),
        out_shape=f32(shares, held * pair // LANES, LANES),
        compiler_params=room(32),
        name="last_forward",
    )(got, two, across(sent_too), residual, coefs, links)
    got = lax.all_to_all(message, axes, 0, 0, tiled=True)
    return pl.pallas_call(
        home_kernel,
        out_shape=[f32(rows, sensors, length)] * 2,
        compiler_params=room(16),
        name="to_time",
    )(got, jnp.asarray(basis.transpose(3, 1, 2, 0).reshape(length, length)), noise)


def fits(mesh, args):
    vectors, _, _, _, coefficient, _ = args
    sen, par = mesh.shape["sen"], mesh.shape["par"]
    rows, sensors, length = vectors.shape
    half, low = length // 2, sen // 2
    if sen % 2 or half % (low * par) or sensors % sen or coefficient.shape[0] != par:
        return False
    each, pair = half // (low * par), 2 * (sensors // sen)
    return (
        pair == 16
        and 3 * rows * pair < LANES
        and each % 8 == 0
        and LANES % (LANES - 3 * rows * pair) == 0
        and 4 * tail_lanes(rows, pair)[1] == 2 * each
        and low * LANES >= coefficient.shape[1]
        and low * pair % LANES == 0
        and coefficient.shape[1] % LANES == 0
    )


def solution(mesh):
    def whole(*args):
        if fits(mesh, args):
            body, sen = body_fast, ("top", "low")
            shape = (2, mesh.shape["sen"] // 2, mesh.shape["par"])
            within = Mesh(mesh.devices.reshape(shape), sen + ("par",))
        else:
            body, sen, within = body_plain, "sen", mesh
        record = P(None, sen, None)
        return jax.shard_map(
            body,
            mesh=within,
            in_specs=(
                record,
                record,
                P(None, None, sen, "par"),
                P(sen),
                P("par", None),
                P("par", None),
            ),
            out_specs=(record, record),
            check_vma=False,
        )(*args)

    return whole
```

```python
import functools
import math

import jax
import jax.numpy as jnp
import numpy as np
from jax import lax
from jax.experimental import pallas as pl
from jax.experimental.pallas import tpu as pltpu
from jax.sharding import Mesh
from jax.sharding import PartitionSpec as P

SWEEPS = 4
REACH = 3
LANES = 128
DEPTH = 256


def make_basis(length):
    half = length // 2
    times = np.arange(length)[:, None]
    freqs = np.arange(half)[None, :]
    phase = (2 * freqs + 1) * times % (2 * length)
    angle = phase.astype(np.float64) * (math.pi / length)
    scale = math.sqrt(2.0 / length)
    return (np.concatenate([np.cos(angle), np.sin(angle)], axis=1) * scale).astype(np.float32)


def halo(field, axis, dim):
    count = lax.axis_size(axis)
    if count == 1:
        edge = jnp.zeros_like(lax.slice_in_dim(field, 0, 1, axis=dim))
        return jnp.concatenate([edge, field, edge], axis=dim)
    ends = count - 1
    head = lax.slice_in_dim(field, 0, 1, axis=dim)
    tail = lax.slice_in_dim(field, field.shape[dim] - 1, field.shape[dim], axis=dim)
    return jnp.concatenate(
        [
            lax.ppermute(tail, axis, [(i, i + 1) for i in range(ends)]),
            field,
            lax.ppermute(head, axis, [(i + 1, i) for i in range(ends)]),
        ],
        axis=dim,
    )


def zero_halo(field):
    return jnp.pad(field, [(0, 0)] * (field.ndim - 2) + [(1, 1), (0, 0)])


def smooth(field, coefficient, offsets, extend):
    width = field.shape[-1]
    lead = [(0, 0)] * (field.ndim - 1)
    for _ in range(SWEEPS):
        padded = extend(field)
        upper = padded[..., :-2, :]
        lower = jnp.pad(padded[..., 2:, :], lead + [(REACH, REACH)])
        linked = jnp.zeros_like(field)
        for shift in range(-REACH, REACH + 1):
            start = REACH + shift
            linked = linked + jnp.where(offsets == shift, lower[..., start : start + width], 0.0)
        sides = jnp.pad(field, lead + [(1, 1)])
        field = field + coefficient * (
            sides[..., :-2] + sides[..., 2:] + upper + linked - 4.0 * field
        )
    return field


def apply_part(spectrum, operator, coefficient, offsets, extend):
    low = spectrum.astype(jnp.bfloat16)

    def adjoint_of(spec, resp):
        return jnp.einsum("frs,fsp->frp", spec, resp, preferred_element_type=jnp.float32)

    def forward_of(par, resp):
        return jnp.einsum("frp,fsp->frs", par, resp, preferred_element_type=jnp.float32)

    real = adjoint_of(low[0], operator[0]) + adjoint_of(low[1], operator[1])
    imag = adjoint_of(low[1], operator[0]) - adjoint_of(low[0], operator[1])
    adjoint = jnp.stack([real, imag])
    grid = adjoint.reshape(adjoint.shape[:3] + coefficient.shape)
    prior = smooth(grid, coefficient, offsets, extend).astype(jnp.bfloat16)
    prior = prior.reshape(adjoint.shape)
    real = forward_of(prior[0], operator[0]) - forward_of(prior[1], operator[1])
    imag = forward_of(prior[1], operator[0]) + forward_of(prior[0], operator[1])
    return jnp.stack([real, imag])


def body_plain(vectors, observed, operator, noise, coefficient, offsets):
    sen, par = lax.axis_size("sen"), lax.axis_size("par")
    rows, sensors, length = vectors.shape
    half = length // 2
    grid_rows, width = coefficient.shape
    basis = jnp.asarray(make_basis(length))
    both = jnp.stack([vectors, observed])
    spectra = jnp.dot(
        both.reshape(2 * rows * sensors, length), basis, precision=lax.Precision.HIGHEST
    )
    spectra = spectra.reshape(2, rows, sensors, 2, half)
    whole_cells = half % (sen * par) == 0
    axes = ("sen", "par") if whole_cells else "sen"
    shares = sen * par if whole_cells else sen
    each = half // shares

    cut = operator.reshape(2, shares, each, sensors, grid_rows, width)
    cut = lax.all_to_all(cut, axes, 1, 1, tiled=True)
    if whole_cells:
        resp = cut.reshape(2, sen, par, each, sensors, grid_rows, width)
        resp = resp.transpose(0, 3, 1, 4, 2, 5, 6)
        resp = resp.reshape(2, each, sen * sensors, par * grid_rows * width)
        coefficient = lax.all_gather(coefficient, "par", tiled=True)
        offsets = lax.all_gather(offsets, "par", tiled=True)
        extend = zero_halo
    else:
        resp = cut.transpose(0, 2, 1, 3, 4, 5)
        resp = resp.reshape(2, each, sen * sensors, grid_rows * width)
        extend = lambda field: halo(field, "par", field.ndim - 2)

    def to_frequencies(spec):
        parts = spec.shape[0]
        cut = spec.reshape(parts, rows, sensors, 2, shares, each)
        cut = lax.all_to_all(cut.transpose(4, 0, 3, 5, 1, 2), axes, 0, 0, tiled=True)
        if whole_cells:
            cut = cut.reshape((sen, par) + cut.shape[1:])[:, 0]
        return cut.transpose(1, 2, 3, 4, 0, 5).reshape(parts, 2, each, rows, sen * sensors)

    def to_sensors(spec):
        parts = spec.shape[0]
        cut = spec.reshape(parts, 2, each, rows, sen, sensors).transpose(4, 0, 3, 5, 1, 2)
        if whole_cells:
            cut = jnp.repeat(cut, par, axis=0)
        cut = lax.all_to_all(cut, axes, 0, 0, tiled=True)
        return cut.transpose(1, 2, 3, 4, 0, 5).reshape(parts, rows, sensors, 2 * half)

    def hessian(spectrum):
        forward = apply_part(spectrum, resp, coefficient, offsets, extend)
        return forward if whole_cells else lax.psum(forward, "par")

    rest = spectra[1] - noise[None, :, None, None] * spectra[0]
    own, rest = to_frequencies(jnp.stack([spectra[0], rest]))
    left = rest - hessian(own)
    again = hessian(left)
    home = to_sensors(jnp.stack([left, again]))
    back = jnp.dot(
        home.reshape(2 * rows * sensors, length), basis.T, precision=lax.Precision.HIGHEST
    ).reshape(2, rows, sensors, length)
    residual = back[0]
    applied = back[1] + noise[None, :, None] * residual
    return (residual, applied)


def roll(x, shift, axis):
    size = x.shape[axis]
    return x if shift % size == 0 else pltpu.roll(x, shift % size, axis)


def iota(shape, axis):
    return lax.broadcasted_iota(jnp.int32, shape, axis)


def upright(line):
    count = line.shape[1]
    square = jnp.broadcast_to(line, (count, count))
    square = jnp.where(iota((count, count), 0) == iota((count, count), 1), square, 0.0)
    return jnp.sum(square, axis=1, keepdims=True)


def split(x):
    high = x.astype(jnp.bfloat16).astype(jnp.float32)
    middle = (x - high).astype(jnp.bfloat16).astype(jnp.float32)
    return high, middle, (x - high - middle).astype(jnp.bfloat16).astype(jnp.float32)


def tail_lanes(rows, pair):
    start = 3 * rows * pair
    return start, LANES // (LANES - start), LANES - start


def outbound_kernel(
    resp_hbm, vectors_hbm, observed_hbm, noise_hbm, coef_hbm, link_hbm, basis_hbm, out_ref,
    resp_ref, vectors_ref, observed_ref, noise_ref, coef_ref, link_ref, basis_ref,
    small_sems, in_sems,
):
    _, devices, each, sensors, width = resp_ref.shape
    pair, lines = 2 * sensors, 2 * each
    tiles = width // LANES
    steps = in_sems.shape[0]
    some = devices // steps
    pieces = [pl.ds(i * some, some) for i in range(steps)]
    small = [
        pltpu.make_async_copy(src, dst, small_sems.at[i])
        for i, (src, dst) in enumerate(
            [
                (basis_hbm, basis_ref),
                (vectors_hbm, vectors_ref),
                (observed_hbm, observed_ref),
                (noise_hbm, noise_ref),
                (coef_hbm, coef_ref),
                (link_hbm, link_ref),
            ]
        )
    ]
    loads = [
        pltpu.make_async_copy(resp_hbm.at[:, piece], resp_ref.at[:, piece], in_sems.at[i])
        for i, piece in enumerate(pieces)
    ]
    body = each * tiles * pair
    for copy in small + loads:
        copy.start()

    for copy in small:
        copy.wait()
    rows = vectors_ref.shape[0]
    noise = upright(noise_ref[...])
    records = []
    for r in range(rows):
        record = vectors_ref[r]
        records += [record, observed_ref[r] - noise * record]
    filled = rows * pair
    records.append(jnp.zeros((LANES - filled, records[0].shape[1]), jnp.float32))
    spectra = lax.dot_general(
        basis_ref[...],
        jnp.concatenate(records, axis=0),
        (((1,), (1,)), ((), ())),
        precision=lax.Precision.HIGHEST,
        preferred_element_type=jnp.float32,
    )
    exact = iota(spectra.shape, 1) // sensors % 2 == 1
    high, middle, low = split(spectra)
    packed = high + roll(jnp.where(exact, middle, 0.0), filled, 1)
    packed = packed + roll(jnp.where(exact, low, 0.0), 2 * filled, 1)

    start, chunks, free = tail_lanes(rows, pair)
    turn = lax.axis_index("low") % tiles
    coefs, links = (
        sum(
            jnp.where(turn == j, ref[:, j * LANES : (j + 1) * LANES].astype(jnp.float32), 0.0)
            for j in range(tiles)
        )
        for ref in (coef_ref, link_ref)
    )
    grid = jnp.concatenate([*split(coefs), links], axis=0)
    grid = jnp.concatenate([roll(grid, start - i * free, 1) for i in range(chunks)], axis=0)
    grid = jnp.where(iota(grid.shape, 1) >= start, grid, 0.0)
    packed = packed.reshape(devices, lines, LANES) + grid[None]
    packed = packed.astype(jnp.bfloat16)
    out_ref[:, pl.ds(body, lines), :] = packed

    for i, piece in enumerate(pieces):
        loads[i].wait()
        for f in range(each):
            for j in range(tiles):
                lanes = pl.ds(j * LANES, LANES)
                both = [resp_ref[c, piece, f, :, lanes] for c in range(2)]
                lane_rows = pl.ds((f * tiles + j) * pair, pair)
                out_ref[piece, lane_rows, :] = jnp.concatenate(both, axis=1)


class Share:
    def __init__(self, got_ref, rows, each, width):
        self.got = got_ref
        self.low, self.par = got_ref.shape[:2]
        self.rows, self.each, self.width = rows, each, width
        self.lines = 2 * each
        self.tiles = width // LANES
        self.pair = (got_ref.shape[2] - self.lines) // (each * self.tiles)
        self.sensors = self.pair // 2
        self.lanes = self.low * self.pair
        self.joint = joint_of(each, self.lanes)
        self.groups = each // self.joint
        self.held = rows * 2 * self.joint
        shape = (self.held, self.lanes)
        row = iota(shape, 0)
        self.real_row = row % 2 == 0
        self.real_lane = iota(shape, 1) // self.sensors % 2 == 0
        self.place = row // 2 % self.joint

    def swapped(self, x):
        return jnp.where(self.real_row, roll(x, -1, 0), roll(x, 1, 0))

    def block(self, group, p):
        return jnp.concatenate(
            [
                jnp.concatenate(
                    [
                        self.got[
                            :, p, pl.ds((f * self.tiles + j) * self.pair, self.pair), :
                        ].reshape(self.lanes, LANES)
                        for j in range(self.tiles)
                    ],
                    axis=1,
                )
                for f in range(group * self.joint, (group + 1) * self.joint)
            ],
            axis=0,
        )

    def spectra(self):
        tail = self.got[:, 0, pl.ds(self.got.shape[2] - self.lines, self.lines), :]
        tail = tail.astype(jnp.float32)
        filled = self.rows * self.pair
        shape = (self.lines, LANES)
        at = iota(shape, 1) // self.pair
        per = LANES // self.pair
        found = [
            [jnp.zeros(shape, jnp.float32) for _ in range(self.lanes // LANES)]
            for _ in range(self.rows)
        ]
        for i in range(self.low):
            packed = tail[i]
            packed = packed + roll(packed, -filled, 1) + roll(packed, -2 * filled, 1)
            h, place = divmod(i, per)
            for r in range(self.rows):
                moved = roll(packed, (place - r) * self.pair, 1)
                found[r][h] = jnp.where(at == place, moved, found[r][h])
        found = [jnp.concatenate(line, axis=1) for line in found]
        few = 2 * self.joint
        return [
            jnp.concatenate([line[g * few : (g + 1) * few] for line in found], axis=0)
            for g in range(self.groups)
        ]

    def grid(self):
        start, chunks, free = tail_lanes(self.rows, self.pair)
        kinds = self.lines // chunks
        chunk = iota((kinds, LANES), 1) // free
        coefs, links = [], []
        for p in range(self.par):
            tail = self.got[
                pl.ds(0, self.tiles), p, pl.ds(self.got.shape[2] - self.lines, self.lines), :
            ].astype(jnp.float32)
            found = []
            for j in range(self.tiles):
                line = jnp.zeros((kinds, LANES), jnp.float32)
                for i in range(chunks):
                    part = roll(tail[j, i * kinds : (i + 1) * kinds], i * free - start, 1)
                    line = jnp.where(chunk == i, part, line)
                found.append(line)
            found = jnp.concatenate(found, axis=1)
            coefs.append(found[0:1] + found[1:2] + found[2:3])
            links.append(found[3:4])
        return jnp.concatenate(coefs, axis=0), jnp.concatenate(links, axis=0)

    def adjoint(self, group, record):
        crossed = self.swapped(record)
        crossed = roll(jnp.where(self.real_row, crossed, -crossed), self.sensors, 1)
        left = jnp.where(self.real_lane, record, crossed)
        left = [jnp.where(self.place == i, left, 0.0) for i in range(self.joint)]
        left = jnp.concatenate(left, axis=1).astype(jnp.bfloat16)
        return [
            jnp.dot(left, self.block(group, p), preferred_element_type=jnp.float32)
            for p in range(self.par)
        ]

    def masks(self, coef_ref, link_ref):
        shape = (self.held, self.width)
        column = iota((1, self.width), 1)
        wide = lambda mask: jnp.broadcast_to(jnp.where(mask, 1.0, 0.0), shape)
        coefs, links = [], []
        for x in range(self.par):
            coefs.append(jnp.broadcast_to(coef_ref[x : x + 1, :], shape))
            offset = link_ref[x : x + 1, :]
            links.append(
                [
                    wide((offset == float(k)) & (column + k >= 0) & (column + k < self.width))
                    for k in range(-REACH, REACH + 1)
                ]
            )
        return coefs, links, wide(column > 0), wide(column < self.width - 1)

    def smoothed(self, field, masks):
        coefs, links, after_first, before_last = masks
        for _ in range(SWEEPS):
            after = []
            for x, u in enumerate(field):
                around = roll(u, 1, 1) * after_first + roll(u, -1, 1) * before_last
                if x > 0:
                    around += field[x - 1]
                if x < self.par - 1:
                    linked = jnp.zeros(u.shape, jnp.float32)
                    for mask, shift in zip(links[x], range(-REACH, REACH + 1)):
                        linked += mask * roll(field[x + 1], -shift, 1)
                    around += linked
                after.append(u + coefs[x] * (around - 4.0 * u))
            field = after
        return field

    def forward(self, group, field):
        part = jnp.zeros((self.held, self.joint * self.lanes), jnp.float32)
        for p in range(self.par):
            part += lax.dot_general(
                field[p].astype(jnp.bfloat16),
                self.block(group, p),
                (((1,), (1,)), ((), ())),
                preferred_element_type=jnp.float32,
            )
        out = part[:, : self.lanes]
        for i in range(1, self.joint):
            out = jnp.where(self.place == i, part[:, i * self.lanes : (i + 1) * self.lanes], out)
        crossed = self.swapped(roll(out, -self.sensors, 1))
        return out + jnp.where(self.real_row, -crossed, crossed)

    def message(self, group, residual, applied, out_ref):
        both = jnp.where(self.real_lane, residual, roll(applied, self.sensors, 1))
        per = self.held
        to, lane_group = iota((per, LANES), 0), iota((per, LANES), 1) // self.pair
        for h in range(self.lanes // LANES):
            tile = both[:, h * LANES : (h + 1) * LANES]
            moved = tile
            for turn in range(1, per):
                turned = roll(roll(tile, -turn, 0), turn * self.pair, 1)
                moved = jnp.where((lane_group - to + per) % per == turn, turned, moved)
            for i in range(per):
                for p in range(self.par):
                    place = (h * per + i) * self.par + p
                    out_ref[place, group : group + 1, :] = moved[i : i + 1, :]

    def rows_of(self, group):
        return pl.ds(group * self.held, self.held)

    def give(self, sums, own_ref, sent_ref):
        for p in range(self.par):
            part = jnp.concatenate([line[p] for line in sums], axis=0)
            own_ref[p] = part
            sent_ref[p] = part.astype(sent_ref.dtype)

    def summed(self, own_ref, other_ref):
        whole = [own_ref[p] + other_ref[p].astype(jnp.float32) for p in range(self.par)]
        return [
            [part[g * self.held : (g + 1) * self.held] for part in whole]
            for g in range(self.groups)
        ]


def joint_of(each, lanes):
    return max(1, min(each, DEPTH // lanes))


def first_kernel(share, got_ref, spectra_ref, coef_ref, link_ref, own_ref, sent_ref):
    share = share(got_ref)
    coef_ref[...], link_ref[...] = share.grid()
    sums = []
    for g, spectra in enumerate(share.spectra()):
        spectra_ref[share.rows_of(g), :] = spectra
        sums.append(share.adjoint(g, spectra))
    share.give(sums, own_ref, sent_ref)


def middle_kernel(
    share, got_ref, one_ref, other_ref, spectra_ref, coef_ref, link_ref, residual_ref, own_ref, sent_ref
):
    share = share(got_ref)
    masks = share.masks(coef_ref, link_ref)
    residuals = []
    for g, field in enumerate(share.summed(one_ref, other_ref)):
        rest = roll(spectra_ref[share.rows_of(g), :], -share.sensors, 1)
        residuals.append(rest - share.forward(g, share.smoothed(field, masks)))
        residual_ref[share.rows_of(g), :] = residuals[g]
    share.give([share.adjoint(g, x) for g, x in enumerate(residuals)], own_ref, sent_ref)


def last_kernel(share, got_ref, one_ref, other_ref, residual_ref, coef_ref, link_ref, out_ref):
    share = share(got_ref)
    masks = share.masks(coef_ref, link_ref)
    for g, field in enumerate(share.summed(one_ref, other_ref)):
        applied = share.forward(g, share.smoothed(field, masks))
        share.message(g, residual_ref[share.rows_of(g), :], applied, out_ref)


def home_kernel(got_ref, basis_ref, noise_ref, residual_ref, applied_ref):
    sensors = noise_ref.shape[1]
    rows = residual_ref.shape[0]
    pair = 2 * sensors
    noise = upright(noise_ref[...])
    lines = [[] for _ in range(rows)]
    for g in range(got_ref.shape[1]):
        turned = got_ref[:, g, :].T
        for r in range(rows):
            first, last = r * LANES // rows, (r + 1) * LANES // rows
            lines[r] += [turned[i : i + pair, :] for i in range(first, last, pair)]
    back = jnp.dot(
        jnp.concatenate([jnp.concatenate(line, axis=1) for line in lines], axis=0),
        basis_ref[...],
        precision=lax.Precision.HIGHEST,
        preferred_element_type=jnp.float32,
    )
    for r in range(rows):
        residual = back[r * pair : r * pair + sensors]
        residual_ref[r] = residual
        applied_ref[r] = back[r * pair + sensors : (r + 1) * pair] + noise * residual


def body_fast(vectors, observed, operator, noise, coefficient, offsets):
    top, low, par = (lax.axis_size(axis) for axis in ("top", "low", "par"))
    rows, sensors, length = vectors.shape
    width = coefficient.shape[1]
    shares = low * par
    each = length // 2 // shares
    pair = 2 * sensors
    axes = ("low", "par")
    basis = make_basis(length).reshape(length, 2, shares, each)
    noise = noise[None, :]
    small = (vectors, observed, noise, coefficient, offsets)
    f32 = lambda *shape: jax.ShapeDtypeStruct(shape, jnp.float32)
    room = lambda mib: pltpu.CompilerParams(vmem_limit_bytes=mib * 2**20)

    steps = 2 if shares % 2 == 0 else 1
    tall = each * width // LANES * pair + 2 * each
    operator = operator.reshape(2, shares, each, sensors, width)
    scratch = [
        pltpu.VMEM(array.shape, array.dtype) for array in (operator, *small)
    ]
    message = pl.pallas_call(
        outbound_kernel,
        in_specs=[pl.BlockSpec(memory_space=pl.ANY)] * 7,
        out_specs=pl.BlockSpec(memory_space=pltpu.VMEM),
        out_shape=jax.ShapeDtypeStruct((shares, tall, LANES), jnp.bfloat16),
        scratch_shapes=scratch
        + [
            pltpu.VMEM((length, length), jnp.float32),
            pltpu.SemaphoreType.DMA((6,)),
            pltpu.SemaphoreType.DMA((steps,)),
        ],
        compiler_params=room(50),
        name="outbound",
    )(
        *(
            pltpu.with_memory_space_constraint(x, pltpu.HBM)
            for x in (
                operator,
                *small,
                jnp.asarray(basis.transpose(2, 3, 1, 0).reshape(length, length)),
            )
        )
    )
    got = lax.all_to_all(message, axes, 0, 0, tiled=True).reshape(low, par, tall, LANES)

    def across(sums):
        return lax.ppermute(sums, "top", [(i, (i + 1) % top) for i in range(top)])

    share = functools.partial(Share, rows=rows, each=each, width=width)
    held, lanes = rows * 2 * each, low * pair
    sums = [f32(par, held, width), jax.ShapeDtypeStruct((par, held, width), jnp.bfloat16)]
    grid = [f32(par, width)] * 2
    spectra, coefs, links, one, sent = pl.pallas_call(
        functools.partial(first_kernel, share),
        out_shape=[f32(held, lanes)] + grid + sums,
        compiler_params=room(32),
        name="first_adjoint",
    )(got)
    residual, two, sent_too = pl.pallas_call(
        functools.partial(middle_kernel, share),
        out_shape=[f32(held, lanes)] + sums,
        compiler_params=room(32),
        name="forward_adjoint",
    )(got, one, across(sent), spectra, coefs, links)
    message = pl.pallas_call(
        functools.partial(last_kernel, share),
        out_shape=f32(shares, each // joint_of(each, lanes), LANES),
        compiler_params=room(32),
        name="last_forward",
    )(got, two, across(sent_too), residual, coefs, links)
    got = lax.all_to_all(message, axes, 0, 0, tiled=True)
    return pl.pallas_call(
        home_kernel,
        out_shape=[f32(rows, sensors, length)] * 2,
        compiler_params=room(16),
        name="to_time",
    )(got, jnp.asarray(basis.transpose(3, 1, 2, 0).reshape(length, length)), noise)


def fits(mesh, args):
    vectors, _, _, _, coefficient, _ = args
    sen, par = mesh.shape["sen"], mesh.shape["par"]
    rows, sensors, length = vectors.shape
    half, low = length // 2, sen // 2
    if sen % 2 or half % (low * par) or sensors % sen or coefficient.shape[0] != par:
        return False
    each, pair = half // (low * par), 2 * (sensors // sen)
    return (
        2 * rows * joint_of(each, low * pair) * pair == LANES
        and 3 * rows * pair < LANES
        and each % joint_of(each, low * pair) == 0
        and LANES % (LANES - 3 * rows * pair) == 0
        and 4 * tail_lanes(rows, pair)[1] == 2 * each
        and low * LANES >= coefficient.shape[1]
        and pair == 16
        and low * pair % LANES == 0
        and coefficient.shape[1] % LANES == 0
    )


def solution(mesh):
    def whole(*args):
        if fits(mesh, args):
            body, sen = body_fast, ("top", "low")
            shape = (2, mesh.shape["sen"] // 2, mesh.shape["par"])
            within = Mesh(mesh.devices.reshape(shape), sen + ("par",))
        else:
            body, sen, within = body_plain, "sen", mesh
        record = P(None, sen, None)
        return jax.shard_map(
            body,
            mesh=within,
            in_specs=(
                record,
                record,
                P(None, None, sen, "par"),
                P(sen),
                P("par", None),
                P("par", None),
            ),
            out_specs=(record, record),
            check_vma=False,
        )(*args)

    return whole
```

```python
import functools
import math

import jax
import jax.numpy as jnp
import numpy as np
from jax import lax
from jax.experimental import pallas as pl
from jax.experimental.pallas import tpu as pltpu
from jax.sharding import Mesh
from jax.sharding import PartitionSpec as P

SWEEPS = 4
REACH = 3
LANES = 128
DEPTH = 256


def make_basis(length):
    half = length // 2
    times = np.arange(length)[:, None]
    freqs = np.arange(half)[None, :]
    phase = (2 * freqs + 1) * times % (2 * length)
    angle = phase.astype(np.float64) * (math.pi / length)
    scale = math.sqrt(2.0 / length)
    return (np.concatenate([np.cos(angle), np.sin(angle)], axis=1) * scale).astype(np.float32)


def halo(field, axis, dim):
    count = lax.axis_size(axis)
    if count == 1:
        edge = jnp.zeros_like(lax.slice_in_dim(field, 0, 1, axis=dim))
        return jnp.concatenate([edge, field, edge], axis=dim)
    ends = count - 1
    head = lax.slice_in_dim(field, 0, 1, axis=dim)
    tail = lax.slice_in_dim(field, field.shape[dim] - 1, field.shape[dim], axis=dim)
    return jnp.concatenate(
        [
            lax.ppermute(tail, axis, [(i, i + 1) for i in range(ends)]),
            field,
            lax.ppermute(head, axis, [(i + 1, i) for i in range(ends)]),
        ],
        axis=dim,
    )


def zero_halo(field):
    return jnp.pad(field, [(0, 0)] * (field.ndim - 2) + [(1, 1), (0, 0)])


def smooth(field, coefficient, offsets, extend):
    width = field.shape[-1]
    lead = [(0, 0)] * (field.ndim - 1)
    for _ in range(SWEEPS):
        padded = extend(field)
        upper = padded[..., :-2, :]
        lower = jnp.pad(padded[..., 2:, :], lead + [(REACH, REACH)])
        linked = jnp.zeros_like(field)
        for shift in range(-REACH, REACH + 1):
            start = REACH + shift
            linked = linked + jnp.where(offsets == shift, lower[..., start : start + width], 0.0)
        sides = jnp.pad(field, lead + [(1, 1)])
        field = field + coefficient * (
            sides[..., :-2] + sides[..., 2:] + upper + linked - 4.0 * field
        )
    return field


def apply_part(spectrum, operator, coefficient, offsets, extend):
    low = spectrum.astype(jnp.bfloat16)

    def adjoint_of(spec, resp):
        return jnp.einsum("frs,fsp->frp", spec, resp, preferred_element_type=jnp.float32)

    def forward_of(par, resp):
        return jnp.einsum("frp,fsp->frs", par, resp, preferred_element_type=jnp.float32)

    real = adjoint_of(low[0], operator[0]) + adjoint_of(low[1], operator[1])
    imag = adjoint_of(low[1], operator[0]) - adjoint_of(low[0], operator[1])
    adjoint = jnp.stack([real, imag])
    grid = adjoint.reshape(adjoint.shape[:3] + coefficient.shape)
    prior = smooth(grid, coefficient, offsets, extend).astype(jnp.bfloat16)
    prior = prior.reshape(adjoint.shape)
    real = forward_of(prior[0], operator[0]) - forward_of(prior[1], operator[1])
    imag = forward_of(prior[1], operator[0]) + forward_of(prior[0], operator[1])
    return jnp.stack([real, imag])


def body_plain(vectors, observed, operator, noise, coefficient, offsets):
    sen, par = lax.axis_size("sen"), lax.axis_size("par")
    rows, sensors, length = vectors.shape
    half = length // 2
    grid_rows, width = coefficient.shape
    basis = jnp.asarray(make_basis(length))
    both = jnp.stack([vectors, observed])
    spectra = jnp.dot(
        both.reshape(2 * rows * sensors, length), basis, precision=lax.Precision.HIGHEST
    )
    spectra = spectra.reshape(2, rows, sensors, 2, half)
    whole_cells = half % (sen * par) == 0
    axes = ("sen", "par") if whole_cells else "sen"
    shares = sen * par if whole_cells else sen
    each = half // shares

    cut = operator.reshape(2, shares, each, sensors, grid_rows, width)
    cut = lax.all_to_all(cut, axes, 1, 1, tiled=True)
    if whole_cells:
        resp = cut.reshape(2, sen, par, each, sensors, grid_rows, width)
        resp = resp.transpose(0, 3, 1, 4, 2, 5, 6)
        resp = resp.reshape(2, each, sen * sensors, par * grid_rows * width)
        coefficient = lax.all_gather(coefficient, "par", tiled=True)
        offsets = lax.all_gather(offsets, "par", tiled=True)
        extend = zero_halo
    else:
        resp = cut.transpose(0, 2, 1, 3, 4, 5)
        resp = resp.reshape(2, each, sen * sensors, grid_rows * width)
        extend = lambda field: halo(field, "par", field.ndim - 2)

    def to_frequencies(spec):
        parts = spec.shape[0]
        cut = spec.reshape(parts, rows, sensors, 2, shares, each)
        cut = lax.all_to_all(cut.transpose(4, 0, 3, 5, 1, 2), axes, 0, 0, tiled=True)
        if whole_cells:
            cut = cut.reshape((sen, par) + cut.shape[1:])[:, 0]
        return cut.transpose(1, 2, 3, 4, 0, 5).reshape(parts, 2, each, rows, sen * sensors)

    def to_sensors(spec):
        parts = spec.shape[0]
        cut = spec.reshape(parts, 2, each, rows, sen, sensors).transpose(4, 0, 3, 5, 1, 2)
        if whole_cells:
            cut = jnp.repeat(cut, par, axis=0)
        cut = lax.all_to_all(cut, axes, 0, 0, tiled=True)
        return cut.transpose(1, 2, 3, 4, 0, 5).reshape(parts, rows, sensors, 2 * half)

    def hessian(spectrum):
        forward = apply_part(spectrum, resp, coefficient, offsets, extend)
        return forward if whole_cells else lax.psum(forward, "par")

    rest = spectra[1] - noise[None, :, None, None] * spectra[0]
    own, rest = to_frequencies(jnp.stack([spectra[0], rest]))
    left = rest - hessian(own)
    again = hessian(left)
    home = to_sensors(jnp.stack([left, again]))
    back = jnp.dot(
        home.reshape(2 * rows * sensors, length), basis.T, precision=lax.Precision.HIGHEST
    ).reshape(2, rows, sensors, length)
    residual = back[0]
    applied = back[1] + noise[None, :, None] * residual
    return (residual, applied)


def roll(x, shift, axis):
    size = x.shape[axis]
    return x if shift % size == 0 else pltpu.roll(x, shift % size, axis)


def iota(shape, axis):
    return lax.broadcasted_iota(jnp.int32, shape, axis)


def upright(line):
    count = line.shape[1]
    square = jnp.broadcast_to(line, (count, count))
    square = jnp.where(iota((count, count), 0) == iota((count, count), 1), square, 0.0)
    return jnp.sum(square, axis=1, keepdims=True)


def split(x):
    high = x.astype(jnp.bfloat16).astype(jnp.float32)
    middle = (x - high).astype(jnp.bfloat16).astype(jnp.float32)
    return high, middle, (x - high - middle).astype(jnp.bfloat16).astype(jnp.float32)


def tail_lanes(rows, pair):
    start = 3 * rows * pair
    return start, LANES // (LANES - start), LANES - start


def outbound_kernel(
    resp_hbm, vectors_hbm, observed_hbm, noise_hbm, coef_hbm, link_hbm, basis_hbm, out_ref,
    resp_ref, vectors_ref, observed_ref, noise_ref, coef_ref, link_ref, basis_ref,
    small_sems, in_sems,
):
    _, devices, each, sensors, width = resp_ref.shape
    pair, lines = 2 * sensors, 2 * each
    tiles = width // LANES
    steps = in_sems.shape[0]
    some = devices // steps
    pieces = [pl.ds(i * some, some) for i in range(steps)]
    small = [
        pltpu.make_async_copy(src, dst, small_sems.at[i])
        for i, (src, dst) in enumerate(
            [
                (basis_hbm, basis_ref),
                (vectors_hbm, vectors_ref),
                (observed_hbm, observed_ref),
                (noise_hbm, noise_ref),
                (coef_hbm, coef_ref),
                (link_hbm, link_ref),
            ]
        )
    ]
    loads = [
        pltpu.make_async_copy(resp_hbm.at[:, piece], resp_ref.at[:, piece], in_sems.at[i])
        for i, piece in enumerate(pieces)
    ]
    body = each * tiles * pair
    for copy in small + loads:
        copy.start()

    for copy in small:
        copy.wait()
    rows = vectors_ref.shape[0]
    noise = upright(noise_ref[...])
    records = []
    for r in range(rows):
        record = vectors_ref[r]
        records += [record, observed_ref[r] - noise * record]
    filled = rows * pair
    records.append(jnp.zeros((LANES - filled, records[0].shape[1]), jnp.float32))
    spectra = lax.dot_general(
        basis_ref[...],
        jnp.concatenate(records, axis=0),
        (((1,), (1,)), ((), ())),
        precision=lax.Precision.HIGHEST,
        preferred_element_type=jnp.float32,
    )
    exact = iota(spectra.shape, 1) // sensors % 2 == 1
    high, middle, low = split(spectra)
    packed = high + roll(jnp.where(exact, middle, 0.0), filled, 1)
    packed = packed + roll(jnp.where(exact, low, 0.0), 2 * filled, 1)

    start, chunks, free = tail_lanes(rows, pair)
    turn = lax.axis_index("low") % tiles
    coefs, links = (
        sum(
            jnp.where(turn == j, ref[:, j * LANES : (j + 1) * LANES].astype(jnp.float32), 0.0)
            for j in range(tiles)
        )
        for ref in (coef_ref, link_ref)
    )
    grid = jnp.concatenate([*split(coefs), links], axis=0)
    grid = jnp.concatenate([roll(grid, start - i * free, 1) for i in range(chunks)], axis=0)
    grid = jnp.where(iota(grid.shape, 1) >= start, grid, 0.0)
    packed = packed.reshape(devices, lines, LANES) + grid[None]
    packed = packed.astype(jnp.bfloat16)
    out_ref[:, pl.ds(body, lines), :] = packed

    for i, piece in enumerate(pieces):
        loads[i].wait()
        for f in range(each):
            for j in range(tiles):
                lanes = pl.ds(j * LANES, LANES)
                both = [resp_ref[c, piece, f, :, lanes] for c in range(2)]
                lane_rows = pl.ds((f * tiles + j) * pair, pair)
                out_ref[piece, lane_rows, :] = jnp.concatenate(both, axis=1)


class Share:
    def __init__(self, got_ref, rows, each, width):
        self.got = got_ref
        self.low, self.par = got_ref.shape[:2]
        self.rows, self.each, self.width = rows, each, width
        self.lines = 2 * each
        self.tiles = width // LANES
        self.pair = (got_ref.shape[2] - self.lines) // (each * self.tiles)
        self.sensors = self.pair // 2
        self.lanes = self.low * self.pair
        self.joint = joint_of(each, self.lanes)
        self.groups = each // self.joint
        self.held = rows * 2 * self.joint
        shape = (self.held, self.lanes)
        row = iota(shape, 0)
        self.real_row = row % 2 == 0
        self.real_lane = iota(shape, 1) // self.sensors % 2 == 0
        self.place = row // 2 % self.joint

    def swapped(self, x):
        return jnp.where(self.real_row, roll(x, -1, 0), roll(x, 1, 0))

    def block(self, group, p):
        return jnp.concatenate(
            [
                jnp.concatenate(
                    [
                        self.got[
                            :, p, pl.ds((f * self.tiles + j) * self.pair, self.pair), :
                        ].reshape(self.lanes, LANES)
                        for j in range(self.tiles)
                    ],
                    axis=1,
                )
                for f in range(group * self.joint, (group + 1) * self.joint)
            ],
            axis=0,
        )

    def spectra(self):
        tail = self.got[:, 0, pl.ds(self.got.shape[2] - self.lines, self.lines), :]
        tail = tail.astype(jnp.float32)
        filled = self.rows * self.pair
        shape = (self.lines, LANES)
        at = iota(shape, 1) // self.pair
        per = LANES // self.pair
        found = [
            [jnp.zeros(shape, jnp.float32) for _ in range(self.lanes // LANES)]
            for _ in range(self.rows)
        ]
        for i in range(self.low):
            packed = tail[i]
            packed = packed + roll(packed, -filled, 1) + roll(packed, -2 * filled, 1)
            h, place = divmod(i, per)
            for r in range(self.rows):
                moved = roll(packed, (place - r) * self.pair, 1)
                found[r][h] = jnp.where(at == place, moved, found[r][h])
        found = [jnp.concatenate(line, axis=1) for line in found]
        few = 2 * self.joint
        return [
            jnp.concatenate([line[g * few : (g + 1) * few] for line in found], axis=0)
            for g in range(self.groups)
        ]

    def grid(self):
        start, chunks, free = tail_lanes(self.rows, self.pair)
        kinds = self.lines // chunks
        chunk = iota((kinds, LANES), 1) // free
        coefs, links = [], []
        for p in range(self.par):
            tail = self.got[
                pl.ds(0, self.tiles), p, pl.ds(self.got.shape[2] - self.lines, self.lines), :
            ].astype(jnp.float32)
            found = []
            for j in range(self.tiles):
                line = jnp.zeros((kinds, LANES), jnp.float32)
                for i in range(chunks):
                    part = roll(tail[j, i * kinds : (i + 1) * kinds], i * free - start, 1)
                    line = jnp.where(chunk == i, part, line)
                found.append(line)
            found = jnp.concatenate(found, axis=1)
            coefs.append(found[0:1] + found[1:2] + found[2:3])
            links.append(found[3:4])
        return jnp.concatenate(coefs, axis=0), jnp.concatenate(links, axis=0)

    def adjoint(self, group, record):
        crossed = self.swapped(record)
        crossed = roll(jnp.where(self.real_row, crossed, -crossed), self.sensors, 1)
        left = jnp.where(self.real_lane, record, crossed)
        left = [jnp.where(self.place == i, left, 0.0) for i in range(self.joint)]
        left = jnp.concatenate(left, axis=1).astype(jnp.bfloat16)
        return [
            jnp.dot(left, self.block(group, p), preferred_element_type=jnp.float32)
            for p in range(self.par)
        ]

    def masks(self, coef_ref, link_ref):
        shape = (self.held, self.width)
        column = iota((1, self.width), 1)
        wide = lambda mask: jnp.broadcast_to(jnp.where(mask, 1.0, 0.0), shape)
        coefs, links = [], []
        for x in range(self.par):
            coefs.append(jnp.broadcast_to(coef_ref[x : x + 1, :], shape))
            offset = link_ref[x : x + 1, :]
            links.append(
                [
                    wide((offset == float(k)) & (column + k >= 0) & (column + k < self.width))
                    for k in range(-REACH, REACH + 1)
                ]
            )
        return coefs, links, wide(column > 0), wide(column < self.width - 1)

    def smoothed(self, field, masks):
        coefs, links, after_first, before_last = masks
        for _ in range(SWEEPS):
            after = []
            for x, u in enumerate(field):
                around = roll(u, 1, 1) * after_first + roll(u, -1, 1) * before_last
                if x > 0:
                    around += field[x - 1]
                if x < self.par - 1:
                    linked = jnp.zeros(u.shape, jnp.float32)
                    for mask, shift in zip(links[x], range(-REACH, REACH + 1)):
                        linked += mask * roll(field[x + 1], -shift, 1)
                    around += linked
                after.append(u + coefs[x] * (around - 4.0 * u))
            field = after
        return field

    def forward(self, group, field):
        part = jnp.zeros((self.held, self.joint * self.lanes), jnp.float32)
        for p in range(self.par):
            part += lax.dot_general(
                field[p].astype(jnp.bfloat16),
                self.block(group, p),
                (((1,), (1,)), ((), ())),
                preferred_element_type=jnp.float32,
            )
        out = part[:, : self.lanes]
        for i in range(1, self.joint):
            out = jnp.where(self.place == i, part[:, i * self.lanes : (i + 1) * self.lanes], out)
        crossed = self.swapped(roll(out, -self.sensors, 1))
        return out + jnp.where(self.real_row, -crossed, crossed)

    def message(self, group, residual, applied, out_ref):
        both = jnp.where(self.real_lane, residual, roll(applied, self.sensors, 1))
        per = self.held
        to, lane_group = iota((per, LANES), 0), iota((per, LANES), 1) // self.pair
        for h in range(self.lanes // LANES):
            tile = both[:, h * LANES : (h + 1) * LANES]
            moved = tile
            for turn in range(1, per):
                turned = roll(roll(tile, -turn, 0), turn * self.pair, 1)
                moved = jnp.where((lane_group - to + per) % per == turn, turned, moved)
            for i in range(per):
                for p in range(self.par):
                    place = (h * per + i) * self.par + p
                    out_ref[place, group : group + 1, :] = moved[i : i + 1, :]

    def rows_of(self, group):
        return pl.ds(group * self.held, self.held)

    def give(self, sums, *refs):
        for p in range(self.par):
            part = jnp.concatenate([line[p] for line in sums], axis=0)
            for ref in refs:
                ref[p] = part.astype(ref.dtype)

    def summed(self, own_ref, other_ref):
        whole = [own_ref[p] + other_ref[p].astype(jnp.float32) for p in range(self.par)]
        return [
            [part[g * self.held : (g + 1) * self.held] for part in whole]
            for g in range(self.groups)
        ]


def joint_of(each, lanes):
    return max(1, min(each, DEPTH // lanes))


def first_kernel(share, got_ref, spectra_ref, coef_ref, link_ref, own_ref):
    share = share(got_ref)
    coef_ref[...], link_ref[...] = share.grid()
    sums = []
    for g, spectra in enumerate(share.spectra()):
        spectra_ref[share.rows_of(g), :] = spectra
        sums.append(share.adjoint(g, spectra))
    share.give(sums, own_ref)


def middle_kernel(
    share, got_ref, one_ref, other_ref, spectra_ref, coef_ref, link_ref, residual_ref, own_ref, sent_ref
):
    share = share(got_ref)
    masks = share.masks(coef_ref, link_ref)
    residuals = []
    for g, field in enumerate(share.summed(one_ref, other_ref)):
        rest = roll(spectra_ref[share.rows_of(g), :], -share.sensors, 1)
        residuals.append(rest - share.forward(g, share.smoothed(field, masks)))
        residual_ref[share.rows_of(g), :] = residuals[g]
    share.give([share.adjoint(g, x) for g, x in enumerate(residuals)], own_ref, sent_ref)


def last_kernel(share, got_ref, one_ref, other_ref, residual_ref, coef_ref, link_ref, out_ref):
    share = share(got_ref)
    masks = share.masks(coef_ref, link_ref)
    for g, field in enumerate(share.summed(one_ref, other_ref)):
        applied = share.forward(g, share.smoothed(field, masks))
        share.message(g, residual_ref[share.rows_of(g), :], applied, out_ref)


def home_kernel(got_ref, basis_ref, noise_ref, residual_ref, applied_ref):
    sensors = noise_ref.shape[1]
    rows = residual_ref.shape[0]
    pair = 2 * sensors
    noise = upright(noise_ref[...])
    lines = [[] for _ in range(rows)]
    for g in range(got_ref.shape[1]):
        turned = got_ref[:, g, :].T
        for r in range(rows):
            first, last = r * LANES // rows, (r + 1) * LANES // rows
            lines[r] += [turned[i : i + pair, :] for i in range(first, last, pair)]
    back = jnp.dot(
        jnp.concatenate([jnp.concatenate(line, axis=1) for line in lines], axis=0),
        basis_ref[...],
        precision=lax.Precision.HIGHEST,
        preferred_element_type=jnp.float32,
    )
    for r in range(rows):
        residual = back[r * pair : r * pair + sensors]
        residual_ref[r] = residual
        applied_ref[r] = back[r * pair + sensors : (r + 1) * pair] + noise * residual


def body_fast(vectors, observed, operator, noise, coefficient, offsets):
    top, low, par = (lax.axis_size(axis) for axis in ("top", "low", "par"))
    rows, sensors, length = vectors.shape
    width = coefficient.shape[1]
    shares = low * par
    each = length // 2 // shares
    pair = 2 * sensors
    axes = ("low", "par")
    basis = make_basis(length).reshape(length, 2, shares, each)
    noise = noise[None, :]
    small = (vectors, observed, noise, coefficient, offsets)
    f32 = lambda *shape: jax.ShapeDtypeStruct(shape, jnp.float32)
    room = lambda mib: pltpu.CompilerParams(vmem_limit_bytes=mib * 2**20)

    steps = 2 if shares % 2 == 0 else 1
    tall = each * width // LANES * pair + 2 * each
    operator = operator.reshape(2, shares, each, sensors, width)
    scratch = [
        pltpu.VMEM(array.shape, array.dtype) for array in (operator, *small)
    ]
    message = pl.pallas_call(
        outbound_kernel,
        in_specs=[pl.BlockSpec(memory_space=pl.ANY)] * 7,
        out_specs=pl.BlockSpec(memory_space=pltpu.VMEM),
        out_shape=jax.ShapeDtypeStruct((shares, tall, LANES), jnp.bfloat16),
        scratch_shapes=scratch
        + [
            pltpu.VMEM((length, length), jnp.float32),
            pltpu.SemaphoreType.DMA((6,)),
            pltpu.SemaphoreType.DMA((steps,)),
        ],
        compiler_params=room(50),
        name="outbound",
    )(
        *(
            pltpu.with_memory_space_constraint(x, pltpu.HBM)
            for x in (
                operator,
                *small,
                jnp.asarray(basis.transpose(2, 3, 1, 0).reshape(length, length)),
            )
        )
    )
    got = lax.all_to_all(message, axes, 0, 0, tiled=True).reshape(low, par, tall, LANES)

    def across(sums):
        return lax.ppermute(sums, "top", [(i, (i + 1) % top) for i in range(top)])

    share = functools.partial(Share, rows=rows, each=each, width=width)
    held, lanes = rows * 2 * each, low * pair
    sums = f32(par, held, width)
    rounded = jax.ShapeDtypeStruct(sums.shape, jnp.bfloat16)
    grid = [f32(par, width)] * 2
    spectra, coefs, links, one = pl.pallas_call(
        functools.partial(first_kernel, share),
        out_shape=[f32(held, lanes)] + grid + [sums],
        compiler_params=room(32),
        name="first_adjoint",
    )(got)
    residual, two, sent = pl.pallas_call(
        functools.partial(middle_kernel, share),
        out_shape=[f32(held, lanes), sums, rounded],
        compiler_params=room(32),
        name="forward_adjoint",
    )(got, one, across(one), spectra, coefs, links)
    message = pl.pallas_call(
        functools.partial(last_kernel, share),
        out_shape=f32(shares, each // joint_of(each, lanes), LANES),
        compiler_params=room(32),
        name="last_forward",
    )(got, two, across(sent), residual, coefs, links)
    got = lax.all_to_all(message, axes, 0, 0, tiled=True)
    return pl.pallas_call(
        home_kernel,
        out_shape=[f32(rows, sensors, length)] * 2,
        compiler_params=room(16),
        name="to_time",
    )(got, jnp.asarray(basis.transpose(3, 1, 2, 0).reshape(length, length)), noise)


def fits(mesh, args):
    vectors, _, _, _, coefficient, _ = args
    sen, par = mesh.shape["sen"], mesh.shape["par"]
    rows, sensors, length = vectors.shape
    half, low = length // 2, sen // 2
    if sen % 2 or half % (low * par) or sensors % sen or coefficient.shape[0] != par:
        return False
    each, pair = half // (low * par), 2 * (sensors // sen)
    return (
        2 * rows * joint_of(each, low * pair) * pair == LANES
        and 3 * rows * pair < LANES
        and each % joint_of(each, low * pair) == 0
        and LANES % (LANES - 3 * rows * pair) == 0
        and 4 * tail_lanes(rows, pair)[1] == 2 * each
        and low * LANES >= coefficient.shape[1]
        and pair == 16
        and low * pair % LANES == 0
        and coefficient.shape[1] % LANES == 0
    )


def solution(mesh):
    def whole(*args):
        if fits(mesh, args):
            body, sen = body_fast, ("top", "low")
            shape = (2, mesh.shape["sen"] // 2, mesh.shape["par"])
            within = Mesh(mesh.devices.reshape(shape), sen + ("par",))
        else:
            body, sen, within = body_plain, "sen", mesh
        record = P(None, sen, None)
        return jax.shard_map(
            body,
            mesh=within,
            in_specs=(
                record,
                record,
                P(None, None, sen, "par"),
                P(sen),
                P("par", None),
                P("par", None),
            ),
            out_specs=(record, record),
            check_vma=False,
        )(*args)

    return whole
```

```python
import functools
import math

import jax
import jax.numpy as jnp
import numpy as np
from jax import lax
from jax.experimental import pallas as pl
from jax.experimental.pallas import tpu as pltpu
from jax.sharding import Mesh
from jax.sharding import PartitionSpec as P

SWEEPS = 4
REACH = 3
LANES = 128
DEPTH = 256
KINDS = 4


def make_basis(length):
    half = length // 2
    times = np.arange(length)[:, None]
    freqs = np.arange(half)[None, :]
    phase = (2 * freqs + 1) * times % (2 * length)
    angle = phase.astype(np.float64) * (math.pi / length)
    scale = math.sqrt(2.0 / length)
    return (np.concatenate([np.cos(angle), np.sin(angle)], axis=1) * scale).astype(np.float32)


def halo(field, axis, dim):
    count = lax.axis_size(axis)
    if count == 1:
        edge = jnp.zeros_like(lax.slice_in_dim(field, 0, 1, axis=dim))
        return jnp.concatenate([edge, field, edge], axis=dim)
    ends = count - 1
    head = lax.slice_in_dim(field, 0, 1, axis=dim)
    tail = lax.slice_in_dim(field, field.shape[dim] - 1, field.shape[dim], axis=dim)
    return jnp.concatenate(
        [
            lax.ppermute(tail, axis, [(i, i + 1) for i in range(ends)]),
            field,
            lax.ppermute(head, axis, [(i + 1, i) for i in range(ends)]),
        ],
        axis=dim,
    )


def zero_halo(field):
    return jnp.pad(field, [(0, 0)] * (field.ndim - 2) + [(1, 1), (0, 0)])


def smooth(field, coefficient, offsets, extend):
    width = field.shape[-1]
    lead = [(0, 0)] * (field.ndim - 1)
    for _ in range(SWEEPS):
        padded = extend(field)
        upper = padded[..., :-2, :]
        lower = jnp.pad(padded[..., 2:, :], lead + [(REACH, REACH)])
        linked = jnp.zeros_like(field)
        for shift in range(-REACH, REACH + 1):
            start = REACH + shift
            linked = linked + jnp.where(offsets == shift, lower[..., start : start + width], 0.0)
        sides = jnp.pad(field, lead + [(1, 1)])
        field = field + coefficient * (
            sides[..., :-2] + sides[..., 2:] + upper + linked - 4.0 * field
        )
    return field


def apply_part(spectrum, operator, coefficient, offsets, extend):
    low = spectrum.astype(jnp.bfloat16)

    def adjoint_of(spec, resp):
        return jnp.einsum("frs,fsp->frp", spec, resp, preferred_element_type=jnp.float32)

    def forward_of(par, resp):
        return jnp.einsum("frp,fsp->frs", par, resp, preferred_element_type=jnp.float32)

    real = adjoint_of(low[0], operator[0]) + adjoint_of(low[1], operator[1])
    imag = adjoint_of(low[1], operator[0]) - adjoint_of(low[0], operator[1])
    adjoint = jnp.stack([real, imag])
    grid = adjoint.reshape(adjoint.shape[:3] + coefficient.shape)
    prior = smooth(grid, coefficient, offsets, extend).astype(jnp.bfloat16)
    prior = prior.reshape(adjoint.shape)
    real = forward_of(prior[0], operator[0]) - forward_of(prior[1], operator[1])
    imag = forward_of(prior[1], operator[0]) + forward_of(prior[0], operator[1])
    return jnp.stack([real, imag])


def body_plain(vectors, observed, operator, noise, coefficient, offsets):
    sen, par = lax.axis_size("sen"), lax.axis_size("par")
    rows, sensors, length = vectors.shape
    half = length // 2
    grid_rows, width = coefficient.shape
    basis = jnp.asarray(make_basis(length))
    both = jnp.stack([vectors, observed])
    spectra = jnp.dot(
        both.reshape(2 * rows * sensors, length), basis, precision=lax.Precision.HIGHEST
    )
    spectra = spectra.reshape(2, rows, sensors, 2, half)
    whole_cells = half % (sen * par) == 0
    axes = ("sen", "par") if whole_cells else "sen"
    shares = sen * par if whole_cells else sen
    each = half // shares

    cut = operator.reshape(2, shares, each, sensors, grid_rows, width)
    cut = lax.all_to_all(cut, axes, 1, 1, tiled=True)
    if whole_cells:
        resp = cut.reshape(2, sen, par, each, sensors, grid_rows, width)
        resp = resp.transpose(0, 3, 1, 4, 2, 5, 6)
        resp = resp.reshape(2, each, sen * sensors, par * grid_rows * width)
        coefficient = lax.all_gather(coefficient, "par", tiled=True)
        offsets = lax.all_gather(offsets, "par", tiled=True)
        extend = zero_halo
    else:
        resp = cut.transpose(0, 2, 1, 3, 4, 5)
        resp = resp.reshape(2, each, sen * sensors, grid_rows * width)
        extend = lambda field: halo(field, "par", field.ndim - 2)

    def to_frequencies(spec):
        parts = spec.shape[0]
        cut = spec.reshape(parts, rows, sensors, 2, shares, each)
        cut = lax.all_to_all(cut.transpose(4, 0, 3, 5, 1, 2), axes, 0, 0, tiled=True)
        if whole_cells:
            cut = cut.reshape((sen, par) + cut.shape[1:])[:, 0]
        return cut.transpose(1, 2, 3, 4, 0, 5).reshape(parts, 2, each, rows, sen * sensors)

    def to_sensors(spec):
        parts = spec.shape[0]
        cut = spec.reshape(parts, 2, each, rows, sen, sensors).transpose(4, 0, 3, 5, 1, 2)
        if whole_cells:
            cut = jnp.repeat(cut, par, axis=0)
        cut = lax.all_to_all(cut, axes, 0, 0, tiled=True)
        return cut.transpose(1, 2, 3, 4, 0, 5).reshape(parts, rows, sensors, 2 * half)

    def hessian(spectrum):
        forward = apply_part(spectrum, resp, coefficient, offsets, extend)
        return forward if whole_cells else lax.psum(forward, "par")

    rest = spectra[1] - noise[None, :, None, None] * spectra[0]
    own, rest = to_frequencies(jnp.stack([spectra[0], rest]))
    left = rest - hessian(own)
    again = hessian(left)
    home = to_sensors(jnp.stack([left, again]))
    back = jnp.dot(
        home.reshape(2 * rows * sensors, length), basis.T, precision=lax.Precision.HIGHEST
    ).reshape(2, rows, sensors, length)
    residual = back[0]
    applied = back[1] + noise[None, :, None] * residual
    return (residual, applied)


def roll(x, shift, axis):
    size = x.shape[axis]
    return x if shift % size == 0 else pltpu.roll(x, shift % size, axis)


def iota(shape, axis):
    return lax.broadcasted_iota(jnp.int32, shape, axis)


def upright(line):
    count = line.shape[1]
    square = jnp.broadcast_to(line, (count, count))
    square = jnp.where(iota((count, count), 0) == iota((count, count), 1), square, 0.0)
    return jnp.sum(square, axis=1, keepdims=True)


def split(x):
    high = x.astype(jnp.bfloat16).astype(jnp.float32)
    middle = (x - high).astype(jnp.bfloat16).astype(jnp.float32)
    return high, middle, (x - high - middle).astype(jnp.bfloat16).astype(jnp.float32)


def tail_lanes(each, pair):
    start = 2 * 3 * pair
    return start, LANES - start, each // KINDS


def outbound_kernel(
    resp_hbm, vectors_hbm, observed_hbm, noise_hbm, coef_hbm, link_hbm, basis_hbm, out_ref,
    resp_ref, vectors_ref, observed_ref, noise_ref, coef_ref, link_ref, basis_ref,
    small_sems, in_sems,
):
    _, devices, each, sensors, width = resp_ref.shape
    pair, tiles = 2 * sensors, width // LANES
    steps = in_sems.shape[0]
    some = devices // steps
    pieces = [pl.ds(i * some, some) for i in range(steps)]
    small = [
        pltpu.make_async_copy(src, dst, small_sems.at[i])
        for i, (src, dst) in enumerate(
            [
                (basis_hbm, basis_ref),
                (vectors_hbm, vectors_ref),
                (observed_hbm, observed_ref),
                (noise_hbm, noise_ref),
                (coef_hbm, coef_ref),
                (link_hbm, link_ref),
            ]
        )
    ]
    loads = [
        pltpu.make_async_copy(resp_hbm.at[:, piece], resp_ref.at[:, piece], in_sems.at[i])
        for i, piece in enumerate(pieces)
    ]
    body = each * tiles * pair
    for copy in small + loads:
        copy.start()

    for copy in small:
        copy.wait()
    noise = upright(noise_ref[...])
    core = lax.axis_index("par")
    record = vectors_ref[core]
    records = [record, observed_ref[core] - noise * record]
    records.append(jnp.zeros((LANES - pair, record.shape[1]), jnp.float32))
    spectra = lax.dot_general(
        basis_ref[...],
        jnp.concatenate(records, axis=0),
        (((1,), (1,)), ((), ())),
        precision=lax.Precision.HIGHEST,
        preferred_element_type=jnp.float32,
    )
    exact = iota(spectra.shape, 1) // sensors % 2 == 1
    high, middle, low = split(spectra)
    packed = high + roll(jnp.where(exact, middle, 0.0), pair, 1)
    packed = packed + roll(jnp.where(exact, low, 0.0), 2 * pair, 1)
    packed = packed[: devices * each] + roll(packed[devices * each :], 3 * pair, 1)

    start, free, chunks = tail_lanes(each, pair)
    piece = chunks * free
    per = LANES // piece
    turn = lax.axis_index("low") % (width // piece)
    coefs, links = (
        sum(
            jnp.where(turn // per == j, ref[:, j * LANES : (j + 1) * LANES].astype(jnp.float32), 0.0)
            for j in range(tiles)
        )
        for ref in (coef_ref, link_ref)
    )
    whole = jnp.concatenate([*split(coefs), links], axis=0)
    grid = whole
    for i in range(1, per):
        grid = jnp.where(turn % per == i, roll(whole, -i * piece, 1), grid)
    grid = jnp.concatenate([roll(grid, start - i * free, 1) for i in range(chunks)], axis=0)
    grid = jnp.where(iota(grid.shape, 1) >= start, grid, 0.0)
    packed = packed.reshape(devices, each, LANES) + grid[None]
    packed = packed.astype(jnp.bfloat16)
    out_ref[:, pl.ds(body, each), :] = packed

    for i, piece in enumerate(pieces):
        loads[i].wait()
        for f in range(each):
            for j in range(tiles):
                lanes = pl.ds(j * LANES, LANES)
                both = [resp_ref[c, piece, f, :, lanes] for c in range(2)]
                lane_rows = pl.ds((f * tiles + j) * pair, pair)
                out_ref[piece, lane_rows, :] = jnp.concatenate(both, axis=1)


class Share:
    def __init__(self, got_ref, rows, each, width):
        self.got = got_ref
        self.low, self.par = got_ref.shape[:2]
        self.rows, self.each, self.width = rows, each, width
        self.tiles = width // LANES
        self.pair = (got_ref.shape[2] - each) // (each * self.tiles)
        self.sensors = self.pair // 2
        self.lanes = self.low * self.pair
        self.joint = joint_of(each, self.lanes)
        self.groups = each // self.joint
        self.held = rows * 2 * self.joint
        shape = (self.held, self.lanes)
        row = iota(shape, 0)
        self.real_row = row // self.joint % 2 == 0
        self.real_lane = iota(shape, 1) // self.sensors % 2 == 0
        self.place = row % self.joint

    def swapped(self, x):
        return jnp.where(self.real_row, roll(x, -self.joint, 0), roll(x, self.joint, 0))

    def block(self, group, p):
        return jnp.concatenate(
            [
                jnp.concatenate(
                    [
                        self.got[
                            :, p, pl.ds((f * self.tiles + j) * self.pair, self.pair), :
                        ].reshape(self.lanes, LANES)
                        for j in range(self.tiles)
                    ],
                    axis=1,
                )
                for f in range(group * self.joint, (group + 1) * self.joint)
            ],
            axis=0,
        )

    def tail(self, count):
        rows = pl.ds(self.got.shape[2] - self.each, self.each)
        return self.got[pl.ds(0, count), :, rows, :].astype(jnp.float32)

    def spectra(self):
        tail = self.tail(self.low)
        shape = (self.each, LANES)
        at = iota(shape, 1) // self.pair
        per = LANES // self.pair
        found = [
            [jnp.zeros(shape, jnp.float32) for _ in range(self.lanes // LANES)]
            for _ in range(2 * self.rows)
        ]
        for i in range(self.low):
            h, place = divmod(i, per)
            for r in range(self.rows):
                packed = tail[i, r]
                packed = packed + roll(packed, -self.pair, 1) + roll(packed, -2 * self.pair, 1)
                for c in range(2):
                    moved = roll(packed, (place - 3 * c) * self.pair, 1)
                    line = found[2 * r + c]
                    line[h] = jnp.where(at == place, moved, line[h])
        found = [jnp.concatenate(line, axis=1) for line in found]
        return [
            jnp.concatenate([line[g * self.joint : (g + 1) * self.joint] for line in found], axis=0)
            for g in range(self.groups)
        ]

    def grid(self):
        start, free, chunks = tail_lanes(self.each, self.pair)
        count = self.width // (chunks * free)
        tail = self.tail(count)
        chunk = iota((KINDS, LANES), 1) // free
        coefs, links = [], []
        for p in range(self.par):
            found = [jnp.zeros((KINDS, LANES), jnp.float32) for _ in range(self.tiles)]
            for i in range(count * chunks):
                part = tail[i // chunks, p, i % chunks * KINDS : (i % chunks + 1) * KINDS]
                j, at = divmod(i * free, LANES)
                found[j] = jnp.where(chunk == at // free, roll(part, at - start, 1), found[j])
            found = jnp.concatenate(found, axis=1)
            coefs.append(found[0:1] + found[1:2] + found[2:3])
            links.append(found[3:4])
        return jnp.concatenate(coefs, axis=0), jnp.concatenate(links, axis=0)

    def adjoint(self, group, record):
        crossed = self.swapped(record)
        crossed = roll(jnp.where(self.real_row, crossed, -crossed), self.sensors, 1)
        left = jnp.where(self.real_lane, record, crossed)
        left = [jnp.where(self.place == i, left, 0.0) for i in range(self.joint)]
        left = jnp.concatenate(left, axis=1).astype(jnp.bfloat16)
        return [
            jnp.dot(left, self.block(group, p), preferred_element_type=jnp.float32)
            for p in range(self.par)
        ]

    def masks(self, coef_ref, link_ref):
        shape = (self.held, self.width)
        column = iota((1, self.width), 1)
        wide = lambda mask: jnp.broadcast_to(jnp.where(mask, 1.0, 0.0), shape)
        coefs, links = [], []
        for x in range(self.par):
            coefs.append(jnp.broadcast_to(coef_ref[x : x + 1, :], shape))
            offset = link_ref[x : x + 1, :]
            links.append(
                [
                    wide((offset == float(k)) & (column + k >= 0) & (column + k < self.width))
                    for k in range(-REACH, REACH + 1)
                ]
            )
        return coefs, links, wide(column > 0), wide(column < self.width - 1)

    def smoothed(self, field, masks):
        coefs, links, after_first, before_last = masks
        for _ in range(SWEEPS):
            after = []
            for x, u in enumerate(field):
                around = roll(u, 1, 1) * after_first + roll(u, -1, 1) * before_last
                if x > 0:
                    around += field[x - 1]
                if x < self.par - 1:
                    linked = jnp.zeros(u.shape, jnp.float32)
                    for mask, shift in zip(links[x], range(-REACH, REACH + 1)):
                        linked += mask * roll(field[x + 1], -shift, 1)
                    around += linked
                after.append(u + coefs[x] * (around - 4.0 * u))
            field = after
        return field

    def forward(self, group, field):
        part = jnp.zeros((self.held, self.joint * self.lanes), jnp.float32)
        for p in range(self.par):
            part += lax.dot_general(
                field[p].astype(jnp.bfloat16),
                self.block(group, p),
                (((1,), (1,)), ((), ())),
                preferred_element_type=jnp.float32,
            )
        out = part[:, : self.lanes]
        for i in range(1, self.joint):
            out = jnp.where(self.place == i, part[:, i * self.lanes : (i + 1) * self.lanes], out)
        crossed = self.swapped(roll(out, -self.sensors, 1))
        return out + jnp.where(self.real_row, -crossed, crossed)

    def message(self, group, residual, applied, out_ref):
        both = jnp.where(self.real_lane, residual, roll(applied, self.sensors, 1))
        per = self.held
        to, lane_group = iota((per, LANES), 0), iota((per, LANES), 1) // self.pair
        for h in range(self.lanes // LANES):
            tile = both[:, h * LANES : (h + 1) * LANES]
            moved = tile
            for turn in range(1, per):
                turned = roll(roll(tile, -turn, 0), turn * self.pair, 1)
                moved = jnp.where((lane_group - to + per) % per == turn, turned, moved)
            for i in range(per):
                for p in range(self.par):
                    place = (h * per + i) * self.par + p
                    out_ref[place, group : group + 1, :] = moved[i : i + 1, :]

    def rows_of(self, group):
        return pl.ds(group * self.held, self.held)

    def give(self, sums, *refs):
        for p in range(self.par):
            part = jnp.concatenate([line[p] for line in sums], axis=0)
            for ref in refs:
                ref[p] = part.astype(ref.dtype)

    def summed(self, own_ref, other_ref):
        whole = [own_ref[p] + other_ref[p].astype(jnp.float32) for p in range(self.par)]
        return [
            [part[g * self.held : (g + 1) * self.held] for part in whole]
            for g in range(self.groups)
        ]


def joint_of(each, lanes):
    return max(1, min(each, DEPTH // lanes))


def first_kernel(share, got_ref, spectra_ref, coef_ref, link_ref, own_ref):
    share = share(got_ref)
    coef_ref[...], link_ref[...] = share.grid()
    sums = []
    for g, spectra in enumerate(share.spectra()):
        spectra_ref[share.rows_of(g), :] = spectra
        sums.append(share.adjoint(g, spectra))
    share.give(sums, own_ref)


def middle_kernel(
    share, got_ref, one_ref, other_ref, spectra_ref, coef_ref, link_ref, residual_ref, own_ref, sent_ref
):
    share = share(got_ref)
    masks = share.masks(coef_ref, link_ref)
    residuals = []
    for g, field in enumerate(share.summed(one_ref, other_ref)):
        rest = roll(spectra_ref[share.rows_of(g), :], -share.sensors, 1)
        residuals.append(rest - share.forward(g, share.smoothed(field, masks)))
        residual_ref[share.rows_of(g), :] = residuals[g]
    share.give([share.adjoint(g, x) for g, x in enumerate(residuals)], own_ref, sent_ref)


def last_kernel(share, got_ref, one_ref, other_ref, residual_ref, coef_ref, link_ref, out_ref):
    share = share(got_ref)
    masks = share.masks(coef_ref, link_ref)
    for g, field in enumerate(share.summed(one_ref, other_ref)):
        applied = share.forward(g, share.smoothed(field, masks))
        share.message(g, residual_ref[share.rows_of(g), :], applied, out_ref)


def home_kernel(got_ref, basis_ref, noise_ref, residual_ref, applied_ref):
    sensors = noise_ref.shape[1]
    rows = residual_ref.shape[0]
    pair = 2 * sensors
    noise = upright(noise_ref[...])
    lines = [[] for _ in range(rows)]
    for g in range(got_ref.shape[1]):
        turned = got_ref[:, g, :].T
        for r in range(rows):
            first, last = r * LANES // rows, (r + 1) * LANES // rows
            lines[r] += [turned[i : i + pair, :] for i in range(first, last, pair)]
    back = jnp.dot(
        jnp.concatenate([jnp.concatenate(line, axis=1) for line in lines], axis=0),
        basis_ref[...],
        precision=lax.Precision.HIGHEST,
        preferred_element_type=jnp.float32,
    )
    for r in range(rows):
        residual = back[r * pair : r * pair + sensors]
        residual_ref[r] = residual
        applied_ref[r] = back[r * pair + sensors : (r + 1) * pair] + noise * residual


def body_fast(vectors, observed, operator, noise, coefficient, offsets):
    top, low, par = (lax.axis_size(axis) for axis in ("top", "low", "par"))
    rows, sensors, length = vectors.shape
    width = coefficient.shape[1]
    shares = low * par
    each = length // 2 // shares
    pair = 2 * sensors
    axes = ("low", "par")
    basis = make_basis(length).reshape(length, 2, shares, each)
    noise = noise[None, :]
    small = (vectors, observed, noise, coefficient, offsets)
    f32 = lambda *shape: jax.ShapeDtypeStruct(shape, jnp.float32)
    room = lambda mib: pltpu.CompilerParams(vmem_limit_bytes=mib * 2**20)

    steps = 2 if shares % 2 == 0 else 1
    tall = each * width // LANES * pair + each
    operator = operator.reshape(2, shares, each, sensors, width)
    scratch = [
        pltpu.VMEM(array.shape, array.dtype) for array in (operator, *small)
    ]
    message = pl.pallas_call(
        outbound_kernel,
        in_specs=[pl.BlockSpec(memory_space=pl.ANY)] * 7,
        out_specs=pl.BlockSpec(memory_space=pltpu.VMEM),
        out_shape=jax.ShapeDtypeStruct((shares, tall, LANES), jnp.bfloat16),
        scratch_shapes=scratch
        + [
            pltpu.VMEM((length, length), jnp.float32),
            pltpu.SemaphoreType.DMA((6,)),
            pltpu.SemaphoreType.DMA((steps,)),
        ],
        compiler_params=room(50),
        name="outbound",
    )(
        *(
            pltpu.with_memory_space_constraint(x, pltpu.HBM)
            for x in (
                operator,
                *small,
                jnp.asarray(basis.transpose(1, 2, 3, 0).reshape(length, length)),
            )
        )
    )
    got = lax.all_to_all(message, axes, 0, 0, tiled=True).reshape(low, par, tall, LANES)

    def across(sums):
        return lax.ppermute(sums, "top", [(i, (i + 1) % top) for i in range(top)])

    share = functools.partial(Share, rows=rows, each=each, width=width)
    held, lanes = rows * 2 * each, low * pair
    joint = joint_of(each, lanes)
    sums = f32(par, held, width)
    rounded = jax.ShapeDtypeStruct(sums.shape, jnp.bfloat16)
    grid = [f32(par, width)] * 2
    spectra, coefs, links, one = pl.pallas_call(
        functools.partial(first_kernel, share),
        out_shape=[f32(held, lanes)] + grid + [sums],
        compiler_params=room(32),
        name="first_adjoint",
    )(got)
    residual, two, sent = pl.pallas_call(
        functools.partial(middle_kernel, share),
        out_shape=[f32(held, lanes), sums, rounded],
        compiler_params=room(32),
        name="forward_adjoint",
    )(got, one, across(one), spectra, coefs, links)
    message = pl.pallas_call(
        functools.partial(last_kernel, share),
        out_shape=f32(shares, each // joint, LANES),
        compiler_params=room(32),
        name="last_forward",
    )(got, two, across(sent), residual, coefs, links)
    got = lax.all_to_all(message, axes, 0, 0, tiled=True)
    turned = basis.reshape(length, 2, shares, each // joint, joint)
    return pl.pallas_call(
        home_kernel,
        out_shape=[f32(rows, sensors, length)] * 2,
        compiler_params=room(16),
        name="to_time",
    )(got, jnp.asarray(turned.transpose(3, 1, 4, 2, 0).reshape(length, length)), noise)


def fits(mesh, args):
    vectors, _, _, _, coefficient, _ = args
    sen, par = mesh.shape["sen"], mesh.shape["par"]
    rows, sensors, length = vectors.shape
    half, low = length // 2, sen // 2
    if sen % 2 or half % (low * par) or sensors % sen or coefficient.shape[0] != par:
        return False
    each, pair = half // (low * par), 2 * (sensors // sen)
    start, free, chunks = tail_lanes(each, pair)
    piece = chunks * free
    return (
        rows == par
        and pair == 16
        and each % KINDS == 0
        and each % joint_of(each, low * pair) == 0
        and 2 * rows * joint_of(each, low * pair) * pair == LANES
        and low * pair % LANES == 0
        and coefficient.shape[1] % LANES == 0
        and start < LANES
        and LANES % piece == 0
        and low * piece >= coefficient.shape[1]
    )


def solution(mesh):
    def whole(*args):
        if fits(mesh, args):
            body, sen = body_fast, ("top", "low")
            shape = (2, mesh.shape["sen"] // 2, mesh.shape["par"])
            within = Mesh(mesh.devices.reshape(shape), sen + ("par",))
        else:
            body, sen, within = body_plain, "sen", mesh
        record = P(None, sen, None)
        return jax.shard_map(
            body,
            mesh=within,
            in_specs=(
                record,
                record,
                P(None, None, sen, "par"),
                P(sen),
                P("par", None),
                P("par", None),
            ),
            out_specs=(record, record),
            check_vma=False,
        )(*args)

    return whole
```

```python
import functools
import math

import jax
import jax.numpy as jnp
import numpy as np
from jax import lax
from jax.experimental import pallas as pl
from jax.experimental.pallas import tpu as pltpu
from jax.sharding import Mesh
from jax.sharding import PartitionSpec as P

SWEEPS = 4
REACH = 3
LANES = 128
DEPTH = 256
PARTS = 2
KINDS = 4


def make_basis(length):
    half = length // 2
    times = np.arange(length)[:, None]
    freqs = np.arange(half)[None, :]
    phase = (2 * freqs + 1) * times % (2 * length)
    angle = phase.astype(np.float64) * (math.pi / length)
    scale = math.sqrt(2.0 / length)
    return (np.concatenate([np.cos(angle), np.sin(angle)], axis=1) * scale).astype(np.float32)


def thirds(x):
    parts = []
    for _ in range(3):
        parts.append(x.astype(jnp.bfloat16))
        x = x - parts[-1].astype(np.float32)
    return np.stack(parts)


def halo(field, axis, dim):
    count = lax.axis_size(axis)
    if count == 1:
        edge = jnp.zeros_like(lax.slice_in_dim(field, 0, 1, axis=dim))
        return jnp.concatenate([edge, field, edge], axis=dim)
    ends = count - 1
    head = lax.slice_in_dim(field, 0, 1, axis=dim)
    tail = lax.slice_in_dim(field, field.shape[dim] - 1, field.shape[dim], axis=dim)
    return jnp.concatenate(
        [
            lax.ppermute(tail, axis, [(i, i + 1) for i in range(ends)]),
            field,
            lax.ppermute(head, axis, [(i + 1, i) for i in range(ends)]),
        ],
        axis=dim,
    )


def zero_halo(field):
    return jnp.pad(field, [(0, 0)] * (field.ndim - 2) + [(1, 1), (0, 0)])


def smooth(field, coefficient, offsets, extend):
    width = field.shape[-1]
    lead = [(0, 0)] * (field.ndim - 1)
    for _ in range(SWEEPS):
        padded = extend(field)
        upper = padded[..., :-2, :]
        lower = jnp.pad(padded[..., 2:, :], lead + [(REACH, REACH)])
        linked = jnp.zeros_like(field)
        for shift in range(-REACH, REACH + 1):
            start = REACH + shift
            linked = linked + jnp.where(offsets == shift, lower[..., start : start + width], 0.0)
        sides = jnp.pad(field, lead + [(1, 1)])
        field = field + coefficient * (
            sides[..., :-2] + sides[..., 2:] + upper + linked - 4.0 * field
        )
    return field


def apply_part(spectrum, operator, coefficient, offsets, extend):
    low = spectrum.astype(jnp.bfloat16)

    def adjoint_of(spec, resp):
        return jnp.einsum("frs,fsp->frp", spec, resp, preferred_element_type=jnp.float32)

    def forward_of(par, resp):
        return jnp.einsum("frp,fsp->frs", par, resp, preferred_element_type=jnp.float32)

    real = adjoint_of(low[0], operator[0]) + adjoint_of(low[1], operator[1])
    imag = adjoint_of(low[1], operator[0]) - adjoint_of(low[0], operator[1])
    adjoint = jnp.stack([real, imag])
    grid = adjoint.reshape(adjoint.shape[:3] + coefficient.shape)
    prior = smooth(grid, coefficient, offsets, extend).astype(jnp.bfloat16)
    prior = prior.reshape(adjoint.shape)
    real = forward_of(prior[0], operator[0]) - forward_of(prior[1], operator[1])
    imag = forward_of(prior[1], operator[0]) + forward_of(prior[0], operator[1])
    return jnp.stack([real, imag])


def body_plain(vectors, observed, operator, noise, coefficient, offsets):
    sen, par = lax.axis_size("sen"), lax.axis_size("par")
    rows, sensors, length = vectors.shape
    half = length // 2
    grid_rows, width = coefficient.shape
    basis = jnp.asarray(make_basis(length))
    both = jnp.stack([vectors, observed])
    spectra = jnp.dot(
        both.reshape(2 * rows * sensors, length), basis, precision=lax.Precision.HIGHEST
    )
    spectra = spectra.reshape(2, rows, sensors, 2, half)
    whole_cells = half % (sen * par) == 0
    axes = ("sen", "par") if whole_cells else "sen"
    shares = sen * par if whole_cells else sen
    each = half // shares

    cut = operator.reshape(2, shares, each, sensors, grid_rows, width)
    cut = lax.all_to_all(cut, axes, 1, 1, tiled=True)
    if whole_cells:
        resp = cut.reshape(2, sen, par, each, sensors, grid_rows, width)
        resp = resp.transpose(0, 3, 1, 4, 2, 5, 6)
        resp = resp.reshape(2, each, sen * sensors, par * grid_rows * width)
        coefficient = lax.all_gather(coefficient, "par", tiled=True)
        offsets = lax.all_gather(offsets, "par", tiled=True)
        extend = zero_halo
    else:
        resp = cut.transpose(0, 2, 1, 3, 4, 5)
        resp = resp.reshape(2, each, sen * sensors, grid_rows * width)
        extend = lambda field: halo(field, "par", field.ndim - 2)

    def to_frequencies(spec):
        parts = spec.shape[0]
        cut = spec.reshape(parts, rows, sensors, 2, shares, each)
        cut = lax.all_to_all(cut.transpose(4, 0, 3, 5, 1, 2), axes, 0, 0, tiled=True)
        if whole_cells:
            cut = cut.reshape((sen, par) + cut.shape[1:])[:, 0]
        return cut.transpose(1, 2, 3, 4, 0, 5).reshape(parts, 2, each, rows, sen * sensors)

    def to_sensors(spec):
        parts = spec.shape[0]
        cut = spec.reshape(parts, 2, each, rows, sen, sensors).transpose(4, 0, 3, 5, 1, 2)
        if whole_cells:
            cut = jnp.repeat(cut, par, axis=0)
        cut = lax.all_to_all(cut, axes, 0, 0, tiled=True)
        return cut.transpose(1, 2, 3, 4, 0, 5).reshape(parts, rows, sensors, 2 * half)

    def hessian(spectrum):
        forward = apply_part(spectrum, resp, coefficient, offsets, extend)
        return forward if whole_cells else lax.psum(forward, "par")

    rest = spectra[1] - noise[None, :, None, None] * spectra[0]
    own, rest = to_frequencies(jnp.stack([spectra[0], rest]))
    left = rest - hessian(own)
    again = hessian(left)
    home = to_sensors(jnp.stack([left, again]))
    back = jnp.dot(
        home.reshape(2 * rows * sensors, length), basis.T, precision=lax.Precision.HIGHEST
    ).reshape(2, rows, sensors, length)
    residual = back[0]
    applied = back[1] + noise[None, :, None] * residual
    return (residual, applied)


def roll(x, shift, axis):
    size = x.shape[axis]
    return x if shift % size == 0 else pltpu.roll(x, shift % size, axis)


def iota(shape, axis):
    return lax.broadcasted_iota(jnp.int32, shape, axis)


def upright(line):
    count = line.shape[1]
    square = jnp.broadcast_to(line, (count, count))
    square = jnp.where(iota((count, count), 0) == iota((count, count), 1), square, 0.0)
    return jnp.sum(square, axis=1, keepdims=True)


def split(x):
    high = x.astype(jnp.bfloat16).astype(jnp.float32)
    middle = (x - high).astype(jnp.bfloat16).astype(jnp.float32)
    return high, middle, (x - high - middle).astype(jnp.bfloat16).astype(jnp.float32)


def tail_lanes(each, pair):
    start = 2 * 3 * pair
    return start, LANES - start, each // KINDS


def outbound_kernel(
    resp_hbm, vectors_hbm, observed_hbm, noise_hbm, coef_hbm, link_hbm, basis_hbm, out_ref,
    resp_ref, vectors_ref, observed_ref, noise_ref, coef_ref, link_ref, basis_ref,
    small_sems, in_sems,
):
    _, devices, each, sensors, width = resp_ref.shape
    pair, tiles = 2 * sensors, width // LANES
    steps = in_sems.shape[0]
    some = devices // steps
    pieces = [pl.ds(i * some, some) for i in range(steps)]
    small = [
        pltpu.make_async_copy(src, dst, small_sems.at[i])
        for i, (src, dst) in enumerate(
            [
                (basis_hbm, basis_ref),
                (vectors_hbm, vectors_ref),
                (observed_hbm, observed_ref),
                (noise_hbm, noise_ref),
                (coef_hbm, coef_ref),
                (link_hbm, link_ref),
            ]
        )
    ]
    loads = [
        pltpu.make_async_copy(resp_hbm.at[:, piece], resp_ref.at[:, piece], in_sems.at[i])
        for i, piece in enumerate(pieces)
    ]
    body = each * tiles * pair
    for copy in small + loads:
        copy.start()

    for copy in small:
        copy.wait()
    noise = upright(noise_ref[...])
    core = lax.axis_index("par")
    record = vectors_ref[core]
    records = [record, observed_ref[core] - noise * record]
    records.append(jnp.zeros((LANES - pair, record.shape[1]), jnp.float32))
    spectra = lax.dot_general(
        basis_ref[...],
        jnp.concatenate(records, axis=0),
        (((1,), (1,)), ((), ())),
        precision=lax.Precision.HIGHEST,
        preferred_element_type=jnp.float32,
    )
    exact = iota(spectra.shape, 1) // sensors % 2 == 1
    high, middle, low = split(spectra)
    packed = high + roll(jnp.where(exact, middle, 0.0), pair, 1)
    packed = packed + roll(jnp.where(exact, low, 0.0), 2 * pair, 1)
    packed = packed[: devices * each] + roll(packed[devices * each :], 3 * pair, 1)

    start, free, chunks = tail_lanes(each, pair)
    piece = chunks * free
    per = LANES // piece
    turn = lax.axis_index("low") % (width // piece)
    coefs, links = (
        sum(
            jnp.where(turn // per == j, ref[:, j * LANES : (j + 1) * LANES].astype(jnp.float32), 0.0)
            for j in range(tiles)
        )
        for ref in (coef_ref, link_ref)
    )
    whole = jnp.concatenate([*split(coefs), links], axis=0)
    grid = whole
    for i in range(1, per):
        grid = jnp.where(turn % per == i, roll(whole, -i * piece, 1), grid)
    grid = jnp.concatenate([roll(grid, start - i * free, 1) for i in range(chunks)], axis=0)
    grid = jnp.where(iota(grid.shape, 1) >= start, grid, 0.0)
    packed = packed.reshape(devices, each, LANES) + grid[None]
    packed = packed.astype(jnp.bfloat16)
    out_ref[:, pl.ds(body, each), :] = packed

    for i, piece in enumerate(pieces):
        loads[i].wait()
        for f in range(each):
            for j in range(tiles):
                lanes = pl.ds(j * LANES, LANES)
                both = [resp_ref[c, piece, f, :, lanes] for c in range(2)]
                lane_rows = pl.ds((f * tiles + j) * pair, pair)
                out_ref[piece, lane_rows, :] = jnp.concatenate(both, axis=1)


class Share:
    def __init__(self, got_ref, rows, each, width):
        self.got = got_ref
        self.low, self.par = got_ref.shape[:2]
        self.rows, self.each, self.width = rows, each, width
        self.tiles = width // LANES
        self.pair = (got_ref.shape[2] - each) // (each * self.tiles)
        self.sensors = self.pair // 2
        self.lanes = self.low * self.pair
        self.joint = joint_of(each, self.lanes)
        self.groups = each // self.joint
        self.held = rows * 2 * self.joint
        shape = (self.held, self.lanes)
        row = iota(shape, 0)
        self.real_row = row // self.joint % 2 == 0
        self.real_lane = iota(shape, 1) // self.sensors % 2 == 0
        self.place = row % self.joint

    def swapped(self, x):
        return jnp.where(self.real_row, roll(x, -self.joint, 0), roll(x, self.joint, 0))

    def block(self, group, p):
        return jnp.concatenate(
            [
                jnp.concatenate(
                    [
                        self.got[
                            :, p, pl.ds((f * self.tiles + j) * self.pair, self.pair), :
                        ].reshape(self.lanes, LANES)
                        for j in range(self.tiles)
                    ],
                    axis=1,
                )
                for f in range(group * self.joint, (group + 1) * self.joint)
            ],
            axis=0,
        )

    def tail(self, count):
        rows = pl.ds(self.got.shape[2] - self.each, self.each)
        return self.got[pl.ds(0, count), :, rows, :].astype(jnp.float32)

    def spectra(self):
        tail = self.tail(self.low)
        shape = (self.each, LANES)
        at = iota(shape, 1) // self.pair
        per = LANES // self.pair
        found = [
            [jnp.zeros(shape, jnp.float32) for _ in range(self.lanes // LANES)]
            for _ in range(2 * self.rows)
        ]
        for i in range(self.low):
            h, place = divmod(i, per)
            for r in range(self.rows):
                packed = tail[i, r]
                packed = packed + roll(packed, -self.pair, 1) + roll(packed, -2 * self.pair, 1)
                for c in range(2):
                    moved = roll(packed, (place - 3 * c) * self.pair, 1)
                    line = found[2 * r + c]
                    line[h] = jnp.where(at == place, moved, line[h])
        found = [jnp.concatenate(line, axis=1) for line in found]
        return [
            jnp.concatenate([line[g * self.joint : (g + 1) * self.joint] for line in found], axis=0)
            for g in range(self.groups)
        ]

    def grid(self):
        start, free, chunks = tail_lanes(self.each, self.pair)
        count = self.width // (chunks * free)
        tail = self.tail(count)
        chunk = iota((KINDS, LANES), 1) // free
        coefs, links = [], []
        for p in range(self.par):
            found = [jnp.zeros((KINDS, LANES), jnp.float32) for _ in range(self.tiles)]
            for i in range(count * chunks):
                part = tail[i // chunks, p, i % chunks * KINDS : (i % chunks + 1) * KINDS]
                j, at = divmod(i * free, LANES)
                found[j] = jnp.where(chunk == at // free, roll(part, at - start, 1), found[j])
            found = jnp.concatenate(found, axis=1)
            coefs.append(found[0:1] + found[1:2] + found[2:3])
            links.append(found[3:4])
        return jnp.concatenate(coefs, axis=0), jnp.concatenate(links, axis=0)

    def adjoint(self, group, record):
        crossed = self.swapped(record)
        crossed = roll(jnp.where(self.real_row, crossed, -crossed), self.sensors, 1)
        left = jnp.where(self.real_lane, record, crossed)
        left = [jnp.where(self.place == i, left, 0.0) for i in range(self.joint)]
        left = jnp.concatenate(left, axis=1).astype(jnp.bfloat16)
        return [
            jnp.dot(left, self.block(group, p), preferred_element_type=jnp.float32)
            for p in range(self.par)
        ]

    def masks(self, coef_ref, link_ref):
        shape = (self.held, self.width)
        column = iota((1, self.width), 1)
        wide = lambda mask: jnp.broadcast_to(jnp.where(mask, 1.0, 0.0), shape)
        coefs, links = [], []
        for x in range(self.par):
            coefs.append(jnp.broadcast_to(coef_ref[x : x + 1, :], shape))
            offset = link_ref[x : x + 1, :]
            links.append(
                [
                    wide((offset == float(k)) & (column + k >= 0) & (column + k < self.width))
                    for k in range(-REACH, REACH + 1)
                ]
            )
        return coefs, links, wide(column > 0), wide(column < self.width - 1)

    def smoothed(self, field, masks):
        coefs, links, after_first, before_last = masks
        for _ in range(SWEEPS):
            after = []
            for x, u in enumerate(field):
                around = roll(u, 1, 1) * after_first + roll(u, -1, 1) * before_last
                if x > 0:
                    around += field[x - 1]
                if x < self.par - 1:
                    linked = jnp.zeros(u.shape, jnp.float32)
                    for mask, shift in zip(links[x], range(-REACH, REACH + 1)):
                        linked += mask * roll(field[x + 1], -shift, 1)
                    around += linked
                after.append(u + coefs[x] * (around - 4.0 * u))
            field = after
        return field

    def forward(self, group, field):
        part = jnp.zeros((self.held, self.joint * self.lanes), jnp.float32)
        for p in range(self.par):
            part += lax.dot_general(
                field[p].astype(jnp.bfloat16),
                self.block(group, p),
                (((1,), (1,)), ((), ())),
                preferred_element_type=jnp.float32,
            )
        out = part[:, : self.lanes]
        for i in range(1, self.joint):
            out = jnp.where(self.place == i, part[:, i * self.lanes : (i + 1) * self.lanes], out)
        crossed = self.swapped(roll(out, -self.sensors, 1))
        return out + jnp.where(self.real_row, -crossed, crossed)

    def message(self, group, residual, applied, out_ref):
        both = jnp.where(self.real_lane, residual, roll(applied, self.sensors, 1))
        per = self.held
        to, lane_group = iota((per, LANES), 0), iota((per, LANES), 1) // self.pair
        for h in range(self.lanes // LANES):
            tile = both[:, h * LANES : (h + 1) * LANES]
            moved = tile
            for turn in range(1, per):
                turned = roll(roll(tile, -turn, 0), turn * self.pair, 1)
                moved = jnp.where((lane_group - to + per) % per == turn, turned, moved)
            for i in range(per):
                for p in range(self.par):
                    place = (h * per + i) * self.par + p
                    out_ref[place, group : group + 1, :] = moved[i : i + 1, :]

    def rows_of(self, group):
        return pl.ds(group * self.held, self.held)

    def give(self, sums, *refs):
        for p in range(self.par):
            part = jnp.concatenate([line[p] for line in sums], axis=0)
            for ref in refs:
                ref[p] = part.astype(ref.dtype)

    def summed(self, own_ref, other_ref):
        whole = [own_ref[p] + other_ref[p].astype(jnp.float32) for p in range(self.par)]
        return [
            [part[i : i + self.held] for part in whole]
            for i in range(0, own_ref.shape[1], self.held)
        ]


def joint_of(each, lanes):
    return max(1, min(each, DEPTH // lanes))


def first_kernel(share, got_ref, spectra_ref, coef_ref, link_ref, own_ref):
    share = share(got_ref)
    coef_ref[...], link_ref[...] = share.grid()
    sums = []
    for g, spectra in enumerate(share.spectra()):
        spectra_ref[share.rows_of(g), :] = spectra
        if g * share.held < own_ref.shape[1]:
            sums.append(share.adjoint(g, spectra))
    share.give(sums, own_ref)


def more_kernel(share, first, got_ref, spectra_ref, own_ref):
    share = share(got_ref)
    groups = range(first, first + own_ref.shape[1] // share.held)
    share.give([share.adjoint(g, spectra_ref[share.rows_of(g), :]) for g in groups], own_ref)


def middle_kernel(share, first, got_ref, one_ref, other_ref, spectra_ref, coef_ref, link_ref, *refs):
    *before, residual_ref, own_ref, sent_ref = refs
    share = share(got_ref)
    masks = share.masks(coef_ref, link_ref)
    residuals = []
    for i, field in enumerate(share.summed(one_ref, other_ref)):
        rest = roll(spectra_ref[share.rows_of(first + i), :], -share.sensors, 1)
        residuals.append(rest - share.forward(first + i, share.smoothed(field, masks)))
        residual_ref[share.rows_of(first + i), :] = residuals[i]
    sums = [share.adjoint(first + i, x) for i, x in enumerate(residuals)]
    done = first * share.held
    for old, new in zip(before, (residual_ref, own_ref, sent_ref)):
        new[..., :done, :] = old[...]
    for p in range(share.par):
        part = jnp.concatenate([line[p] for line in sums], axis=0)
        own_ref[p, done:, :] = part
        sent_ref[p, done:, :] = part.astype(sent_ref.dtype)


def last_kernel(share, got_ref, one_ref, other_ref, residual_ref, coef_ref, link_ref, out_ref):
    share = share(got_ref)
    masks = share.masks(coef_ref, link_ref)
    for g, field in enumerate(share.summed(one_ref, other_ref)):
        applied = share.forward(g, share.smoothed(field, masks))
        share.message(g, residual_ref[share.rows_of(g), :], applied, out_ref)


def home_kernel(got_ref, basis_ref, noise_ref, residual_ref, applied_ref):
    sensors = noise_ref.shape[1]
    rows = residual_ref.shape[0]
    pair = 2 * sensors
    noise = upright(noise_ref[...])
    lines = [[] for _ in range(rows)]
    for g in range(got_ref.shape[1]):
        turned = got_ref[:, g, :].T
        for r in range(rows):
            first, last = r * LANES // rows, (r + 1) * LANES // rows
            lines[r] += [turned[i : i + pair, :] for i in range(first, last, pair)]
    spectra = jnp.concatenate([jnp.concatenate(line, axis=1) for line in lines], axis=0)
    parts = [part.astype(jnp.bfloat16) for part in split(spectra)]
    back = jnp.zeros((spectra.shape[0], basis_ref.shape[2]), jnp.float32)
    for i in reversed(range(len(parts))):
        left = jnp.concatenate(parts[: len(parts) - i], axis=0)
        product = jnp.dot(left, basis_ref[i], preferred_element_type=jnp.float32)
        for k in reversed(range(len(parts) - i)):
            back += product[k * spectra.shape[0] : (k + 1) * spectra.shape[0]]
    for r in range(rows):
        residual = back[r * pair : r * pair + sensors]
        residual_ref[r] = residual
        applied_ref[r] = back[r * pair + sensors : (r + 1) * pair] + noise * residual


def body_fast(vectors, observed, operator, noise, coefficient, offsets):
    top, low, par = (lax.axis_size(axis) for axis in ("top", "low", "par"))
    rows, sensors, length = vectors.shape
    width = coefficient.shape[1]
    shares = low * par
    each = length // 2 // shares
    pair = 2 * sensors
    axes = ("low", "par")
    basis = make_basis(length).reshape(length, 2, shares, each)
    noise = noise[None, :]
    small = (vectors, observed, noise, coefficient, offsets)
    f32 = lambda *shape: jax.ShapeDtypeStruct(shape, jnp.float32)
    room = lambda mib: pltpu.CompilerParams(vmem_limit_bytes=mib * 2**20)

    steps = 2 if shares % 2 == 0 else 1
    tall = each * width // LANES * pair + each
    operator = operator.reshape(2, shares, each, sensors, width)
    scratch = [
        pltpu.VMEM(array.shape, array.dtype) for array in (operator, *small)
    ]
    message = pl.pallas_call(
        outbound_kernel,
        in_specs=[pl.BlockSpec(memory_space=pl.ANY)] * 7,
        out_specs=pl.BlockSpec(memory_space=pltpu.VMEM),
        out_shape=jax.ShapeDtypeStruct((shares, tall, LANES), jnp.bfloat16),
        scratch_shapes=scratch
        + [
            pltpu.VMEM((length, length), jnp.float32),
            pltpu.SemaphoreType.DMA((6,)),
            pltpu.SemaphoreType.DMA((steps,)),
        ],
        compiler_params=room(50),
        name="outbound",
    )(
        *(
            pltpu.with_memory_space_constraint(x, pltpu.HBM)
            for x in (
                operator,
                *small,
                jnp.asarray(basis.transpose(1, 2, 3, 0).reshape(length, length)),
            )
        )
    )
    got = lax.all_to_all(message, axes, 0, 0, tiled=True).reshape(low, par, tall, LANES)

    def across(sums):
        return lax.ppermute(sums, "top", [(i, (i + 1) % top) for i in range(top)])

    share = functools.partial(Share, rows=rows, each=each, width=width)
    held, lanes = rows * 2 * each, low * pair
    joint = joint_of(each, lanes)
    groups = each // joint_of(each, lanes)
    parts = PARTS if groups % PARTS == 0 else 1
    some = groups // parts
    grid = [f32(par, width)] * 2
    part = f32(par, held // parts, width)
    spectra, coefs, links, one = pl.pallas_call(
        functools.partial(first_kernel, share),
        out_shape=[f32(held, lanes)] + grid + [part],
        compiler_params=room(32),
        name="first_adjoint",
    )(got)
    ones = [one] + [
        pl.pallas_call(
            functools.partial(more_kernel, share, i * some),
            out_shape=part,
            compiler_params=room(32),
            name="more_adjoint",
        )(got, spectra)
        for i in range(1, parts)
    ]
    others = [across(one) for one in ones]
    middle = []
    for i in range(parts):
        done = held * (i + 1) // parts
        sent = jax.ShapeDtypeStruct((par, done, width), jnp.bfloat16)
        middle = pl.pallas_call(
            functools.partial(middle_kernel, share, i * some),
            out_shape=[f32(done, lanes), f32(par, done, width), sent],
            compiler_params=room(32),
            name="forward_adjoint",
        )(got, ones[i], others[i], spectra, coefs, links, *middle)
    residual, two, sent = middle
    message = pl.pallas_call(
        functools.partial(last_kernel, share),
        out_shape=f32(shares, groups, LANES),
        compiler_params=room(32),
        name="last_forward",
    )(got, two, across(sent), residual, coefs, links)
    got = lax.all_to_all(message, axes, 0, 0, tiled=True)
    turned = basis.reshape(length, 2, shares, each // joint, joint)
    return pl.pallas_call(
        home_kernel,
        out_shape=[f32(rows, sensors, length)] * 2,
        compiler_params=room(16),
        name="to_time",
    )(got, jnp.asarray(thirds(turned.transpose(3, 1, 4, 2, 0).reshape(length, length))), noise)


def fits(mesh, args):
    vectors, _, _, _, coefficient, _ = args
    sen, par = mesh.shape["sen"], mesh.shape["par"]
    rows, sensors, length = vectors.shape
    half, low = length // 2, sen // 2
    if sen % 2 or half % (low * par) or sensors % sen or coefficient.shape[0] != par:
        return False
    each, pair = half // (low * par), 2 * (sensors // sen)
    start, free, chunks = tail_lanes(each, pair)
    piece = chunks * free
    return (
        rows == par
        and pair == 16
        and each % KINDS == 0
        and each % joint_of(each, low * pair) == 0
        and 2 * rows * joint_of(each, low * pair) * pair == LANES
        and low * pair % LANES == 0
        and coefficient.shape[1] % LANES == 0
        and start < LANES
        and LANES % piece == 0
        and low * piece >= coefficient.shape[1]
    )


def solution(mesh):
    def whole(*args):
        if fits(mesh, args):
            body, sen = body_fast, ("top", "low")
            shape = (2, mesh.shape["sen"] // 2, mesh.shape["par"])
            within = Mesh(mesh.devices.reshape(shape), sen + ("par",))
        else:
            body, sen, within = body_plain, "sen", mesh
        record = P(None, sen, None)
        return jax.shard_map(
            body,
            mesh=within,
            in_specs=(
                record,
                record,
                P(None, None, sen, "par"),
                P(sen),
                P("par", None),
                P("par", None),
            ),
            out_specs=(record, record),
            check_vma=False,
        )(*args)

    return whole
```
